128 devices in a mesh: circ: 16 (over z_hi, y, core), axial: 8 (over z_lo, x).
Axes of the slice: x: 4, y: 4, z: 4 (z_hi: 2, z_lo: 2; z = z_hi * 2 + z_lo), core: 2. Of those that a mesh axis runs over, the one named last changes fastest.
Arguments:
- flow_state: float32 [5, 256, 16384], P(None, 'circ', 'axial'), may hold values from -6 to 6
- circ_speed: float32 [256, 16384], P('circ', 'axial'), may hold values from -1 to 1
- axial_speed: float32 [256, 16384], P('circ', 'axial'), may hold values from -1 to 1
- time_step: float32 [256, 16384], P('circ', 'axial'), may hold values from 0.05 to 0.25
- lsq_weights: float32 [256, 64, 192], P('axial'), may hold values from -0.4375 to 0.4375
- partner: int32 [16384], P('axial'), may hold values from 0 to 2047, as said below
- merge_owner: int32 [16384, 1], P(('circ', 'axial')), may hold values from 0 to 127, as said below
- merge_source: int32 [16384], P(('circ', 'axial')), may hold values from 0 to 511
- merge_host: int32 [16384], P(('circ', 'axial')), may hold values from 0 to 511
- merge_frac: float32 [16384, 64], P(('circ', 'axial')), may hold values from 0.3 to 1
Outputs:
- new_state: float32 [5, 256, 16384], P(None, 'circ', 'axial')
- last_rate: float32 [5, 256, 16384], P(None, 'circ', 'axial')
The draws below stay inside these ranges and needn't reach their ends.
Inputs may be any that keep to these rules, and one draw needn't show every extreme that they name: `partner`: each aligned group of 2048 entries is a permutation of 0 to 2047; it names a column within the same group. `merge_owner`: owner g is the device at circ index g // 8 and axial index g % 8. The owner of a device's block is that device itself or a neighbour whose circ index differs by at most one (around the closed circ axis) and whose axial index differs by at most one. Among the 128 rows of one device no owner other than the device itself appears more than 8 times, and some other owner appears exactly 8 times. `merge_source`: A block number row * 32 + axial block on the sending device. `merge_host`: A block number row * 32 + axial block on the owning device.
All inputs are finite; a program needn't handle non-finite values.
Results may differ from the reference program's by a relative error of at most 0.0001.
Values sent between devices are 32-bit elements; how exact they have to be, the bound alone decides.
A program may use at most 128 MiB of HBM per device.

```python
import math
import jax
import jax.numpy as jnp
from jax import lax

NV = 5
BLK = 64
CC = 16
BA = 32
SB = 128
STEPS = 2
CAP = 8
CA = 2048
NC = 256
NA = 16384
NBA = 256
TOTAL_SB = 16384
N_CIRC = 16
N_AXIAL = 8
DEVICES = 128


def draw_partner(key, part):
    shard_count = NA // CA
    key_list = jax.random.split(key, shard_count)
    perms = jax.vmap(lambda single: jax.random.permutation(single, CA))(key_list)
    return perms.reshape(-1).astype(jnp.int32)


def draw_merge_owner(key, part):
    base = jax.random.fold_in(key, 71)
    first_key, second_key, third_key = jax.random.split(base, 3)
    devices = jnp.arange(DEVICES, dtype=jnp.int32)
    circ_index = devices // N_AXIAL
    axial_index = devices % N_AXIAL
    circ_steps = jnp.array([-1, -1, -1, 0, 0, 1, 1, 1], jnp.int32)
    axial_steps = jnp.array([-1, 0, 1, -1, 1, -1, 0, 1], jnp.int32)
    axial_target = axial_index[:, None] + axial_steps[None, :]
    valid = (axial_target >= 0) & (axial_target < N_AXIAL)
    counts = jax.random.randint(first_key, (DEVICES, 8), CAP // 2, CAP + 1).astype(jnp.int32)
    scores = jax.vmap(lambda single: jax.random.permutation(single, 8))(jax.random.split(second_key, DEVICES)).astype(jnp.int32)
    star = jnp.argmax(jnp.where(valid, scores + 8, 0), axis=1).astype(jnp.int32)
    counts = jnp.where(valid, counts, 0)
    counts = jnp.where(jnp.arange(8, dtype=jnp.int32)[None, :] == star[:, None], CAP, counts)
    bounds = jnp.cumsum(counts, axis=1)
    places = jnp.arange(SB, dtype=jnp.int32)
    which = jnp.sum((places[None, :, None] >= bounds[:, None, :]).astype(jnp.int32), axis=2)
    orders = jax.vmap(lambda single: jax.random.permutation(single, SB))(jax.random.split(third_key, DEVICES)).astype(jnp.int32)
    which = jnp.take_along_axis(which, orders, axis=1)
    clipped = jnp.minimum(which, 7)
    circ_move = jnp.where(which < 8, circ_steps[clipped], 0)
    axial_move = jnp.where(which < 8, axial_steps[clipped], 0)
    owner = (circ_index[:, None] + circ_move) % N_CIRC * N_AXIAL + axial_index[:, None] + axial_move
    return owner.reshape(-1, 1).astype(jnp.int32)


def plant(values, key, low, high):
    shape = values.shape
    index_at = [jax.random.randint(jax.random.fold_in(key, axis), (), 0, shape[axis]) for axis in range(len(shape))]
    values = values.at[tuple(index_at)].set(low)
    longest = shape.index(max(shape))
    index_at[longest] = (index_at[longest] + 1) % shape[longest]
    return values.at[tuple(index_at)].set(high)


def block_levels(rng, shape, pieces, low, high):
    level = 1.0
    for dim, shards_of in pieces:
        steps = jax.random.uniform(jax.random.fold_in(jax.random.fold_in(rng, 6), dim), (shards_of,), jnp.float32, low / len(pieces), high / len(pieces))
        level = level * jnp.repeat(jnp.exp(steps), shape[dim] // shards_of).reshape((-1,) + (1,) * (len(shape) - 1 - dim))
    return level


def gaussian(key, extent, width, limit, pieces=(), held_as=jnp.bfloat16):
    factor_of = block_levels(key, extent, pieces, -0.22, 0.18) if pieces else 1.0
    values = jax.random.normal(key, extent, jnp.float32) * width * factor_of
    return jnp.minimum(jnp.maximum(values, -limit), limit).astype(held_as)


def setup_inputs(seed: int = 0) -> dict:
    keys = jax.random.split(jax.random.key(seed), 11)
    flow_state = gaussian(keys[0], (NV, NC, NA), 1.0, 6.0, ((1, 16), (2, 8)), jnp.float32)
    circ_speed = jnp.clip(jax.random.uniform(keys[1], (NC, NA), jnp.float32, -1.0, 1.0) * block_levels(keys[1], (NC, NA), ((0, 16), (1, 8)), -0.4, 0.0), -1.0, 1.0)
    axial_speed = jnp.clip(jax.random.uniform(keys[2], (NC, NA), jnp.float32, -1.0, 1.0) * block_levels(keys[2], (NC, NA), ((0, 16), (1, 8)), -0.4, 0.0), -1.0, 1.0)
    time_step = jnp.clip(jnp.exp(math.log(0.25) - 1.609438 * jax.random.uniform(keys[3], (NC, NA), jnp.float32) ** block_levels(keys[3], (NC, NA), ((0, 16), (1, 8)), -0.2, 0.2)), 0.05, 0.25)
    lsq_weights = gaussian(keys[4], (NBA, BLK, 3 * BLK), (3 * BLK) ** -0.5, 0.4375, ((0, 8),), jnp.float32)
    partner = draw_partner(jax.random.fold_in(keys[10], 71), 0)
    merge_owner = draw_merge_owner(jax.random.fold_in(keys[10], 71), 0)
    merge_source = plant(jax.random.randint(keys[7], (TOTAL_SB,), 0, CC * BA), jax.random.fold_in(keys[7], 1), 0, (CC * BA) - 1).astype(jnp.int32)
    merge_host = plant(jax.random.randint(keys[8], (TOTAL_SB,), 0, CC * BA), jax.random.fold_in(keys[8], 1), 0, (CC * BA) - 1).astype(jnp.int32)
    merge_frac = jnp.clip(0.3 + 0.7 * jax.random.uniform(keys[9], (TOTAL_SB, BLK), jnp.float32) ** block_levels(keys[9], (TOTAL_SB, BLK), ((0, 128),), -0.2, 0.2), 0.3, 1.0)
    return {"flow_state": flow_state, "circ_speed": circ_speed, "axial_speed": axial_speed, "time_step": time_step, "lsq_weights": lsq_weights, "partner": partner, "merge_owner": merge_owner, "merge_source": merge_source, "merge_host": merge_host, "merge_frac": merge_frac}


def up_rows(values, global_partner):
    return jnp.concatenate([values[..., 1:, :], values[..., :1, :][..., global_partner]], axis=-2)


def down_rows(values, global_inverse):
    return jnp.concatenate([values[..., -1:, :][..., global_inverse], values[..., :-1, :]], axis=-2)


def upwind(velocity, left_side, right_side):
    return velocity * 0.5 * (left_side + right_side) - 0.5 * jnp.abs(velocity) * (right_side - left_side)


def lsq_axial(flow_values, lsq_weights):
    def one_var(plane):
        grouped = plane.reshape(NC, NA // BLK, BLK)
        zero_block = jnp.zeros((NC, 1, BLK), plane.dtype)
        padded = jnp.concatenate([zero_block, grouped, zero_block], axis=1)
        window = jnp.concatenate([padded[:, :-2], padded[:, 1:-1], padded[:, 2:]], axis=-1)
        result = jnp.einsum("cbj,bij->cbi", window, lsq_weights, precision=lax.Precision.HIGHEST)
        return result.reshape(NC, NA)
    return lax.map(one_var, flow_values)


def balance(flow_values, circ_speed, axial_speed, lsq_weights, global_partner, global_inverse, merge_owner, merge_source, merge_host, merge_frac):
    upper = up_rows(flow_values, global_partner)
    lower = down_rows(flow_values, global_inverse)
    slope_circ = 0.5 * (upper - lower)
    flux_circ = upwind(circ_speed, flow_values + 0.5 * slope_circ, upper - 0.5 * up_rows(slope_circ, global_partner))
    rate_circ = flux_circ - down_rows(flux_circ, global_inverse)
    slope_local = lsq_axial(flow_values, lsq_weights)
    grouped = slope_local.reshape(NV, NC, NA // BLK, BLK)
    sender = (jnp.arange(TOTAL_SB) // SB).astype(jnp.int32)
    src_row = (sender // N_AXIAL) * CC + merge_source // BA
    src_blk = (sender % N_AXIAL) * BA + merge_source % BA
    payload = grouped[:, src_row, src_blk, :] * merge_frac[None]
    target = merge_owner[:, 0]
    host_row = (target // N_AXIAL) * CC + merge_host // BA
    host_blk = (target % N_AXIAL) * BA + merge_host % BA
    grouped = grouped.at[:, host_row, host_blk, :].add(payload)
    slope_axial = grouped.reshape(NV, NC, NA)
    zero_col = jnp.zeros((NV, NC, 1), jnp.float32)
    next_values = jnp.concatenate([flow_values[:, :, 1:], zero_col], axis=-1)
    next_slope = jnp.concatenate([slope_axial[:, :, 1:], zero_col], axis=-1)
    flux_axial = upwind(axial_speed, flow_values + 0.5 * slope_axial, next_values - 0.5 * next_slope)
    rate_axial = flux_axial - jnp.concatenate([zero_col, flux_axial[:, :, :-1]], axis=-1)
    return rate_circ + rate_axial


def reference(flow_state, circ_speed, axial_speed, time_step, lsq_weights, partner, merge_owner, merge_source, merge_host, merge_frac):
    positions = jnp.arange(NA).astype(jnp.int32)
    global_partner = ((positions // CA) * CA + partner).astype(jnp.int32)
    global_inverse = jnp.zeros((NA,), jnp.int32).at[global_partner].set(positions)
    current = flow_state
    last_rate = jnp.zeros_like(flow_state)
    for step_index in range(STEPS):
        first_rate = balance(current, circ_speed, axial_speed, lsq_weights, global_partner, global_inverse, merge_owner, merge_source, merge_host, merge_frac)
        middle = current - time_step * first_rate
        last_rate = balance(middle, circ_speed, axial_speed, lsq_weights, global_partner, global_inverse, merge_owner, merge_source, merge_host, merge_frac)
        current = 0.5 * (current + middle - time_step * last_rate)
    return current, last_rate
```

```python
import jax
import jax.numpy as jnp
from jax import lax
from jax.experimental import pallas as pl
from jax.experimental.pallas import tpu as pltpu
from jax.sharding import PartitionSpec as P

STEPS = 2
BALANCES = 2 * STEPS
CAP = 8
NV = 5
ROWS = 16
LANES = 128
TILES = 16
HALF = 64
SMALL = 128
BLOCKS = 32
N_CIRC = 16
N_AXIAL = 8
STACK = NV * ROWS
WIDE = NV * LANES
FIRST = 8
MESH = pl.DeviceIdType.MESH
F32 = jnp.float32
BF16 = jnp.bfloat16
NEIGHBOURS = [(dc, da) for dc in (-1, 0, 1) for da in (-1, 0, 1) if (dc, da) != (0, 0)]


def split(x):
    high = x.astype(BF16)
    return high, (x - high.astype(F32)).astype(BF16)


def lanes_of(shape):
    return lax.broadcasted_iota(jnp.int32, shape, len(shape) - 1)


def rolled(x, steps):
    return pltpu.roll(x, steps, x.ndim - 1)


def var_rows(v):
    return slice(v * ROWS, (v + 1) * ROWS)


def var_lanes(v):
    return slice(v * LANES, (v + 1) * LANES)


def cells(p):
    return pl.ds(pl.multiple_of(p * LANES, LANES), LANES)


def kernel(
    flow, cspd, aspd, dt, w, partner_row, partner_tile, owner, source, host, frac,
    out_u, out_rate,
    cur, base, cs, xs, wts, s32, shi, slo, rc, gout, gloc, fout, floc, a_loc, a_arr, c_loc, c_arr,
    edges, consts, f_keep, halo, perm, permuted,
    ax_send, ax_recv, ini_send, ini_recv, ci_send, ci_recv, lab_send, lab_recv, outbox, inbox,
    ax_ss, ax_rs, ini_ss, ini_rs, ci_ss, ci_rs, lab_ss, lab_rs, box_ss, box_rs,
):
    c = lax.axis_index("circ")
    a = lax.axis_index("axial")

    def peer(dc, da):
        return (lax.rem(c + dc + N_CIRC, N_CIRC), lax.rem(a + da + N_AXIAL, N_AXIAL))

    def remote(src, dst, send, recv, dc, da):
        return pltpu.make_async_remote_copy(
            src_ref=src, dst_ref=dst, send_sem=send, recv_sem=recv,
            device_id=peer(dc, da), device_id_type=MESH,
        )

    def axial_copy(n, side):
        return remote(
            ax_send.at[n, side], ax_recv.at[n, side], ax_ss.at[n, side], ax_rs.at[n, side],
            0, 2 * side - 1,
        )

    def init_copy(side):
        return remote(
            ini_send.at[side], ini_recv.at[side], ini_ss.at[side], ini_rs.at[side], 0, 2 * side - 1
        )

    def circ_copy(n, side):
        return remote(
            ci_send.at[n, side], ci_recv.at[n, side], ci_ss.at[n, side], ci_rs.at[n, side],
            2 * side - 1, 0,
        )

    def label_copy(k):
        dc, da = NEIGHBOURS[k]
        rows = pl.ds(k * CAP, CAP)
        return remote(lab_send.at[rows], lab_recv.at[rows], lab_ss.at[k], lab_rs.at[k], dc, da)

    def box_copy(n, k):
        dc, da = NEIGHBOURS[k]
        rows = pl.ds(k * CAP, CAP)
        return remote(
            outbox.at[n, rows], inbox.at[n, rows], box_ss.at[n, k], box_rs.at[n, k], dc, da
        )

    own = slice(FIRST, FIRST + ROWS)
    lane = lanes_of((ROWS, LANES))

    barrier = pltpu.get_barrier_semaphore()
    for dc, da in NEIGHBOURS:
        pl.semaphore_signal(barrier, inc=1, device_id=peer(dc, da), device_id_type=MESH)

    def stage(p, _):
        for v in range(NV):
            cur[p, v, own, :] = flow[v, :, cells(p)]
        cs[p, own, :] = cspd[:, cells(p)]
        return 0

    lax.fori_loop(0, TILES, stage, 0)

    for v in range(NV):
        ax_send[0, 0, var_rows(v), :] = jnp.where(lane < HALF, cur[0, v, own, :], 0.0)
        ax_send[0, 1, var_rows(v), :] = jnp.where(lane >= HALF, cur[TILES - 1, v, own, :], 0.0)
    ini_send[0, 0] = dt[:, 0:LANES]
    ini_send[0, 1] = dt[:, 0:LANES]
    ini_send[1, 0] = dt[:, (TILES - 1) * LANES:]
    ini_send[1, 1] = aspd[:, (TILES - 1) * LANES:]
    edges[...] = jnp.zeros_like(edges)

    square = (SMALL, SMALL)
    t_row = owner[...]
    s_row = source[...]
    h_row = host[...]

    def as_columns(row):
        return jnp.broadcast_to(row.astype(F32), square).T.astype(jnp.int32)

    t_col, s_col, h_col = as_columns(t_row), as_columns(s_row), as_columns(h_row)
    myself = c * N_AXIAL + a
    first = lax.broadcasted_iota(jnp.int32, square, 0)
    second = lax.broadcasted_iota(jnp.int32, square, 1)
    shares = jnp.where((jnp.broadcast_to(t_row, square) == t_col) & (first < second), 1.0, 0.0)
    rank = jnp.sum(shares, axis=0, keepdims=True).astype(jnp.int32)
    circ_off = ((t_row >> 3) - c + 1 + N_CIRC) & (N_CIRC - 1)
    number = circ_off * 3 + (t_row & (N_AXIAL - 1)) - a + 1
    number = jnp.where(number > 4, number - 1, number)
    place = jnp.where(t_row == myself, -1, number * CAP + rank)
    slots = len(NEIGHBOURS) * CAP
    chosen = jnp.where(
        jnp.broadcast_to(place, (slots, SMALL))
        == lax.broadcasted_iota(jnp.int32, (slots, SMALL), 0),
        1.0, 0.0,
    )

    def row_index(s):
        return ((s & (BLOCKS - 1)) >> 1) * ROWS + (s >> 5)

    host_index = row_index(h_row)
    labels = jnp.sum(chosen * (host_index + 1).astype(F32), axis=1, keepdims=True) - 1.0
    lab_send[...] = jnp.broadcast_to(labels, (slots, LANES))

    pl.semaphore_wait(barrier, len(NEIGHBOURS))
    for side in range(2):
        axial_copy(0, side).start()
        init_copy(side).start()
    for k in range(len(NEIGHBOURS)):
        label_copy(k).start()

    frac_twice = jnp.concatenate([frac[...], frac[...]], axis=1)
    placed = jnp.where((second >> 6) == (h_col & 1), frac_twice, 0.0)
    same_half = (s_col & 1) == (h_col & 1)
    straight = jnp.where(same_half, placed, 0.0)
    crossed = jnp.where(same_half, 0.0, placed)
    is_local = t_col == myself
    floc[0] = jnp.where(is_local, straight, 0.0)
    floc[1] = jnp.where(is_local, crossed, 0.0)
    fout[0] = jnp.dot(chosen, straight, precision=lax.Precision.HIGHEST)
    fout[1] = jnp.dot(chosen, crossed, precision=lax.Precision.HIGHEST)
    s_index = row_index(s_col)
    pick = jnp.concatenate(
        [
            jnp.where(s_index == second, 1.0, 0.0),
            jnp.where(s_index == second + LANES, 1.0, 0.0),
        ],
        axis=1,
    ).astype(BF16)
    gloc[...] = pick
    gout[...] = jnp.dot(chosen.astype(BF16), pick, preferred_element_type=F32).astype(BF16)
    tall = (TILES * ROWS, SMALL)
    tall_rows = lax.broadcasted_iota(jnp.int32, tall, 0)
    wanted = jnp.where(t_row == myself, host_index, -1)
    land = jnp.where(jnp.broadcast_to(wanted, tall) == tall_rows, 1.0, 0.0).astype(BF16)
    a_loc[...] = jnp.concatenate([land, land], axis=1)

    @pl.when(c == N_CIRC - 1)
    def _():
        perm[0] = partner_tile[...] >> 7
        perm[1] = partner_tile[...] & (LANES - 1)

    @pl.when(c == 0)
    def _():
        columns = TILES * LANES
        target = partner_row[...]
        upper = jnp.where(
            jnp.broadcast_to(target >> 7, (TILES, columns))
            == lax.broadcasted_iota(jnp.int32, (TILES, columns), 0),
            1.0, 0.0,
        ).astype(BF16)
        tall_lanes = (LANES, columns)
        here = jnp.broadcast_to(target & (LANES - 1), tall_lanes) == lax.broadcasted_iota(
            jnp.int32, tall_lanes, 0
        )
        position = lanes_of(tall_lanes)
        for part, value in enumerate((position >> 7, position & (LANES - 1))):
            lower = jnp.where(here, value.astype(F32), 0.0).astype(BF16)
            perm[part] = lax.dot_general(
                upper, lower, (((1,), (1,)), ((), ())), preferred_element_type=F32
            ).astype(jnp.int32)

    def weigh(p, _):
        gap = jnp.zeros((HALF, HALF), F32)
        both = jnp.concatenate(
            [
                jnp.concatenate([w[2 * p], gap], axis=1),
                jnp.concatenate([gap, w[2 * p + 1]], axis=1),
            ],
            axis=0,
        )
        high, low = split(both.T)
        wts[p, :, 0:LANES] = high
        wts[p, :, LANES:] = low
        return 0

    lax.fori_loop(0, TILES, weigh, 0)

    for k in range(len(NEIGHBOURS)):
        label_copy(k).wait()
    arrived_labels = lab_recv[...].astype(jnp.int32)
    label_row = (
        jnp.concatenate([arrived_labels, arrived_labels], axis=0).astype(F32).T.astype(jnp.int32)
    )
    a_arr[...] = jnp.where(
        jnp.concatenate([label_row, label_row], axis=0) == tall_rows, 1.0, 0.0
    ).astype(BF16)
    for side in range(2):
        init_copy(side).wait()
    consts[0] = jnp.where(a > 0, ini_recv[1, 0], 0.0)
    consts[1] = jnp.where(a < N_AXIAL - 1, ini_recv[0, 0], 0.0)
    consts[2] = jnp.where((a > 0) & (lane == 0), rolled(ini_recv[1, 1], 1), 0.0)
    consts[3] = jnp.where(lane == LANES - 1, aspd[:, (TILES - 1) * LANES:], 0.0)

    def fix_edges(n, factor, also_rate):
        for side in range(2):
            axial_copy(n, side).wait()
        left_speed, right_speed = consts[2], consts[3]
        last = (TILES - 1) * LANES
        for v in range(NV):
            vr = var_rows(v)
            from_left = jnp.where(a > 0, ax_recv[n, 1, vr, :], 0.0)
            from_right = jnp.where(a < N_AXIAL - 1, ax_recv[n, 0, vr, :], 0.0)
            left_flux = jnp.maximum(left_speed, 0.0) * from_left + jnp.minimum(
                left_speed, 0.0
            ) * edges[0, vr, :]
            right_flux = jnp.maximum(right_speed, 0.0) * edges[1, vr, :] + jnp.minimum(
                right_speed, 0.0
            ) * from_right
            cur[0, v, own, :] = cur[0, v, own, :] + factor * dt[:, 0:LANES] * left_flux
            cur[TILES - 1, v, own, :] = (
                cur[TILES - 1, v, own, :] - factor * dt[:, last:] * right_flux
            )
            if also_rate:
                out_rate[v, :, 0:LANES] = out_rate[v, :, 0:LANES] - left_flux
                out_rate[v, :, last:] = out_rate[v, :, last:] + right_flux
            else:
                halo[0, v] = from_left - factor * consts[0] * rolled(left_flux, LANES - 1)
                halo[1, v] = from_right + factor * consts[1] * rolled(right_flux, 1)

    def shift(q, left_tile, right_tile):
        for v in range(NV):
            moved = rolled(jnp.where(lane >= HALF, left_tile(v), right_tile(v)), HALF)
            high, low = split(moved)
            xs[q, var_rows(v), :] = high
            xs[q, STACK + v * ROWS:STACK + (v + 1) * ROWS, :] = low

    def slopes(p):
        left = jnp.concatenate([xs[p], xs[p + 1]], axis=1)
        full = jnp.dot(left, wts[p], preferred_element_type=F32)
        total = full[:STACK, :LANES] + full[:STACK, LANES:] + full[STACK:, :LANES]
        s32[p] = total
        high, low = split(total)
        rows = pl.ds(pl.multiple_of(p * ROWS, ROWS), ROWS)
        for v in range(NV):
            shi[rows, var_lanes(v)] = high[var_rows(v)]
            slo[rows, var_lanes(v)] = low[var_rows(v)]

    def gathered(picks, factors, v):
        vl = var_lanes(v)
        picked = jnp.dot(picks[...], shi[:, vl], preferred_element_type=F32) + jnp.dot(
            picks[...], slo[:, vl], preferred_element_type=F32
        )
        return picked * factors[0] + rolled(picked, HALF) * factors[1]

    def scatter(matrix, values, v):
        added = jnp.dot(matrix[...], values[:, var_lanes(v)], preferred_element_type=F32)
        for p in range(TILES):
            s32[p, var_rows(v), :] = s32[p, var_rows(v), :] + added[p * ROWS:(p + 1) * ROWS]

    def circ_pack(n):
        def pack(p, _):
            for v in range(NV):
                pair = slice(2 * v, 2 * v + 2)
                ci_send[n, 0, p, pair, :] = cur[p, v, FIRST:FIRST + 2, :]
                ci_send[n, 1, p, pair, :] = cur[p, v, FIRST + ROWS - 2:FIRST + ROWS, :]
            ci_send[n, 1, p, 10:11, :] = cs[p, FIRST + ROWS - 1:FIRST + ROWS, :]
            return 0

        lax.fori_loop(0, TILES, pack, 0)

    def unpack(upper, lower):
        def one(p, _):
            for v in range(NV):
                pair = slice(2 * v, 2 * v + 2)
                if upper is not None:
                    cur[p, v, FIRST + ROWS:FIRST + ROWS + 2, :] = upper[p, pair, :]
                if lower is not None:
                    cur[p, v, FIRST - 2:FIRST, :] = lower[p, pair, :]
            if lower is not None:
                cs[p, FIRST - 1:FIRST, :] = lower[p, 10:11, :]
            return 0

        lax.fori_loop(0, TILES, one, 0)

    def permute(rows):
        def one(p, _):
            tile = jnp.broadcast_to(perm[0, pl.ds(p, 1), :], (ROWS, LANES))
            column = jnp.broadcast_to(perm[1, pl.ds(p, 1), :], (ROWS, LANES))
            total = jnp.zeros((ROWS, LANES), F32)
            for q in range(TILES):
                found = jnp.take_along_axis(rows[q], column, axis=1)
                total = jnp.where(tile == q, found, total)
            permuted[p] = total
            return 0

        lax.fori_loop(0, TILES, one, 0)

    def circ_rates(p, _):
        above = cs[p, own, :]
        below = cs[p, FIRST - 1:FIRST + ROWS - 1, :]
        above_pos, above_neg = jnp.maximum(above, 0.0), jnp.minimum(above, 0.0)
        below_pos, below_neg = jnp.maximum(below, 0.0), jnp.minimum(below, 0.0)
        for v in range(NV):
            at = [cur[p, v, FIRST + k:FIRST + k + ROWS, :] for k in (-2, -1, 0, 1, 2)]
            slope_below = 0.25 * (at[2] - at[0])
            slope_here = 0.25 * (at[3] - at[1])
            slope_above = 0.25 * (at[4] - at[2])
            upper = above_pos * (at[2] + slope_here) + above_neg * (at[3] - slope_above)
            lower = below_pos * (at[1] + slope_below) + below_neg * (at[2] - slope_here)
            rc[p, var_rows(v), :] = upper - lower
        return 0

    def face(p, v, kind):
        half_slope = 0.5 * s32[p, var_rows(v), :]
        here = cur[p, v, own, :]
        return here + half_slope if kind == 0 else here - half_slope

    def flux(p, v, right_lane):
        speed = aspd[:, cells(p)]
        right = rolled(jnp.where(lane == 0, right_lane, face(p, v, 1)), LANES - 1)
        return jnp.maximum(speed, 0.0) * face(p, v, 0) + jnp.minimum(speed, 0.0) * right

    def advance(p, v, flux_here, flux_left, first_stage, factor):
        before = rolled(jnp.where(lane == LANES - 1, flux_left, flux_here), 1)
        rate = rc[p, var_rows(v), :] + flux_here - before
        here = cur[p, v, own, :]
        start = jnp.where(first_stage, here, base[p, var_rows(v), :])
        base[p, var_rows(v), :] = start
        out_rate[v, :, cells(p)] = rate
        new = 0.5 * (start + here) - factor * (dt[:, cells(p)] * rate)
        cur[p, v, own, :] = new
        return new

    def balance(n, _):
        odd = lax.rem(n, 2)
        first_stage = odd == 0
        factor = jnp.where(first_stage, 1.0, 0.5).astype(F32)
        earlier = jnp.where(first_stage, 0.5, 1.0).astype(F32)

        def shift_inner(q, _):
            shift(q, lambda v: cur[q - 1, v, own, :], lambda v: cur[q, v, own, :])
            return 0

        def slopes_inner(p, _):
            slopes(p)
            return 0

        lax.fori_loop(1, TILES, shift_inner, 0)
        lax.fori_loop(1, TILES - 1, slopes_inner, 0)
        fix_edges(n, earlier, False)
        shift(0, lambda v: halo[0, v], lambda v: cur[0, v, own, :])
        shift(TILES, lambda v: cur[TILES - 1, v, own, :], lambda v: halo[1, v])
        slopes(0)
        slopes(TILES - 1)

        circ_pack(n)
        for side in range(2):
            circ_copy(n, side).start()
        for v in range(NV):
            outbox[n, :, var_lanes(v)] = gathered(gout, fout, v)
        for k in range(len(NEIGHBOURS)):
            box_copy(n, k).start()

        for v in range(NV):
            high, low = split(gathered(gloc, floc, v))
            c_loc[:SMALL, var_lanes(v)] = high
            c_loc[SMALL:, var_lanes(v)] = low
        for v in range(NV):
            scatter(a_loc, c_loc, v)

        for side in range(2):
            circ_copy(n, side).wait()
        unpack(ci_recv.at[n, 0], ci_recv.at[n, 1])

        @pl.when(c == 0)
        def _():
            permute(ci_recv.at[n, 1])
            unpack(None, permuted)

        @pl.when(c == N_CIRC - 1)
        def _():
            permute(ci_recv.at[n, 0])
            unpack(permuted, None)

        lax.fori_loop(0, TILES, circ_rates, 0)

        for k in range(len(NEIGHBOURS)):
            box_copy(n, k).wait()
        for v in range(NV):
            high, low = split(inbox[n, :, var_lanes(v)])
            c_arr[:slots, var_lanes(v)] = high
            c_arr[slots:, var_lanes(v)] = low
        for v in range(NV):
            scatter(a_arr, c_arr, v)

        end = TILES - 1
        for v in range(NV):
            vr = var_rows(v)
            right_face = face(0, v, 1)
            flux_first = flux(0, v, face(1, v, 1))
            left_face = face(end, v, 0)
            flux_before = flux(end - 1, v, face(end, v, 1))
            flux_last = jnp.where(lane == LANES - 1, 0.0, flux(end, v, 0.0))
            edges[0, vr, :] = right_face
            edges[1, vr, :] = left_face
            f_keep[0, vr, :] = flux_first
            f_keep[1, vr, :] = flux_before
            new_first = advance(0, v, flux_first, 0.0, first_stage, factor)
            new_last = advance(end, v, flux_last, flux_before, first_stage, factor)
            ax_send[n + 1, 0, vr, :] = jnp.where(
                lane < HALF, new_first, rolled(right_face, LANES - 1)
            )
            ax_send[n + 1, 1, vr, :] = jnp.where(lane >= HALF, new_last, rolled(left_face, 1))
        for side in range(2):
            axial_copy(n + 1, side).start()

        def update(p, before):
            after = []
            for v in range(NV):
                here = flux(p, v, face(p + 1, v, 1))
                advance(p, v, here, before[v], first_stage, factor)
                after.append(here)
            return tuple(after)

        carried = tuple(f_keep[0, var_rows(v), :] for v in range(NV))
        carried = lax.fori_loop(1, end - 1, update, carried)
        for v in range(NV):
            advance(end - 1, v, f_keep[1, var_rows(v), :], carried[v], first_stage, factor)
        return 0

    lax.fori_loop(0, BALANCES, balance, 0)
    fix_edges(BALANCES, jnp.float32(0.5), True)

    def finish(p, _):
        for v in range(NV):
            out_u[v, :, cells(p)] = cur[p, v, own, :]
        return 0

    lax.fori_loop(0, TILES, finish, 0)


def local(
    flow_state, circ_speed, axial_speed, time_step, lsq_weights,
    partner, merge_owner, merge_source, merge_host, merge_frac,
):
    columns = TILES * LANES
    slots = len(NEIGHBOURS) * CAP
    vmem = pl.BlockSpec(memory_space=pltpu.VMEM)
    dma = pltpu.SemaphoreType.DMA
    shape = jax.ShapeDtypeStruct((NV, ROWS, columns), F32)
    scratch = [
        pltpu.VMEM((TILES, NV, 2 * ROWS, LANES), F32),
        pltpu.VMEM((TILES, STACK, LANES), F32),
        pltpu.VMEM((TILES, 2 * ROWS, LANES), F32),
        pltpu.VMEM((TILES + 1, 2 * STACK, LANES), BF16),
        pltpu.VMEM((TILES, 2 * LANES, 2 * LANES), BF16),
        pltpu.VMEM((TILES, STACK, LANES), F32),
        pltpu.VMEM((TILES * ROWS, WIDE), BF16),
        pltpu.VMEM((TILES * ROWS, WIDE), BF16),
        pltpu.VMEM((TILES, STACK, LANES), F32),
        pltpu.VMEM((slots, TILES * ROWS), BF16),
        pltpu.VMEM((SMALL, TILES * ROWS), BF16),
        pltpu.VMEM((2, slots, LANES), F32),
        pltpu.VMEM((2, SMALL, LANES), F32),
        pltpu.VMEM((TILES * ROWS, 2 * SMALL), BF16),
        pltpu.VMEM((TILES * ROWS, 2 * slots), BF16),
        pltpu.VMEM((2 * SMALL, WIDE), BF16),
        pltpu.VMEM((2 * slots, WIDE), BF16),
        pltpu.VMEM((2, STACK, LANES), F32),
        pltpu.VMEM((4, ROWS, LANES), F32),
        pltpu.VMEM((2, STACK, LANES), F32),
        pltpu.VMEM((2, NV, ROWS, LANES), F32),
        pltpu.VMEM((2, TILES, LANES), jnp.int32),
        pltpu.VMEM((TILES, ROWS, LANES), F32),
        pltpu.VMEM((BALANCES + 1, 2, STACK, LANES), F32),
        pltpu.VMEM((BALANCES + 1, 2, STACK, LANES), F32),
        pltpu.VMEM((2, 2, ROWS, LANES), F32),
        pltpu.VMEM((2, 2, ROWS, LANES), F32),
        pltpu.VMEM((BALANCES, 2, TILES, ROWS, LANES), F32),
        pltpu.VMEM((BALANCES, 2, TILES, ROWS, LANES), F32),
        pltpu.VMEM((slots, LANES), F32),
        pltpu.VMEM((slots, LANES), F32),
        pltpu.VMEM((BALANCES, slots, WIDE), F32),
        pltpu.VMEM((BALANCES, slots, WIDE), F32),
        dma((BALANCES + 1, 2)), dma((BALANCES + 1, 2)),
        dma((2,)), dma((2,)),
        dma((BALANCES, 2)), dma((BALANCES, 2)),
        dma((len(NEIGHBOURS),)), dma((len(NEIGHBOURS),)),
        dma((BALANCES, len(NEIGHBOURS))), dma((BALANCES, len(NEIGHBOURS))),
    ]
    return pl.pallas_call(
        kernel,
        out_shape=(shape, shape),
        in_specs=[vmem] * 11,
        out_specs=(vmem, vmem),
        scratch_shapes=scratch,
        compiler_params=pltpu.CompilerParams(
            collective_id=0, has_side_effects=True, vmem_limit_bytes=48 * 1024 * 1024
        ),
    )(
        flow_state, circ_speed, axial_speed, time_step, lsq_weights,
        partner.reshape(1, columns), partner.reshape(TILES, LANES),
        merge_owner.reshape(1, SMALL), merge_source.reshape(1, SMALL),
        merge_host.reshape(1, SMALL), merge_frac,
    )


def solution(mesh):
    in_specs = (
        P(None, "circ", "axial"),
        P("circ", "axial"),
        P("circ", "axial"),
        P("circ", "axial"),
        P("axial", None, None),
        P("axial"),
        P(("circ", "axial"), None),
        P(("circ", "axial")),
        P(("circ", "axial")),
        P(("circ", "axial"), None),
    )
    out_specs = (P(None, "circ", "axial"), P(None, "circ", "axial"))
    return jax.shard_map(local, mesh=mesh, in_specs=in_specs, out_specs=out_specs, check_vma=False)
```

```python
import jax
import jax.numpy as jnp
from jax import lax
from jax.experimental import pallas as pl
from jax.experimental.pallas import tpu as pltpu
from jax.sharding import PartitionSpec as P

STEPS = 2
BALANCES = 2 * STEPS
CAP = 8
NV = 5
ROWS = 16
LANES = 128
TILES = 16
HALF = 64
SMALL = 128
BLOCKS = 32
N_CIRC = 16
N_AXIAL = 8
STACK = NV * ROWS
WIDE = NV * LANES
ROW_TILES = 20
EARLY = 17
FIRST = 8
MESH = pl.DeviceIdType.MESH
F32 = jnp.float32
BF16 = jnp.bfloat16
NEIGHBOURS = [(dc, da) for dc in (-1, 0, 1) for da in (-1, 0, 1) if (dc, da) != (0, 0)]


def split(x):
    high = x.astype(BF16)
    return high, (x - high.astype(F32)).astype(BF16)


def lanes_of(shape):
    return lax.broadcasted_iota(jnp.int32, shape, len(shape) - 1)


def rolled(x, steps):
    return pltpu.roll(x, steps, x.ndim - 1)


def var_rows(v):
    return slice(v * ROWS, (v + 1) * ROWS)


def var_lanes(v):
    return slice(v * LANES, (v + 1) * LANES)


def cells(p):
    return slice(p * LANES, (p + 1) * LANES)


def kernel(
    flow_hbm, cspd_hbm, aspd_hbm, dt_hbm, w_hbm, prow_hbm, ptile_hbm, owner_hbm, source_hbm,
    host_hbm, frac_hbm,
    out_u, out_rate,
    flow, cspd, aspd, dt, w, partner_row, partner_tile, owner, source, host, frac, load_sem,
    cur, base, cs, xs, wts, s32, shi, slo, rc, gout, gloc, fout, floc, a_loc, a_arr, c_loc, c_arr,
    edges, consts, f_keep, halo, perm,
    ax_send, ax_recv, ini_send, ini_recv, row_send, row_recv, ci_send, ci_recv, lab_send, lab_recv, outbox, inbox,
    ax_ss, ax_rs, ini_ss, ini_rs, row_ss, row_rs, ci_ss, ci_rs, lab_ss, lab_rs, box_ss, box_rs,
):
    c = lax.axis_index("circ")
    a = lax.axis_index("axial")

    def peer(dc, da):
        return (lax.rem(c + dc + N_CIRC, N_CIRC), lax.rem(a + da + N_AXIAL, N_AXIAL))

    def remote(src, dst, send, recv, dc, da):
        return pltpu.make_async_remote_copy(
            src_ref=src, dst_ref=dst, send_sem=send, recv_sem=recv,
            device_id=peer(dc, da), device_id_type=MESH,
        )

    def axial_copy(n, side):
        return remote(
            ax_send.at[n, side], ax_recv.at[n, side], ax_ss.at[n, side], ax_rs.at[n, side],
            0, 2 * side - 1,
        )

    def init_copy(side):
        return remote(
            ini_send.at[side], ini_recv.at[side], ini_ss.at[side], ini_rs.at[side], 0, 2 * side - 1
        )

    def circ_copy(n, side, late):
        part = pl.ds(EARLY, ROW_TILES - EARLY) if late else pl.ds(0, EARLY)
        return remote(
            ci_send.at[n, side, part], ci_recv.at[n, side, part],
            ci_ss.at[n, side, late], ci_rs.at[n, side, late], 2 * side - 1, 0,
        )

    def row_copy():
        return remote(row_send, row_recv, row_ss.at[0], row_rs.at[0], 1, 0)

    def label_copy(k):
        dc, da = NEIGHBOURS[k]
        rows = pl.ds(k * CAP, CAP)
        return remote(lab_send.at[rows], lab_recv.at[rows], lab_ss.at[k], lab_rs.at[k], dc, da)

    def box_copy(n, k):
        dc, da = NEIGHBOURS[k]
        rows = pl.ds(k * CAP, CAP)
        return remote(
            outbox.at[n, rows], inbox.at[n, rows], box_ss.at[n, k], box_rs.at[n, k], dc, da
        )

    own = slice(FIRST, FIRST + ROWS)
    lane = lanes_of((ROWS, LANES))

    loads = [
        pltpu.make_async_copy(src, dst, load_sem.at[i])
        for i, (src, dst) in enumerate(
            (
                (owner_hbm, owner), (source_hbm, source), (host_hbm, host), (flow_hbm, flow),
                (dt_hbm, dt), (aspd_hbm, aspd), (cspd_hbm, cspd), (frac_hbm, frac),
                (prow_hbm, partner_row), (ptile_hbm, partner_tile), (w_hbm, w),
            )
        )
    ]
    for load in loads:
        load.start()

    barrier = pltpu.get_barrier_semaphore()
    for dc, da in NEIGHBOURS:
        pl.semaphore_signal(barrier, inc=1, device_id=peer(dc, da), device_id_type=MESH)

    def pair_place(p, v):
        slot = p - 1 if 0 < p < TILES - 1 else TILES - 2 + p // (TILES - 1)
        if v < NV - 1:
            return (slot if slot < TILES - 2 else slot + 3), 2 * v
        group = slot // 4
        return (TILES - 2 + group if group < 3 else ROW_TILES - 1), 2 * (slot % 4)

    def pack_rows(n, p, v, tile):
        where, row = pair_place(p, v)
        ci_send[n, 0, where, row:row + 2, :] = tile[0:2]
        ci_send[n, 1, where, row:row + 2, :] = tile[ROWS - 2:ROWS]

    def shift(q, v, left_tile, right_tile):
        moved = rolled(jnp.where(lane >= HALF, left_tile, right_tile), HALF)
        high, low = split(moved)
        xs[q, var_rows(v), :] = high
        xs[q, STACK + v * ROWS:STACK + (v + 1) * ROWS, :] = low

    for load in loads[:3]:
        load.wait()
    square = (SMALL, SMALL)
    t_row = owner[...]
    s_row = source[...]
    h_row = host[...]

    def as_columns(row):
        return jnp.broadcast_to(row.astype(F32), square).T.astype(jnp.int32)

    t_col, s_col, h_col = as_columns(t_row), as_columns(s_row), as_columns(h_row)
    myself = c * N_AXIAL + a
    first = lax.broadcasted_iota(jnp.int32, square, 0)
    second = lax.broadcasted_iota(jnp.int32, square, 1)
    shares = jnp.where((jnp.broadcast_to(t_row, square) == t_col) & (first < second), 1.0, 0.0)
    rank = jnp.sum(shares, axis=0, keepdims=True).astype(jnp.int32)
    circ_off = ((t_row >> 3) - c + 1 + N_CIRC) & (N_CIRC - 1)
    number = circ_off * 3 + (t_row & (N_AXIAL - 1)) - a + 1
    number = jnp.where(number > 4, number - 1, number)
    place = jnp.where(t_row == myself, -1, number * CAP + rank)
    slots = len(NEIGHBOURS) * CAP
    chosen = jnp.where(
        jnp.broadcast_to(place, (slots, SMALL))
        == lax.broadcasted_iota(jnp.int32, (slots, SMALL), 0),
        1.0, 0.0,
    )

    def row_index(s):
        return ((s & (BLOCKS - 1)) >> 1) * ROWS + (s >> 5)

    host_index = row_index(h_row)
    labels = jnp.sum(chosen * (host_index + 1).astype(F32), axis=1, keepdims=True) - 1.0
    lab_send[...] = jnp.broadcast_to(labels, (slots, LANES))

    for load in loads[3:7]:
        load.wait()
    for v in range(NV):
        first_tile = flow[v, :, 0:LANES]
        last_tile = flow[v, :, (TILES - 1) * LANES:]
        ax_send[0, 0, var_rows(v), :] = jnp.where(lane < HALF, first_tile, 0.0)
        ax_send[0, 1, var_rows(v), :] = jnp.where(lane >= HALF, last_tile, 0.0)
    ini_send[0, 0] = dt[:, 0:LANES]
    ini_send[0, 1] = dt[:, 0:LANES]
    ini_send[1, 0] = dt[:, (TILES - 1) * LANES:]
    ini_send[1, 1] = aspd[:, (TILES - 1) * LANES:]
    edges[...] = jnp.zeros_like(edges)
    pl.semaphore_wait(barrier, len(NEIGHBOURS))
    for side in range(2):
        axial_copy(0, side).start()
        init_copy(side).start()
    for p in range(TILES):
        columns = slice(p * LANES, (p + 1) * LANES)
        speed = cspd[:, columns]
        cs[p, own, :] = speed
        row_send[p:p + 1, :] = speed[ROWS - 1:ROWS]
    row_copy().start()
    for v in range(NV):
        before = None
        for p in range(TILES):
            tile = flow[v, :, p * LANES:(p + 1) * LANES]
            cur[p, v, own, :] = tile
            pack_rows(0, p, v, tile)
            if p > 0:
                shift(p, v, before, tile)
            before = tile
    for side in range(2):
        circ_copy(0, side, 0).start()
    for k in range(len(NEIGHBOURS)):
        label_copy(k).start()

    for load in loads[7:10]:
        load.wait()
    frac_twice = jnp.concatenate([frac[...], frac[...]], axis=0).T
    placed = jnp.where((second >> 6) == (h_col & 1), frac_twice, 0.0)
    same_half = (s_col & 1) == (h_col & 1)
    straight = jnp.where(same_half, placed, 0.0)
    crossed = jnp.where(same_half, 0.0, placed)
    is_local = t_col == myself
    floc[0] = jnp.where(is_local, straight, 0.0)
    floc[1] = jnp.where(is_local, crossed, 0.0)
    fout[0] = jnp.dot(chosen, straight, precision=lax.Precision.HIGHEST)
    fout[1] = jnp.dot(chosen, crossed, precision=lax.Precision.HIGHEST)
    s_index = row_index(s_col)
    pick = jnp.concatenate(
        [
            jnp.where(s_index == second, 1.0, 0.0),
            jnp.where(s_index == second + LANES, 1.0, 0.0),
        ],
        axis=1,
    ).astype(BF16)
    gloc[...] = pick
    gout[...] = jnp.dot(chosen.astype(BF16), pick, preferred_element_type=F32).astype(BF16)
    tall = (TILES * ROWS, SMALL)
    tall_rows = lax.broadcasted_iota(jnp.int32, tall, 0)
    wanted = jnp.where(t_row == myself, host_index, -1)
    land = jnp.where(jnp.broadcast_to(wanted, tall) == tall_rows, 1.0, 0.0).astype(BF16)
    a_loc[...] = jnp.concatenate([land, land], axis=1)

    @pl.when(c > 0)
    def _():
        perm[0] = partner_tile[...] >> 7
        perm[1] = partner_tile[...] & (LANES - 1)

    @pl.when(c == 0)
    def _():
        columns = TILES * LANES
        target = partner_row[...]
        upper = jnp.where(
            jnp.broadcast_to(target >> 7, (TILES, columns))
            == lax.broadcasted_iota(jnp.int32, (TILES, columns), 0),
            1.0, 0.0,
        ).astype(BF16)
        tall_lanes = (LANES, columns)
        here = jnp.broadcast_to(target & (LANES - 1), tall_lanes) == lax.broadcasted_iota(
            jnp.int32, tall_lanes, 0
        )
        position = lanes_of(tall_lanes)
        for part, value in enumerate((position >> 7, position & (LANES - 1))):
            lower = jnp.where(here, value.astype(F32), 0.0).astype(BF16)
            perm[part] = lax.dot_general(
                upper, lower, (((1,), (1,)), ((), ())), preferred_element_type=F32
            ).astype(jnp.int32)

    def weigh(p, _):
        gap = jnp.zeros((HALF, HALF), F32)
        both = jnp.concatenate(
            [
                jnp.concatenate([w[2 * p], gap], axis=1),
                jnp.concatenate([gap, w[2 * p + 1]], axis=1),
            ],
            axis=0,
        )
        high, low = split(both.T)
        wts[p, :, 0:LANES] = high
        wts[p, :, LANES:] = low
        return 0

    loads[10].wait()
    lax.fori_loop(0, TILES, weigh, 0)

    for k in range(len(NEIGHBOURS)):
        label_copy(k).wait()
    arrived_labels = lab_recv[...].astype(jnp.int32)
    label_row = (
        jnp.concatenate([arrived_labels, arrived_labels], axis=0).astype(F32).T.astype(jnp.int32)
    )
    a_arr[...] = jnp.where(
        jnp.concatenate([label_row, label_row], axis=0) == tall_rows, 1.0, 0.0
    ).astype(BF16)
    for side in range(2):
        init_copy(side).wait()
    consts[0] = jnp.where(a > 0, ini_recv[1, 0], 0.0)
    consts[1] = jnp.where(a < N_AXIAL - 1, ini_recv[0, 0], 0.0)
    consts[2] = jnp.where((a > 0) & (lane == 0), rolled(ini_recv[1, 1], 1), 0.0)
    consts[3] = jnp.where(lane == LANES - 1, aspd[:, (TILES - 1) * LANES:], 0.0)

    row_copy().wait()
    for half in range(2):
        some = slice(half * 8, half * 8 + 8)
        below_row = row_recv[some, :]
        mixed = jnp.zeros_like(below_row)
        for q in range(TILES):
            found = jnp.take_along_axis(
                jnp.broadcast_to(row_recv[q:q + 1, :], below_row.shape), perm[1, some, :], axis=1
            )
            mixed = jnp.where(perm[0, some, :] == q, found, mixed)
        below_row = jnp.where(c == 0, mixed, below_row)
        for k in range(8):
            cs[half * 8 + k, FIRST - 1:FIRST, :] = below_row[k:k + 1]

    def fix_edges(n, factor, also_rate):
        for side in range(2):
            axial_copy(n, side).wait()
        left_speed, right_speed = consts[2], consts[3]
        last = (TILES - 1) * LANES
        for v in range(NV):
            vr = var_rows(v)
            from_left = jnp.where(a > 0, ax_recv[n, 1, vr, :], 0.0)
            from_right = jnp.where(a < N_AXIAL - 1, ax_recv[n, 0, vr, :], 0.0)
            left_flux = jnp.maximum(left_speed, 0.0) * from_left + jnp.minimum(
                left_speed, 0.0
            ) * edges[0, vr, :]
            right_flux = jnp.maximum(right_speed, 0.0) * edges[1, vr, :] + jnp.minimum(
                right_speed, 0.0
            ) * from_right
            cur[0, v, own, :] = cur[0, v, own, :] + factor * dt[:, 0:LANES] * left_flux
            cur[TILES - 1, v, own, :] = (
                cur[TILES - 1, v, own, :] - factor * dt[:, last:] * right_flux
            )
            if also_rate:
                out_rate[v, :, 0:LANES] = out_rate[v, :, 0:LANES] - left_flux
                out_rate[v, :, last:] = out_rate[v, :, last:] + right_flux
            else:
                halo[0, v] = from_left - factor * consts[0] * rolled(left_flux, LANES - 1)
                halo[1, v] = from_right + factor * consts[1] * rolled(right_flux, 1)

    def slopes(p):
        left = jnp.concatenate([xs[p], xs[p + 1]], axis=1)
        full = jnp.dot(left, wts[p], preferred_element_type=F32)
        total = full[:STACK, :LANES] + full[:STACK, LANES:] + full[STACK:, :LANES]
        s32[p] = total
        high, low = split(total)
        rows = slice(p * ROWS, (p + 1) * ROWS)
        for v in range(NV):
            shi[rows, var_lanes(v)] = high[var_rows(v)]
            slo[rows, var_lanes(v)] = low[var_rows(v)]

    def gathered(picks, factors, v):
        vl = var_lanes(v)
        picked = jnp.dot(picks[...], shi[:, vl], preferred_element_type=F32) + jnp.dot(
            picks[...], slo[:, vl], preferred_element_type=F32
        )
        return picked * factors[0] + rolled(picked, HALF) * factors[1]

    def scatter(matrix, values, v):
        added = jnp.dot(matrix[...], values[:, var_lanes(v)], preferred_element_type=F32)
        for p in range(TILES):
            s32[p, var_rows(v), :] = s32[p, var_rows(v), :] + added[p * ROWS:(p + 1) * ROWS]

    def late_rows(n):
        for v in range(NV):
            for p in (0, TILES - 1):
                pack_rows(n, p, v, cur[p, v, own, :])

    def unpack(n, side):
        start = FIRST - 2 if side else FIRST + ROWS
        for p in range(TILES):
            for v in range(NV):
                where, row = pair_place(p, v)
                cur[p, v, start:start + 2, :] = ci_recv[n, side, where, row:row + 2, :]

    def permute(n, side):
        start = FIRST - 2 if side else FIRST + ROWS
        rows = lax.broadcasted_iota(jnp.int32, (8, LANES), 0)
        slot_of = [p - 1 if 0 < p < TILES - 1 else TILES - 2 + p // (TILES - 1) for p in range(TILES)]

        def one(p):
            tile = jnp.broadcast_to(perm[0, pl.ds(p, 1), :], (8, LANES))
            column = jnp.broadcast_to(perm[1, pl.ds(p, 1), :], (8, LANES))
            slot = jnp.where(
                tile == 0, TILES - 2, jnp.where(tile == TILES - 1, TILES - 1, tile - 1)
            )
            total = jnp.zeros((8, LANES), F32)
            for q in range(TILES):
                where, _ = pair_place(q, 0)
                found = jnp.take_along_axis(ci_recv[n, side, where], column, axis=1)
                total = jnp.where(slot == slot_of[q], found, total)
            last = jnp.zeros((8, LANES), F32)
            offset = slot - (rows >> 1)
            for g in range(4):
                where = TILES - 2 + g if g < 3 else ROW_TILES - 1
                found = jnp.take_along_axis(ci_recv[n, side, where], column, axis=1)
                last = jnp.where(offset == 4 * g, found, last)
            last = last + pltpu.roll(last, 4, 0)
            last = last + pltpu.roll(last, 2, 0)
            for v in range(NV - 1):
                cur[p, v, start:start + 2, :] = total[2 * v:2 * v + 2]
            cur[p, NV - 1, start:start + 2, :] = last[0:2]

        def four(i, _):
            for k in range(4):
                one(4 * i + k)
            return 0

        lax.fori_loop(0, TILES // 4, four, 0)

    def circ_rates(p, _):
        above = cs[p, own, :]
        below = cs[p, FIRST - 1:FIRST + ROWS - 1, :]
        above_pos, above_neg = jnp.maximum(above, 0.0), jnp.minimum(above, 0.0)
        below_pos, below_neg = jnp.maximum(below, 0.0), jnp.minimum(below, 0.0)
        for v in range(NV):
            at = [cur[p, v, FIRST + k:FIRST + k + ROWS, :] for k in (-2, -1, 0, 1, 2)]
            slope_below = 0.25 * (at[2] - at[0])
            slope_here = 0.25 * (at[3] - at[1])
            slope_above = 0.25 * (at[4] - at[2])
            upper = above_pos * (at[2] + slope_here) + above_neg * (at[3] - slope_above)
            lower = below_pos * (at[1] + slope_below) + below_neg * (at[2] - slope_here)
            rc[p, var_rows(v), :] = upper - lower
        return 0

    def face(p, v, kind):
        half_slope = 0.5 * s32[p, var_rows(v), :]
        here = cur[p, v, own, :]
        return here + half_slope if kind == 0 else here - half_slope

    def flux(p, v, right_lane):
        speed = aspd[:, cells(p)]
        right = rolled(jnp.where(lane == 0, right_lane, face(p, v, 1)), LANES - 1)
        return jnp.maximum(speed, 0.0) * face(p, v, 0) + jnp.minimum(speed, 0.0) * right

    def advance(p, v, flux_here, flux_left, first_stage, factor):
        before = rolled(jnp.where(lane == LANES - 1, flux_left, flux_here), 1)
        rate = rc[p, var_rows(v), :] + flux_here - before
        here = cur[p, v, own, :]
        start = jnp.where(first_stage, here, base[p, var_rows(v), :])
        base[p, var_rows(v), :] = start
        out_rate[v, :, cells(p)] = rate
        new = 0.5 * (start + here) - factor * (dt[:, cells(p)] * rate)
        cur[p, v, own, :] = new
        return new

    def balance(n, _):
        odd = lax.rem(n, 2)
        first_stage = odd == 0
        factor = jnp.where(first_stage, 1.0, 0.5).astype(F32)
        earlier = jnp.where(first_stage, 0.5, 1.0).astype(F32)
        end = TILES - 1

        for p in range(1, end):
            slopes(p)
        fix_edges(n, earlier, False)
        for v in range(NV):
            shift(0, v, halo[0, v], cur[0, v, own, :])
            shift(TILES, v, cur[end, v, own, :], halo[1, v])
        late_rows(n)
        for side in range(2):
            circ_copy(n, side, 1).start()
        slopes(0)
        slopes(end)

        for v in range(NV):
            outbox[n, :, var_lanes(v)] = gathered(gout, fout, v)
        for k in range(len(NEIGHBOURS)):
            box_copy(n, k).start()

        for v in range(NV):
            high, low = split(gathered(gloc, floc, v))
            c_loc[:SMALL, var_lanes(v)] = high
            c_loc[SMALL:, var_lanes(v)] = low
        for v in range(NV):
            scatter(a_loc, c_loc, v)

        for side in range(2):
            for late in range(2):
                circ_copy(n, side, late).wait()

        @pl.when(c > 0)
        def _():
            unpack(n, 1)

        @pl.when(c < N_CIRC - 1)
        def _():
            unpack(n, 0)

        @pl.when(c == 0)
        def _():
            permute(n, 1)

        @pl.when(c == N_CIRC - 1)
        def _():
            permute(n, 0)

        for p in range(TILES):
            circ_rates(p, 0)

        for k in range(len(NEIGHBOURS)):
            box_copy(n, k).wait()
        for v in range(NV):
            high, low = split(inbox[n, :, var_lanes(v)])
            c_arr[:slots, var_lanes(v)] = high
            c_arr[slots:, var_lanes(v)] = low
        for v in range(NV):
            scatter(a_arr, c_arr, v)

        for v in range(NV):
            vr = var_rows(v)
            right_face = face(0, v, 1)
            flux_first = flux(0, v, face(1, v, 1))
            left_face = face(end, v, 0)
            flux_before = flux(end - 1, v, face(end, v, 1))
            flux_last = jnp.where(lane == LANES - 1, 0.0, flux(end, v, 0.0))
            edges[0, vr, :] = right_face
            edges[1, vr, :] = left_face
            f_keep[0, vr, :] = flux_first
            f_keep[1, vr, :] = flux_before
            new_first = advance(0, v, flux_first, 0.0, first_stage, factor)
            new_last = advance(end, v, flux_last, flux_before, first_stage, factor)
            ax_send[n + 1, 0, vr, :] = jnp.where(
                lane < HALF, new_first, rolled(right_face, LANES - 1)
            )
            ax_send[n + 1, 1, vr, :] = jnp.where(lane >= HALF, new_last, rolled(left_face, 1))
        for side in range(2):
            axial_copy(n + 1, side).start()

        for v in range(NV):
            before = f_keep[0, var_rows(v), :]
            tile = cur[0, v, own, :]
            for p in range(1, end):
                here = flux(p, v, face(p + 1, v, 1)) if p < end - 1 else f_keep[1, var_rows(v), :]
                new = advance(p, v, here, before, first_stage, factor)
                pack_rows(n + 1, p, v, new)
                shift(p, v, tile, new)
                before, tile = here, new
            shift(end, v, tile, cur[end, v, own, :])

        @pl.when(n < BALANCES - 1)
        def _():
            for side in range(2):
                circ_copy(n + 1, side, 0).start()

        return 0

    lax.fori_loop(0, BALANCES, balance, 0)
    fix_edges(BALANCES, jnp.float32(0.5), True)

    for p in range(TILES):
        for v in range(NV):
            out_u[v, :, cells(p)] = cur[p, v, own, :]


def local(
    flow_state, circ_speed, axial_speed, time_step, lsq_weights,
    partner, merge_owner, merge_source, merge_host, merge_frac,
):
    columns = TILES * LANES
    slots = len(NEIGHBOURS) * CAP
    vmem = pl.BlockSpec(memory_space=pltpu.VMEM)
    hbm = pl.BlockSpec(memory_space=pltpu.HBM)
    dma = pltpu.SemaphoreType.DMA
    shape = jax.ShapeDtypeStruct((NV, ROWS, columns), F32)
    scratch = [
        pltpu.VMEM((NV, ROWS, columns), F32),
        pltpu.VMEM((ROWS, columns), F32),
        pltpu.VMEM((ROWS, columns), F32),
        pltpu.VMEM((ROWS, columns), F32),
        pltpu.VMEM((BLOCKS, HALF, 3 * HALF), F32),
        pltpu.VMEM((1, columns), jnp.int32),
        pltpu.VMEM((TILES, LANES), jnp.int32),
        pltpu.VMEM((1, SMALL), jnp.int32),
        pltpu.VMEM((1, SMALL), jnp.int32),
        pltpu.VMEM((1, SMALL), jnp.int32),
        pltpu.VMEM((HALF, SMALL), F32),
        dma((11,)),
        pltpu.VMEM((TILES, NV, 2 * ROWS, LANES), F32),
        pltpu.VMEM((TILES, STACK, LANES), F32),
        pltpu.VMEM((TILES, 2 * ROWS, LANES), F32),
        pltpu.VMEM((TILES + 1, 2 * STACK, LANES), BF16),
        pltpu.VMEM((TILES, 2 * LANES, 2 * LANES), BF16),
        pltpu.VMEM((TILES, STACK, LANES), F32),
        pltpu.VMEM((TILES * ROWS, WIDE), BF16),
        pltpu.VMEM((TILES * ROWS, WIDE), BF16),
        pltpu.VMEM((TILES, STACK, LANES), F32),
        pltpu.VMEM((slots, TILES * ROWS), BF16),
        pltpu.VMEM((SMALL, TILES * ROWS), BF16),
        pltpu.VMEM((2, slots, LANES), F32),
        pltpu.VMEM((2, SMALL, LANES), F32),
        pltpu.VMEM((TILES * ROWS, 2 * SMALL), BF16),
        pltpu.VMEM((TILES * ROWS, 2 * slots), BF16),
        pltpu.VMEM((2 * SMALL, WIDE), BF16),
        pltpu.VMEM((2 * slots, WIDE), BF16),
        pltpu.VMEM((2, STACK, LANES), F32),
        pltpu.VMEM((4, ROWS, LANES), F32),
        pltpu.VMEM((2, STACK, LANES), F32),
        pltpu.VMEM((2, NV, ROWS, LANES), F32),
        pltpu.VMEM((2, TILES, LANES), jnp.int32),
        pltpu.VMEM((BALANCES + 1, 2, STACK, LANES), F32),
        pltpu.VMEM((BALANCES + 1, 2, STACK, LANES), F32),
        pltpu.VMEM((2, 2, ROWS, LANES), F32),
        pltpu.VMEM((2, 2, ROWS, LANES), F32),
        pltpu.VMEM((TILES, LANES), F32),
        pltpu.VMEM((TILES, LANES), F32),
        pltpu.VMEM((BALANCES + 1, 2, ROW_TILES, 8, LANES), F32),
        pltpu.VMEM((BALANCES, 2, ROW_TILES, 8, LANES), F32),
        pltpu.VMEM((slots, LANES), F32),
        pltpu.VMEM((slots, LANES), F32),
        pltpu.VMEM((BALANCES, slots, WIDE), F32),
        pltpu.VMEM((BALANCES, slots, WIDE), F32),
        dma((BALANCES + 1, 2)), dma((BALANCES + 1, 2)),
        dma((2,)), dma((2,)),
        dma((1,)), dma((1,)),
        dma((BALANCES, 2, 2)), dma((BALANCES, 2, 2)),
        dma((len(NEIGHBOURS),)), dma((len(NEIGHBOURS),)),
        dma((BALANCES, len(NEIGHBOURS))), dma((BALANCES, len(NEIGHBOURS))),
    ]
    return pl.pallas_call(
        kernel,
        out_shape=(shape, shape),
        in_specs=[hbm] * 11,
        out_specs=(vmem, vmem),
        scratch_shapes=scratch,
        compiler_params=pltpu.CompilerParams(
            collective_id=0, has_side_effects=True, vmem_limit_bytes=56 * 1024 * 1024
        ),
    )(
        flow_state, circ_speed, axial_speed, time_step, lsq_weights,
        partner.reshape(1, columns), partner.reshape(TILES, LANES),
        merge_owner.reshape(1, SMALL), merge_source.reshape(1, SMALL),
        merge_host.reshape(1, SMALL), merge_frac.T,
    )


def solution(mesh):
    in_specs = (
        P(None, "circ", "axial"),
        P("circ", "axial"),
        P("circ", "axial"),
        P("circ", "axial"),
        P("axial", None, None),
        P("axial"),
        P(("circ", "axial"), None),
        P(("circ", "axial")),
        P(("circ", "axial")),
        P(("circ", "axial"), None),
    )
    out_specs = (P(None, "circ", "axial"), P(None, "circ", "axial"))
    return jax.shard_map(local, mesh=mesh, in_specs=in_specs, out_specs=out_specs, check_vma=False)
```

```python
import jax
import jax.numpy as jnp
from jax import lax
from jax.experimental import pallas as pl
from jax.experimental.pallas import tpu as pltpu
from jax.sharding import PartitionSpec as P

STEPS = 2
BALANCES = 2 * STEPS
CAP = 8
NV = 5
ROWS = 16
LANES = 128
TILES = 16
HALF = 64
SMALL = 128
BLOCKS = 32
N_CIRC = 16
N_AXIAL = 8
STACK = NV * ROWS
WIDE = NV * LANES
ROW_TILES = 20
EARLY = 17
FIRST = 8
MESH = pl.DeviceIdType.MESH
F32 = jnp.float32
BF16 = jnp.bfloat16
NEIGHBOURS = [(dc, da) for dc in (-1, 0, 1) for da in (-1, 0, 1) if (dc, da) != (0, 0)]
DIRECT = [(-1, 0), (1, 0), (0, -1), (0, 1)]
FAR_FIRST = (0, 2, 5, 7, 1, 6, 3, 4)


def split(x):
    high = x.astype(BF16)
    return high, (x - high.astype(F32)).astype(BF16)


def lanes_of(shape):
    return lax.broadcasted_iota(jnp.int32, shape, len(shape) - 1)


def rolled(x, steps):
    return pltpu.roll(x, steps, x.ndim - 1)


def var_rows(v):
    return slice(v * ROWS, (v + 1) * ROWS)


def var_lanes(v):
    return slice(v * LANES, (v + 1) * LANES)


def cells(p):
    return slice(p * LANES, (p + 1) * LANES)


def kernel(
    flow_hbm, cspd_hbm, aspd_hbm, dt_hbm, w_hbm, prow_hbm, ptile_hbm, owner_hbm, source_hbm,
    host_hbm, frac_hbm,
    out_u, out_rate,
    flow, cspd, aspd, dt, w, partner_row, partner_tile, owner, source, host, frac, load_sem,
    cur, base, cs, xs, wts, s32, shi, slo, rc, gout, gend, ends, gloc, fout, floc, a_loc, a_arr, a_edge, c_loc, c_arr,
    edges, consts, f_keep, halo, perm,
    ax_send, ax_recv, ini_recv, row_send, row_recv, ci_send, ci_recv, lab_send, lab_recv, outbox, inbox, early_box,
    ax_ss, ax_rs, ini_ss, ini_rs, row_ss, row_rs, ci_ss, ci_rs, lab_ss, lab_rs, box_ss, box_rs,
):
    c = lax.axis_index("circ")
    a = lax.axis_index("axial")

    def peer(dc, da):
        return (lax.rem(c + dc + N_CIRC, N_CIRC), lax.rem(a + da + N_AXIAL, N_AXIAL))

    def remote(src, dst, send, recv, dc, da):
        return pltpu.make_async_remote_copy(
            src_ref=src, dst_ref=dst, send_sem=send, recv_sem=recv,
            device_id=peer(dc, da), device_id_type=MESH,
        )

    def axial_copy(n, side):
        return remote(
            ax_send.at[n, side], ax_recv.at[n, side], ax_ss.at[n, side], ax_rs.at[n, side],
            0, 2 * side - 1,
        )

    head, tail = pl.ds(0, LANES), pl.ds((TILES - 1) * LANES, LANES)

    def first_axial_copy(side):
        return remote(
            flow_hbm.at[:, :, tail if side else head], ax_recv.at[0, side],
            ax_ss.at[0, side], ax_rs.at[0, side], 0, 2 * side - 1,
        )

    def init_copy(k):
        source_of = (dt_hbm.at[:, head], dt_hbm.at[:, tail], aspd_hbm.at[:, tail])
        return remote(
            source_of[k], ini_recv.at[k], ini_ss.at[k], ini_rs.at[k], 0, 1 if k else -1
        )

    def circ_copy(n, side, late):
        part = pl.ds(EARLY, ROW_TILES - EARLY) if late else pl.ds(0, EARLY)
        return remote(
            ci_send.at[n, side, part], ci_recv.at[n, side, part],
            ci_ss.at[n, side, late], ci_rs.at[n, side, late], 2 * side - 1, 0,
        )

    def row_copy():
        return remote(row_send, row_recv, row_ss.at[0], row_rs.at[0], 1, 0)

    def label_copy(k):
        dc, da = NEIGHBOURS[k]
        rows = pl.ds(k * CAP, CAP)
        return remote(lab_send.at[rows], lab_recv.at[rows], lab_ss.at[k], lab_rs.at[k], dc, da)

    def box_copy(n, k):
        dc, da = NEIGHBOURS[k]
        rows = pl.ds(k * CAP, CAP)
        return remote(
            outbox.at[n, rows], inbox.at[n, rows], box_ss.at[n, k], box_rs.at[n, k], dc, da
        )

    own = slice(FIRST, FIRST + ROWS)
    lane = lanes_of((ROWS, LANES))

    loads = [
        pltpu.make_async_copy(src, dst, load_sem.at[i])
        for i, (src, dst) in enumerate(
            (
                (owner_hbm, owner), (source_hbm, source), (host_hbm, host), (flow_hbm, flow),
                (dt_hbm, dt), (aspd_hbm, aspd), (cspd_hbm, cspd), (frac_hbm, frac),
                (prow_hbm, partner_row), (ptile_hbm, partner_tile), (w_hbm, w),
            )
        )
    ]
    for load in loads:
        load.start()

    barrier = pltpu.get_barrier_semaphore()
    for dc, da in DIRECT:
        pl.semaphore_signal(barrier, inc=1, device_id=peer(dc, da), device_id_type=MESH)

    def pair_place(p, v):
        slot = p - 1 if 0 < p < TILES - 1 else TILES - 2 + p // (TILES - 1)
        if v < NV - 1:
            return (slot if slot < TILES - 2 else slot + 3), 2 * v
        group = slot // 4
        return (TILES - 2 + group if group < 3 else ROW_TILES - 1), 2 * (slot % 4)

    def pack_rows(n, p, v, tile):
        where, row = pair_place(p, v)
        ci_send[n, 0, where, row:row + 2, :] = tile[0:2]
        ci_send[n, 1, where, row:row + 2, :] = tile[ROWS - 2:ROWS]

    def shift(q, v, left_tile, right_tile):
        moved = rolled(jnp.where(lane >= HALF, left_tile, right_tile), HALF)
        high, low = split(moved)
        xs[q, var_rows(v), :] = high
        xs[q, STACK + v * ROWS:STACK + (v + 1) * ROWS, :] = low

    for load in loads[:3]:
        load.wait()
    square = (SMALL, SMALL)
    t_row = owner[...]
    s_row = source[...]
    h_row = host[...]

    def as_columns(row):
        return jnp.broadcast_to(row.astype(F32), square).T.astype(jnp.int32)

    t_col, s_col, h_col = as_columns(t_row), as_columns(s_row), as_columns(h_row)
    myself = c * N_AXIAL + a
    first = lax.broadcasted_iota(jnp.int32, square, 0)
    second = lax.broadcasted_iota(jnp.int32, square, 1)
    shares = jnp.where((jnp.broadcast_to(t_row, square) == t_col) & (first < second), 1.0, 0.0)
    rank = jnp.sum(shares, axis=0, keepdims=True).astype(jnp.int32)
    circ_off = ((t_row >> 3) - c + 1 + N_CIRC) & (N_CIRC - 1)
    number = circ_off * 3 + (t_row & (N_AXIAL - 1)) - a + 1
    number = jnp.where(number > 4, number - 1, number)
    place = jnp.where(t_row == myself, -1, number * CAP + rank)
    slots = len(NEIGHBOURS) * CAP
    chosen = jnp.where(
        jnp.broadcast_to(place, (slots, SMALL))
        == lax.broadcasted_iota(jnp.int32, (slots, SMALL), 0),
        1.0, 0.0,
    )

    def row_index(s):
        return ((s & (BLOCKS - 1)) >> 1) * ROWS + (s >> 5)

    host_index = row_index(h_row)
    labels = jnp.sum(chosen * (host_index + 1).astype(F32), axis=1, keepdims=True) - 1.0
    lab_send[...] = jnp.broadcast_to(labels, (slots, LANES))

    edges[...] = jnp.zeros_like(edges)
    consts[...] = jnp.zeros_like(consts)
    pl.semaphore_wait(barrier, len(DIRECT))
    for side in range(2):
        first_axial_copy(side).start()
    for k in range(3):
        init_copy(k).start()
    for load in loads[3:7]:
        load.wait()
    for p in range(TILES):
        columns = slice(p * LANES, (p + 1) * LANES)
        speed = cspd[:, columns]
        cs[p, own, :] = speed
        row_send[p:p + 1, :] = speed[ROWS - 1:ROWS]
    row_copy().start()
    for v in range(NV):
        before = None
        for p in range(TILES):
            tile = flow[v, :, p * LANES:(p + 1) * LANES]
            cur[p, v, own, :] = tile
            pack_rows(0, p, v, tile)
            if p > 0:
                shift(p, v, before, tile)
            before = tile
    for side in range(2):
        circ_copy(0, side, 0).start()
    for load in loads[7:10]:
        load.wait()
    frac_twice = jnp.concatenate([frac[...], frac[...]], axis=0).T
    placed = jnp.where((second >> 6) == (h_col & 1), frac_twice, 0.0)
    same_half = (s_col & 1) == (h_col & 1)
    straight = jnp.where(same_half, placed, 0.0)
    crossed = jnp.where(same_half, 0.0, placed)
    is_local = t_col == myself
    floc[0] = jnp.where(is_local, straight, 0.0)
    floc[1] = jnp.where(is_local, crossed, 0.0)
    fout[0] = jnp.dot(chosen, straight, precision=lax.Precision.HIGHEST)
    fout[1] = jnp.dot(chosen, crossed, precision=lax.Precision.HIGHEST)
    s_index = row_index(s_col)
    pick = jnp.concatenate(
        [
            jnp.where(s_index == second, 1.0, 0.0),
            jnp.where(s_index == second + LANES, 1.0, 0.0),
        ],
        axis=1,
    ).astype(BF16)
    gloc[...] = pick
    picked_out = jnp.dot(chosen.astype(BF16), pick, preferred_element_type=F32)
    gout[...] = picked_out.astype(BF16)
    picked_end = jnp.concatenate([picked_out[:, :ROWS], picked_out[:, -ROWS:]], axis=1)
    gend[...] = jnp.concatenate([picked_end, picked_end], axis=1).astype(BF16)
    tall = (TILES * ROWS, SMALL)
    tall_rows = lax.broadcasted_iota(jnp.int32, tall, 0)
    wanted = jnp.where(t_row == myself, host_index, -1)
    land = jnp.where(jnp.broadcast_to(wanted, tall) == tall_rows, 1.0, 0.0).astype(BF16)
    a_loc[...] = jnp.concatenate([land, land], axis=1)

    @pl.when(c > 0)
    def _():
        perm[0] = partner_tile[...] >> 7
        perm[1] = partner_tile[...] & (LANES - 1)

    @pl.when(c == 0)
    def _():
        columns = TILES * LANES
        target = partner_row[...]
        upper = jnp.where(
            jnp.broadcast_to(target >> 7, (TILES, columns))
            == lax.broadcasted_iota(jnp.int32, (TILES, columns), 0),
            1.0, 0.0,
        ).astype(BF16)
        tall_lanes = (LANES, columns)
        here = jnp.broadcast_to(target & (LANES - 1), tall_lanes) == lax.broadcasted_iota(
            jnp.int32, tall_lanes, 0
        )
        position = lanes_of(tall_lanes)
        for part, value in enumerate((position >> 7, position & (LANES - 1))):
            lower = jnp.where(here, value.astype(F32), 0.0).astype(BF16)
            perm[part] = lax.dot_general(
                upper, lower, (((1,), (1,)), ((), ())), preferred_element_type=F32
            ).astype(jnp.int32)

    def weigh(p, _):
        gap = jnp.zeros((HALF, HALF), F32)
        both = jnp.concatenate(
            [
                jnp.concatenate([w[2 * p], gap], axis=1),
                jnp.concatenate([gap, w[2 * p + 1]], axis=1),
            ],
            axis=0,
        )
        high, low = split(both.T)
        wts[p, :, 0:LANES] = high
        wts[p, :, LANES:] = low
        return 0

    loads[10].wait()
    lax.fori_loop(0, TILES, weigh, 0)

    def receive_constants():
        for k in range(3):
            init_copy(k).wait()
        consts[0] = jnp.where(a > 0, ini_recv[1], 0.0)
        consts[1] = jnp.where(a < N_AXIAL - 1, ini_recv[0], 0.0)
        consts[2] = jnp.where((a > 0) & (lane == 0), rolled(ini_recv[2], 1), 0.0)
        consts[3] = jnp.where(lane == LANES - 1, aspd[:, (TILES - 1) * LANES:], 0.0)
        row_copy().wait()
        for half in range(2):
            some = slice(half * 8, half * 8 + 8)
            below_row = row_recv[some, :]
            mixed = jnp.zeros_like(below_row)
            for q in range(TILES):
                found = jnp.take_along_axis(
                    jnp.broadcast_to(row_recv[q:q + 1, :], below_row.shape), perm[1, some, :], axis=1
                )
                mixed = jnp.where(perm[0, some, :] == q, found, mixed)
            below_row = jnp.where(c == 0, mixed, below_row)
            for k in range(8):
                cs[half * 8 + k, FIRST - 1:FIRST, :] = below_row[k:k + 1]

    def receive_labels():
        for k in range(len(NEIGHBOURS)):
            label_copy(k).wait()
        arrived = lab_recv[...]
        label_row = jnp.concatenate([arrived, arrived], axis=0).T.astype(jnp.int32)
        land_here = jnp.where(
            jnp.concatenate([label_row, label_row], axis=0) == tall_rows, 1.0, 0.0
        ).astype(BF16)
        a_arr[...] = land_here[2 * ROWS:-2 * ROWS]
        a_edge[0:2 * ROWS, :] = land_here[0:2 * ROWS]
        a_edge[2 * ROWS:, :] = land_here[-2 * ROWS:]

    def fix_edges(n, factor, also_rate):
        for side in range(2):
            axial_copy(n, side).wait()
        left_speed, right_speed = consts[2], consts[3]
        last = (TILES - 1) * LANES
        for v in range(NV):
            vr = var_rows(v)
            from_left = jnp.where(a > 0, ax_recv[n, 1, v], 0.0)
            from_right = jnp.where(a < N_AXIAL - 1, ax_recv[n, 0, v], 0.0)
            left_flux = jnp.maximum(left_speed, 0.0) * from_left + jnp.minimum(
                left_speed, 0.0
            ) * edges[0, vr, :]
            right_flux = jnp.maximum(right_speed, 0.0) * edges[1, vr, :] + jnp.minimum(
                right_speed, 0.0
            ) * from_right
            cur[0, v, own, :] = cur[0, v, own, :] + factor * dt[:, 0:LANES] * left_flux
            cur[TILES - 1, v, own, :] = (
                cur[TILES - 1, v, own, :] - factor * dt[:, last:] * right_flux
            )
            if also_rate:
                out_rate[v, :, 0:LANES] = out_rate[v, :, 0:LANES] - left_flux
                out_rate[v, :, last:] = out_rate[v, :, last:] + right_flux
            else:
                halo[0, v] = from_left - factor * consts[0] * rolled(left_flux, LANES - 1)
                halo[1, v] = from_right + factor * consts[1] * rolled(right_flux, 1)

    def slopes(p):
        left = jnp.concatenate([xs[p], xs[p + 1]], axis=1)
        full = jnp.dot(left, wts[p], preferred_element_type=F32)
        total = full[:STACK, :LANES] + full[:STACK, LANES:] + full[STACK:, :LANES]
        s32[p] = total
        high, low = split(total)
        rows = slice(p * ROWS, (p + 1) * ROWS)
        for v in range(NV):
            shi[rows, var_lanes(v)] = high[var_rows(v)]
            slo[rows, var_lanes(v)] = low[var_rows(v)]
            if p in (0, TILES - 1):
                start = ROWS * (p // (TILES - 1))
                ends[start:start + ROWS, var_lanes(v)] = high[var_rows(v)]
                ends[2 * ROWS + start:3 * ROWS + start, var_lanes(v)] = low[var_rows(v)]

    def gathered(picks, factors, v):
        vl = var_lanes(v)
        picked = jnp.dot(picks[...], shi[:, vl], preferred_element_type=F32) + jnp.dot(
            picks[...], slo[:, vl], preferred_element_type=F32
        )
        return picked * factors[0] + rolled(picked, HALF) * factors[1]

    def scatter(matrix, values, v, tiles):
        added = jnp.dot(matrix[...], values[:, var_lanes(v)], preferred_element_type=F32)
        for i, p in enumerate(tiles):
            s32[p, var_rows(v), :] = s32[p, var_rows(v), :] + added[i * ROWS:(i + 1) * ROWS]

    def late_rows(n):
        for v in range(NV):
            for p in (0, TILES - 1):
                pack_rows(n, p, v, cur[p, v, own, :])

    def unpack(n, side):
        start = FIRST - 2 if side else FIRST + ROWS
        for p in range(TILES):
            for v in range(NV):
                where, row = pair_place(p, v)
                cur[p, v, start:start + 2, :] = ci_recv[n, side, where, row:row + 2, :]

    def permute(n, side):
        start = FIRST - 2 if side else FIRST + ROWS
        rows = lax.broadcasted_iota(jnp.int32, (8, LANES), 0)
        slot_of = [p - 1 if 0 < p < TILES - 1 else TILES - 2 + p // (TILES - 1) for p in range(TILES)]

        def one(p):
            tile = jnp.broadcast_to(perm[0, pl.ds(p, 1), :], (8, LANES))
            column = jnp.broadcast_to(perm[1, pl.ds(p, 1), :], (8, LANES))
            slot = jnp.where(
                tile == 0, TILES - 2, jnp.where(tile == TILES - 1, TILES - 1, tile - 1)
            )
            total = jnp.zeros((8, LANES), F32)
            for q in range(TILES):
                where, _ = pair_place(q, 0)
                found = jnp.take_along_axis(ci_recv[n, side, where], column, axis=1)
                total = jnp.where(slot == slot_of[q], found, total)
            last = jnp.zeros((8, LANES), F32)
            offset = slot - (rows >> 1)
            for g in range(4):
                where = TILES - 2 + g if g < 3 else ROW_TILES - 1
                found = jnp.take_along_axis(ci_recv[n, side, where], column, axis=1)
                last = jnp.where(offset == 4 * g, found, last)
            last = last + pltpu.roll(last, 4, 0)
            last = last + pltpu.roll(last, 2, 0)
            for v in range(NV - 1):
                cur[p, v, start:start + 2, :] = total[2 * v:2 * v + 2]
            cur[p, NV - 1, start:start + 2, :] = last[0:2]

        def four(i, _):
            for k in range(4):
                one(4 * i + k)
            return 0

        lax.fori_loop(0, TILES // 4, four, 0)

    def circ_rates(p, _):
        above = cs[p, own, :]
        below = cs[p, FIRST - 1:FIRST + ROWS - 1, :]
        above_pos, above_neg = jnp.maximum(above, 0.0), jnp.minimum(above, 0.0)
        below_pos, below_neg = jnp.maximum(below, 0.0), jnp.minimum(below, 0.0)
        for v in range(NV):
            at = [cur[p, v, FIRST + k:FIRST + k + ROWS, :] for k in (-2, -1, 0, 1, 2)]
            slope_below = 0.25 * (at[2] - at[0])
            slope_here = 0.25 * (at[3] - at[1])
            slope_above = 0.25 * (at[4] - at[2])
            upper = above_pos * (at[2] + slope_here) + above_neg * (at[3] - slope_above)
            lower = below_pos * (at[1] + slope_below) + below_neg * (at[2] - slope_here)
            rc[p, var_rows(v), :] = upper - lower
        return 0

    def face(p, v, kind):
        half_slope = 0.5 * s32[p, var_rows(v), :]
        here = cur[p, v, own, :]
        return here + half_slope if kind == 0 else here - half_slope

    def flux(p, v, right_lane):
        speed = aspd[:, cells(p)]
        right = rolled(jnp.where(lane == 0, right_lane, face(p, v, 1)), LANES - 1)
        return jnp.maximum(speed, 0.0) * face(p, v, 0) + jnp.minimum(speed, 0.0) * right

    def advance(p, v, flux_here, flux_left, first_stage, factor):
        before = rolled(jnp.where(lane == LANES - 1, flux_left, flux_here), 1)
        rate = rc[p, var_rows(v), :] + flux_here - before
        here = cur[p, v, own, :]
        start = jnp.where(first_stage, here, base[p, var_rows(v), :])
        base[p, var_rows(v), :] = start
        out_rate[v, :, cells(p)] = rate
        new = 0.5 * (start + here) - factor * (dt[:, cells(p)] * rate)
        cur[p, v, own, :] = new
        return new

    def balance(n, _):
        odd = lax.rem(n, 2)
        first_stage = odd == 0
        factor = jnp.where(first_stage, 1.0, 0.5).astype(F32)
        earlier = jnp.where(first_stage, 0.5, 1.0).astype(F32)
        end = TILES - 1

        for p in range(1, end):
            slopes(p)
        for rows in (slice(0, ROWS), slice(end * ROWS, TILES * ROWS)):
            shi[rows, :] = jnp.zeros((ROWS, WIDE), BF16)
            slo[rows, :] = jnp.zeros((ROWS, WIDE), BF16)
        for v in range(NV):
            early_box[:, var_lanes(v)] = gathered(gout, fout, v)
        fix_edges(n, earlier, False)
        for v in range(NV):
            shift(0, v, halo[0, v], cur[0, v, own, :])
            shift(TILES, v, cur[end, v, own, :], halo[1, v])
        slopes(0)
        slopes(end)
        for v in range(NV):
            picked = jnp.dot(gend[...], ends[:, var_lanes(v)], preferred_element_type=F32)
            outbox[n, :, var_lanes(v)] = (
                early_box[:, var_lanes(v)] + picked * fout[0] + rolled(picked, HALF) * fout[1]
            )
        for k in FAR_FIRST:
            box_copy(n, k).start()

        @pl.when(n == 0)
        def _():
            for k in FAR_FIRST:
                label_copy(k).start()

        late_rows(n)
        for side in range(2):
            circ_copy(n, side, 1).start()

        @pl.when(n == 0)
        def _():
            receive_constants()

        for v in range(NV):
            high, low = split(gathered(gloc, floc, v))
            c_loc[:SMALL, var_lanes(v)] = high
            c_loc[SMALL:, var_lanes(v)] = low
        for v in range(NV):
            scatter(a_loc, c_loc, v, range(TILES))

        for side in range(2):
            for late in range(2):
                circ_copy(n, side, late).wait()

        @pl.when(c > 0)
        def _():
            unpack(n, 1)

        @pl.when(c < N_CIRC - 1)
        def _():
            unpack(n, 0)

        @pl.when(c == 0)
        def _():
            permute(n, 1)

        @pl.when(c == N_CIRC - 1)
        def _():
            permute(n, 0)

        for p in range(TILES):
            circ_rates(p, 0)

        for k in range(len(NEIGHBOURS)):
            box_copy(n, k).wait()

        @pl.when(n == 0)
        def _():
            receive_labels()

        for v in range(NV):
            high, low = split(inbox[n, :, var_lanes(v)])
            c_arr[:slots, var_lanes(v)] = high
            c_arr[slots:, var_lanes(v)] = low
        for v in range(NV):
            scatter(a_edge, c_arr, v, (0, 1, end - 1, end))

        for v in range(NV):
            vr = var_rows(v)
            right_face = face(0, v, 1)
            flux_first = flux(0, v, face(1, v, 1))
            left_face = face(end, v, 0)
            flux_before = flux(end - 1, v, face(end, v, 1))
            flux_last = jnp.where(lane == LANES - 1, 0.0, flux(end, v, 0.0))
            edges[0, vr, :] = right_face
            edges[1, vr, :] = left_face
            f_keep[0, vr, :] = flux_first
            f_keep[1, vr, :] = flux_before
            new_first = advance(0, v, flux_first, 0.0, first_stage, factor)
            new_last = advance(end, v, flux_last, flux_before, first_stage, factor)
            ax_send[n + 1, 0, v] = jnp.where(
                lane < HALF, new_first, rolled(right_face, LANES - 1)
            )
            ax_send[n + 1, 1, v] = jnp.where(lane >= HALF, new_last, rolled(left_face, 1))
        for side in range(2):
            axial_copy(n + 1, side).start()

        for v in range(NV):
            scatter(a_arr, c_arr, v, range(2, end - 1))
        for v in range(NV):
            before = f_keep[0, var_rows(v), :]
            tile = cur[0, v, own, :]
            for p in range(1, end):
                here = flux(p, v, face(p + 1, v, 1)) if p < end - 1 else f_keep[1, var_rows(v), :]
                new = advance(p, v, here, before, first_stage, factor)
                pack_rows(n + 1, p, v, new)
                shift(p, v, tile, new)
                before, tile = here, new
            shift(end, v, tile, cur[end, v, own, :])

        @pl.when(n < BALANCES - 1)
        def _():
            for side in range(2):
                circ_copy(n + 1, side, 0).start()

        return 0

    lax.fori_loop(0, BALANCES, balance, 0)
    fix_edges(BALANCES, jnp.float32(0.5), True)

    for p in range(TILES):
        for v in range(NV):
            out_u[v, :, cells(p)] = cur[p, v, own, :]


def local(
    flow_state, circ_speed, axial_speed, time_step, lsq_weights,
    partner, merge_owner, merge_source, merge_host, merge_frac,
):
    columns = TILES * LANES
    slots = len(NEIGHBOURS) * CAP
    vmem = pl.BlockSpec(memory_space=pltpu.VMEM)
    hbm = pl.BlockSpec(memory_space=pltpu.HBM)
    dma = pltpu.SemaphoreType.DMA
    shape = jax.ShapeDtypeStruct((NV, ROWS, columns), F32)
    scratch = [
        pltpu.VMEM((NV, ROWS, columns), F32),
        pltpu.VMEM((ROWS, columns), F32),
        pltpu.VMEM((ROWS, columns), F32),
        pltpu.VMEM((ROWS, columns), F32),
        pltpu.VMEM((BLOCKS, HALF, 3 * HALF), F32),
        pltpu.VMEM((1, columns), jnp.int32),
        pltpu.VMEM((TILES, LANES), jnp.int32),
        pltpu.VMEM((1, SMALL), jnp.int32),
        pltpu.VMEM((1, SMALL), jnp.int32),
        pltpu.VMEM((1, SMALL), jnp.int32),
        pltpu.VMEM((HALF, SMALL), F32),
        dma((11,)),
        pltpu.VMEM((TILES, NV, 2 * ROWS, LANES), F32),
        pltpu.VMEM((TILES, STACK, LANES), F32),
        pltpu.VMEM((TILES, 2 * ROWS, LANES), F32),
        pltpu.VMEM((TILES + 1, 2 * STACK, LANES), BF16),
        pltpu.VMEM((TILES, 2 * LANES, 2 * LANES), BF16),
        pltpu.VMEM((TILES, STACK, LANES), F32),
        pltpu.VMEM((TILES * ROWS, WIDE), BF16),
        pltpu.VMEM((TILES * ROWS, WIDE), BF16),
        pltpu.VMEM((TILES, STACK, LANES), F32),
        pltpu.VMEM((slots, TILES * ROWS), BF16),
        pltpu.VMEM((slots, 4 * ROWS), BF16),
        pltpu.VMEM((4 * ROWS, WIDE), BF16),
        pltpu.VMEM((SMALL, TILES * ROWS), BF16),
        pltpu.VMEM((2, slots, LANES), F32),
        pltpu.VMEM((2, SMALL, LANES), F32),
        pltpu.VMEM((TILES * ROWS, 2 * SMALL), BF16),
        pltpu.VMEM(((TILES - 4) * ROWS, 2 * slots), BF16),
        pltpu.VMEM((4 * ROWS, 2 * slots), BF16),
        pltpu.VMEM((2 * SMALL, WIDE), BF16),
        pltpu.VMEM((2 * slots, WIDE), BF16),
        pltpu.VMEM((2, STACK, LANES), F32),
        pltpu.VMEM((4, ROWS, LANES), F32),
        pltpu.VMEM((2, STACK, LANES), F32),
        pltpu.VMEM((2, NV, ROWS, LANES), F32),
        pltpu.VMEM((2, TILES, LANES), jnp.int32),
        pltpu.VMEM((BALANCES + 1, 2, NV, ROWS, LANES), F32),
        pltpu.VMEM((BALANCES + 1, 2, NV, ROWS, LANES), F32),
        pltpu.VMEM((3, ROWS, LANES), F32),
        pltpu.VMEM((TILES, LANES), F32),
        pltpu.VMEM((TILES, LANES), F32),
        pltpu.VMEM((BALANCES + 1, 2, ROW_TILES, 8, LANES), F32),
        pltpu.VMEM((BALANCES, 2, ROW_TILES, 8, LANES), F32),
        pltpu.VMEM((slots, LANES), F32),
        pltpu.VMEM((slots, LANES), F32),
        pltpu.VMEM((BALANCES, slots, WIDE), F32),
        pltpu.VMEM((BALANCES, slots, WIDE), F32),
        pltpu.VMEM((slots, WIDE), F32),
        dma((BALANCES + 1, 2)), dma((BALANCES + 1, 2)),
        dma((3,)), dma((3,)),
        dma((1,)), dma((1,)),
        dma((BALANCES, 2, 2)), dma((BALANCES, 2, 2)),
        dma((len(NEIGHBOURS),)), dma((len(NEIGHBOURS),)),
        dma((BALANCES, len(NEIGHBOURS))), dma((BALANCES, len(NEIGHBOURS))),
    ]
    return pl.pallas_call(
        kernel,
        out_shape=(pltpu.VMEM((NV, ROWS, columns), F32),) * 2,
        in_specs=[hbm] * 11,
        out_specs=(vmem, vmem),
        scratch_shapes=scratch,
        compiler_params=pltpu.CompilerParams(
            collective_id=0, has_side_effects=True, vmem_limit_bytes=56 * 1024 * 1024
        ),
    )(
        flow_state, circ_speed, axial_speed, time_step, lsq_weights,
        partner.reshape(1, columns), partner.reshape(TILES, LANES),
        merge_owner.reshape(1, SMALL), merge_source.reshape(1, SMALL),
        merge_host.reshape(1, SMALL), merge_frac.T,
    )


def solution(mesh):
    in_specs = (
        P(None, "circ", "axial"),
        P("circ", "axial"),
        P("circ", "axial"),
        P("circ", "axial"),
        P("axial", None, None),
        P("axial"),
        P(("circ", "axial"), None),
        P(("circ", "axial")),
        P(("circ", "axial")),
        P(("circ", "axial"), None),
    )
    out_specs = (P(None, "circ", "axial"), P(None, "circ", "axial"))
    return jax.shard_map(local, mesh=mesh, in_specs=in_specs, out_specs=out_specs, check_vma=False)
```

```python
import jax
import jax.numpy as jnp
from jax import lax
from jax.experimental import pallas as pl
from jax.experimental.pallas import tpu as pltpu
from jax.sharding import PartitionSpec as P

STEPS = 2
BALANCES = 2 * STEPS
CAP = 8
NV = 5
ROWS = 16
LANES = 128
TILES = 16
HALF = 64
SMALL = 128
BLOCKS = 32
N_CIRC = 16
N_AXIAL = 8
STACK = NV * ROWS
WIDE = NV * LANES
BOX = 3 * LANES
ROW_TILES = 20
EARLY = 17
FIRST = 8
MESH = pl.DeviceIdType.MESH
F32 = jnp.float32
BF16 = jnp.bfloat16
NEIGHBOURS = [(dc, da) for dc in (-1, 0, 1) for da in (-1, 0, 1) if (dc, da) != (0, 0)]
DIRECT = [(-1, 0), (1, 0), (0, -1), (0, 1)]
FAR_FIRST = (0, 2, 5, 7, 1, 6, 3, 4)


def split(x):
    high = x.astype(BF16)
    return high, (x - high.astype(F32)).astype(BF16)


def lanes_of(shape):
    return lax.broadcasted_iota(jnp.int32, shape, len(shape) - 1)


def rolled(x, steps):
    return pltpu.roll(x, steps, x.ndim - 1)


def var_rows(v):
    return slice(v * ROWS, (v + 1) * ROWS)


def var_lanes(v):
    return slice(v * LANES, (v + 1) * LANES)


def cells(p):
    return slice(p * LANES, (p + 1) * LANES)


def kernel(
    flow_hbm, cspd_hbm, aspd_hbm, dt_hbm, w_hbm, prow_hbm, ptile_hbm, owner_hbm, source_hbm,
    host_hbm, frac_hbm,
    out_u, out_rate,
    flow, cspd, aspd, dt, w, partner_row, partner_tile, owner, source, host, frac, load_sem,
    cur, base, cs, xs, wts, s32, shi, slo, rc, gout, gend, ends, gloc, fout, floc, a_loc, a_arr, a_edge, c_loc, c_arr,
    edges, consts, f_keep, halo, perm, permuted,
    ax_send, ax_recv, ini_recv, row_send, row_recv, ci_send, ci_recv, lab_send, lab_recv, outbox, inbox, box_half, early_box,
    ax_ss, ax_rs, ini_ss, ini_rs, row_ss, row_rs, ci_ss, ci_rs, lab_ss, lab_rs, box_ss, box_rs,
):
    c = lax.axis_index("circ")
    a = lax.axis_index("axial")

    def peer(dc, da):
        return (lax.rem(c + dc + N_CIRC, N_CIRC), lax.rem(a + da + N_AXIAL, N_AXIAL))

    def remote(src, dst, send, recv, dc, da):
        return pltpu.make_async_remote_copy(
            src_ref=src, dst_ref=dst, send_sem=send, recv_sem=recv,
            device_id=peer(dc, da), device_id_type=MESH,
        )

    def axial_copy(n, side):
        return remote(
            ax_send.at[n, side], ax_recv.at[n, side], ax_ss.at[n, side], ax_rs.at[n, side],
            0, 2 * side - 1,
        )

    head, tail = pl.ds(0, LANES), pl.ds((TILES - 1) * LANES, LANES)

    def first_axial_copy(side):
        return remote(
            flow_hbm.at[:, :, tail if side else head], ax_recv.at[0, side],
            ax_ss.at[0, side], ax_rs.at[0, side], 0, 2 * side - 1,
        )

    def init_copy(k):
        source_of = (dt_hbm.at[:, head], dt_hbm.at[:, tail], aspd_hbm.at[:, tail])
        return remote(
            source_of[k], ini_recv.at[k], ini_ss.at[k], ini_rs.at[k], 0, 1 if k else -1
        )

    def circ_copy(n, side, late):
        part = pl.ds(EARLY, ROW_TILES - EARLY) if late else pl.ds(0, EARLY)
        return remote(
            ci_send.at[n, side, part], ci_recv.at[n, side, part],
            ci_ss.at[n, side, late], ci_rs.at[n, side, late], 2 * side - 1, 0,
        )

    def row_copy():
        return remote(row_send, row_recv, row_ss.at[0], row_rs.at[0], 1, 0)

    def label_copy(k):
        dc, da = NEIGHBOURS[k]
        rows = pl.ds(k * CAP, CAP)
        return remote(lab_send.at[rows], lab_recv.at[rows], lab_ss.at[k], lab_rs.at[k], dc, da)

    def box_copy(n, k):
        dc, da = NEIGHBOURS[k]
        rows = pl.ds(k * CAP, CAP)
        return remote(
            outbox.at[n, rows], inbox.at[n, rows], box_ss.at[n, k], box_rs.at[n, k], dc, da
        )

    own = slice(FIRST, FIRST + ROWS)
    lane = lanes_of((ROWS, LANES))
    box_lane = lanes_of((len(NEIGHBOURS) * CAP, LANES))

    loads = [
        pltpu.make_async_copy(src, dst, load_sem.at[i])
        for i, (src, dst) in enumerate(
            (
                (owner_hbm, owner), (source_hbm, source), (host_hbm, host), (flow_hbm, flow),
                (dt_hbm, dt), (aspd_hbm, aspd), (cspd_hbm, cspd), (frac_hbm, frac),
                (prow_hbm, partner_row), (ptile_hbm, partner_tile), (w_hbm, w),
            )
        )
    ]
    for load in loads:
        load.start()

    barrier = pltpu.get_barrier_semaphore()
    for dc, da in DIRECT:
        pl.semaphore_signal(barrier, inc=1, device_id=peer(dc, da), device_id_type=MESH)

    def pair_place(p, v):
        slot = p - 1 if 0 < p < TILES - 1 else TILES - 2 + p // (TILES - 1)
        if v < NV - 1:
            return (slot if slot < TILES - 2 else slot + 3), 2 * v
        group = slot // 4
        return (TILES - 2 + group if group < 3 else ROW_TILES - 1), 2 * (slot % 4)

    def pack_rows(n, p, v, tile):
        where, row = pair_place(p, v)
        ci_send[n, 0, where, row:row + 2, :] = tile[0:2]
        ci_send[n, 1, where, row:row + 2, :] = tile[ROWS - 2:ROWS]

    def shift(q, v, left_tile, right_tile):
        moved = rolled(jnp.where(lane >= HALF, left_tile, right_tile), HALF)
        high, low = split(moved)
        xs[q, var_rows(v), :] = high
        xs[q, STACK + v * ROWS:STACK + (v + 1) * ROWS, :] = low

    for load in loads[:3]:
        load.wait()
    square = (SMALL, SMALL)
    t_row = owner[...]
    s_row = source[...]
    h_row = host[...]

    def as_columns(row):
        return jnp.broadcast_to(row.astype(F32), square).T.astype(jnp.int32)

    t_col, s_col, h_col = as_columns(t_row), as_columns(s_row), as_columns(h_row)
    myself = c * N_AXIAL + a
    first = lax.broadcasted_iota(jnp.int32, square, 0)
    second = lax.broadcasted_iota(jnp.int32, square, 1)
    shares = jnp.where((jnp.broadcast_to(t_row, square) == t_col) & (first < second), 1.0, 0.0)
    rank = jnp.sum(shares, axis=0, keepdims=True).astype(jnp.int32)
    circ_off = ((t_row >> 3) - c + 1 + N_CIRC) & (N_CIRC - 1)
    number = circ_off * 3 + (t_row & (N_AXIAL - 1)) - a + 1
    number = jnp.where(number > 4, number - 1, number)
    place = jnp.where(t_row == myself, -1, number * CAP + rank)
    slots = len(NEIGHBOURS) * CAP
    chosen = jnp.where(
        jnp.broadcast_to(place, (slots, SMALL))
        == lax.broadcasted_iota(jnp.int32, (slots, SMALL), 0),
        1.0, 0.0,
    )

    def row_index(s):
        return ((s & (BLOCKS - 1)) >> 1) * ROWS + (s >> 5)

    host_index = row_index(h_row)
    marks = 2 * (host_index + 1) + (h_row & 1)
    labels = jnp.sum(chosen * marks.astype(F32), axis=1, keepdims=True)
    lab_send[...] = jnp.broadcast_to(labels, (slots, LANES))

    edges[...] = jnp.zeros_like(edges)
    consts[...] = jnp.zeros_like(consts)
    pl.semaphore_wait(barrier, len(DIRECT))
    for side in range(2):
        first_axial_copy(side).start()
    for k in range(3):
        init_copy(k).start()
    for load in loads[3:7]:
        load.wait()
    for p in range(TILES):
        columns = slice(p * LANES, (p + 1) * LANES)
        speed = cspd[:, columns]
        cs[p, own, :] = speed
        row_send[p:p + 1, :] = speed[ROWS - 1:ROWS]
    row_copy().start()
    for v in range(NV):
        before = None
        for p in range(TILES):
            tile = flow[v, :, p * LANES:(p + 1) * LANES]
            cur[p, v, own, :] = tile
            pack_rows(0, p, v, tile)
            if p > 0:
                shift(p, v, before, tile)
            before = tile
    for side in range(2):
        circ_copy(0, side, 0).start()
    for load in loads[7:10]:
        load.wait()
    frac_twice = jnp.concatenate([frac[...], frac[...]], axis=0).T
    placed = jnp.where((second >> 6) == (h_col & 1), frac_twice, 0.0)
    same_half = (s_col & 1) == (h_col & 1)
    straight = jnp.where(same_half, placed, 0.0)
    crossed = jnp.where(same_half, 0.0, placed)
    is_local = t_col == myself
    floc[0] = jnp.where(is_local, straight, 0.0)
    floc[1] = jnp.where(is_local, crossed, 0.0)
    in_source = (second >> 6) == (s_col & 1)
    fout[0] = jnp.dot(
        chosen, jnp.where(in_source, frac_twice, 0.0), precision=lax.Precision.HIGHEST
    )
    fout[1] = jnp.dot(
        chosen, jnp.where(in_source, 0.0, frac_twice), precision=lax.Precision.HIGHEST
    )
    s_index = row_index(s_col)
    pick = jnp.concatenate(
        [
            jnp.where(s_index == second, 1.0, 0.0),
            jnp.where(s_index == second + LANES, 1.0, 0.0),
        ],
        axis=1,
    ).astype(BF16)
    gloc[...] = pick
    picked_out = jnp.dot(chosen.astype(BF16), pick, preferred_element_type=F32)
    gout[...] = picked_out.astype(BF16)
    picked_end = jnp.concatenate([picked_out[:, :ROWS], picked_out[:, -ROWS:]], axis=1)
    gend[...] = jnp.concatenate([picked_end, picked_end], axis=1).astype(BF16)
    tall = (TILES * ROWS, SMALL)
    tall_rows = lax.broadcasted_iota(jnp.int32, tall, 0)
    wanted = jnp.where(t_row == myself, host_index, -1)
    land = jnp.where(jnp.broadcast_to(wanted, tall) == tall_rows, 1.0, 0.0).astype(BF16)
    a_loc[...] = jnp.concatenate([land, land], axis=1)

    @pl.when(c > 0)
    def _():
        perm[0] = partner_tile[...] >> 7
        perm[1] = partner_tile[...] & (LANES - 1)

    @pl.when(c == 0)
    def _():
        columns = TILES * LANES
        target = partner_row[...]
        upper = jnp.where(
            jnp.broadcast_to(target >> 7, (TILES, columns))
            == lax.broadcasted_iota(jnp.int32, (TILES, columns), 0),
            1.0, 0.0,
        ).astype(BF16)
        tall_lanes = (LANES, columns)
        here = jnp.broadcast_to(target & (LANES - 1), tall_lanes) == lax.broadcasted_iota(
            jnp.int32, tall_lanes, 0
        )
        position = lanes_of(tall_lanes)
        for part, value in enumerate((position >> 7, position & (LANES - 1))):
            lower = jnp.where(here, value.astype(F32), 0.0).astype(BF16)
            perm[part] = lax.dot_general(
                upper, lower, (((1,), (1,)), ((), ())), preferred_element_type=F32
            ).astype(jnp.int32)

    def weigh(p, _):
        gap = jnp.zeros((HALF, HALF), F32)
        both = jnp.concatenate(
            [
                jnp.concatenate([w[2 * p], gap], axis=1),
                jnp.concatenate([gap, w[2 * p + 1]], axis=1),
            ],
            axis=0,
        )
        high, low = split(both.T)
        wts[p, :, 0:LANES] = high
        wts[p, :, LANES:] = low
        return 0

    loads[10].wait()
    lax.fori_loop(0, TILES, weigh, 0)

    def receive_constants():
        for k in range(3):
            init_copy(k).wait()
        consts[0] = jnp.where(a > 0, ini_recv[1], 0.0)
        consts[1] = jnp.where(a < N_AXIAL - 1, ini_recv[0], 0.0)
        consts[2] = jnp.where((a > 0) & (lane == 0), rolled(ini_recv[2], 1), 0.0)
        consts[3] = jnp.where(lane == LANES - 1, aspd[:, (TILES - 1) * LANES:], 0.0)
        row_copy().wait()
        for half in range(2):
            some = slice(half * 8, half * 8 + 8)
            below_row = row_recv[some, :]
            mixed = jnp.zeros_like(below_row)
            for q in range(TILES):
                found = jnp.take_along_axis(
                    jnp.broadcast_to(row_recv[q:q + 1, :], below_row.shape), perm[1, some, :], axis=1
                )
                mixed = jnp.where(perm[0, some, :] == q, found, mixed)
            below_row = jnp.where(c == 0, mixed, below_row)
            for k in range(8):
                cs[half * 8 + k, FIRST - 1:FIRST, :] = below_row[k:k + 1]

    def receive_labels():
        for k in range(len(NEIGHBOURS)):
            label_copy(k).wait()
        arrived = lab_recv[...].astype(jnp.int32)
        box_half[...] = jnp.where((lanes_of(arrived.shape) >> 6) == (arrived & 1), 1.0, 0.0)
        places = ((arrived >> 1) - 1).astype(F32)
        label_row = jnp.concatenate([places, places], axis=0).T.astype(jnp.int32)
        land_here = jnp.where(
            jnp.concatenate([label_row, label_row], axis=0) == tall_rows, 1.0, 0.0
        ).astype(BF16)
        a_arr[...] = land_here[2 * ROWS:-2 * ROWS]
        a_edge[0:2 * ROWS, :] = land_here[0:2 * ROWS]
        a_edge[2 * ROWS:, :] = land_here[-2 * ROWS:]

    def fix_edges(n, factor, also_rate):
        for side in range(2):
            axial_copy(n, side).wait()
        left_speed, right_speed = consts[2], consts[3]
        last = (TILES - 1) * LANES
        for v in range(NV):
            vr = var_rows(v)
            from_left = jnp.where(a > 0, ax_recv[n, 1, v], 0.0)
            from_right = jnp.where(a < N_AXIAL - 1, ax_recv[n, 0, v], 0.0)
            left_flux = jnp.maximum(left_speed, 0.0) * from_left + jnp.minimum(
                left_speed, 0.0
            ) * edges[0, vr, :]
            right_flux = jnp.maximum(right_speed, 0.0) * edges[1, vr, :] + jnp.minimum(
                right_speed, 0.0
            ) * from_right
            cur[0, v, own, :] = cur[0, v, own, :] + factor * dt[:, 0:LANES] * left_flux
            cur[TILES - 1, v, own, :] = (
                cur[TILES - 1, v, own, :] - factor * dt[:, last:] * right_flux
            )
            if also_rate:
                out_rate[v, :, 0:LANES] = out_rate[v, :, 0:LANES] - left_flux
                out_rate[v, :, last:] = out_rate[v, :, last:] + right_flux
            else:
                halo[0, v] = from_left - factor * consts[0] * rolled(left_flux, LANES - 1)
                halo[1, v] = from_right + factor * consts[1] * rolled(right_flux, 1)

    def slopes(p):
        left = jnp.concatenate([xs[p], xs[p + 1]], axis=1)
        full = jnp.dot(left, wts[p], preferred_element_type=F32)
        total = full[:STACK, :LANES] + full[:STACK, LANES:] + full[STACK:, :LANES]
        s32[p] = total
        high, low = split(total)
        rows = slice(p * ROWS, (p + 1) * ROWS)
        for v in range(NV):
            shi[rows, var_lanes(v)] = high[var_rows(v)]
            slo[rows, var_lanes(v)] = low[var_rows(v)]
            if p in (0, TILES - 1):
                start = ROWS * (p // (TILES - 1))
                ends[start:start + ROWS, var_lanes(v)] = high[var_rows(v)]
                ends[2 * ROWS + start:3 * ROWS + start, var_lanes(v)] = low[var_rows(v)]

    def gathered(picks, factors, v):
        vl = var_lanes(v)
        picked = jnp.dot(picks[...], shi[:, vl], preferred_element_type=F32) + jnp.dot(
            picks[...], slo[:, vl], preferred_element_type=F32
        )
        return picked * factors[0] + rolled(picked, HALF) * factors[1]

    def scatter(matrix, values, v, tiles):
        added = jnp.dot(matrix[...], values[:, var_lanes(v)], preferred_element_type=F32)
        for i, p in enumerate(tiles):
            s32[p, var_rows(v), :] = s32[p, var_rows(v), :] + added[i * ROWS:(i + 1) * ROWS]

    def late_rows(n):
        for v in range(NV):
            for p in (0, TILES - 1):
                pack_rows(n, p, v, cur[p, v, own, :])

    def is_late(p, v):
        return pair_place(p, v)[0] >= EARLY

    def unpack(n, side, late):
        start = FIRST - 2 if side else FIRST + ROWS
        for p in range(TILES):
            for v in range(NV):
                if is_late(p, v) == late:
                    where, row = pair_place(p, v)
                    cur[p, v, start:start + 2, :] = ci_recv[n, side, where, row:row + 2, :]

    def permute(n, side, late):
        start = FIRST - 2 if side else FIRST + ROWS
        rows = lax.broadcasted_iota(jnp.int32, (8, LANES), 0)

        def one(p):
            tile = jnp.broadcast_to(perm[0, pl.ds(p, 1), :], (8, LANES))
            column = jnp.broadcast_to(perm[1, pl.ds(p, 1), :], (8, LANES))
            slot = jnp.where(
                tile == 0, TILES - 2, jnp.where(tile == TILES - 1, TILES - 1, tile - 1)
            )
            offset = slot - (rows >> 1)
            if late:
                total, last = permuted[0, p], permuted[1, p]
            else:
                total = last = jnp.zeros((8, LANES), F32)
            for q in range(TILES):
                if is_late(q, 0) == late:
                    where, _ = pair_place(q, 0)
                    found = jnp.take_along_axis(ci_recv[n, side, where], column, axis=1)
                    total = jnp.where(tile == q, found, total)
            for g in range(4):
                if (g == 3) == late:
                    where = TILES - 2 + g if g < 3 else ROW_TILES - 1
                    found = jnp.take_along_axis(ci_recv[n, side, where], column, axis=1)
                    last = jnp.where(offset == 4 * g, found, last)
            if not late:
                permuted[0, p], permuted[1, p] = total, last
                return
            last = last + pltpu.roll(last, 4, 0)
            last = last + pltpu.roll(last, 2, 0)
            for v in range(NV - 1):
                cur[p, v, start:start + 2, :] = total[2 * v:2 * v + 2]
            cur[p, NV - 1, start:start + 2, :] = last[0:2]

        def four(i, _):
            for k in range(4):
                one(4 * i + k)
            return 0

        lax.fori_loop(0, TILES // 4, four, 0)

    def halo_rows(n, late):
        for side in range(2):
            circ_copy(n, side, int(late)).wait()

        @pl.when(c > 0)
        def _():
            unpack(n, 1, late)

        @pl.when(c < N_CIRC - 1)
        def _():
            unpack(n, 0, late)

        @pl.when(c == 0)
        def _():
            permute(n, 1, late)

        @pl.when(c == N_CIRC - 1)
        def _():
            permute(n, 0, late)

    def circ_rates(p, _):
        above = cs[p, own, :]
        below = cs[p, FIRST - 1:FIRST + ROWS - 1, :]
        above_pos, above_neg = jnp.maximum(above, 0.0), jnp.minimum(above, 0.0)
        below_pos, below_neg = jnp.maximum(below, 0.0), jnp.minimum(below, 0.0)
        for v in range(NV):
            at = [cur[p, v, FIRST + k:FIRST + k + ROWS, :] for k in (-2, -1, 0, 1, 2)]
            slope_below = 0.25 * (at[2] - at[0])
            slope_here = 0.25 * (at[3] - at[1])
            slope_above = 0.25 * (at[4] - at[2])
            upper = above_pos * (at[2] + slope_here) + above_neg * (at[3] - slope_above)
            lower = below_pos * (at[1] + slope_below) + below_neg * (at[2] - slope_here)
            rc[p, var_rows(v), :] = upper - lower
        return 0

    def face(p, v, kind):
        half_slope = 0.5 * s32[p, var_rows(v), :]
        here = cur[p, v, own, :]
        return here + half_slope if kind == 0 else here - half_slope

    def flux(p, v, right_lane):
        speed = aspd[:, cells(p)]
        right = rolled(jnp.where(lane == 0, right_lane, face(p, v, 1)), LANES - 1)
        return jnp.maximum(speed, 0.0) * face(p, v, 0) + jnp.minimum(speed, 0.0) * right

    def advance(p, v, flux_here, flux_left, first_stage, factor):
        before = rolled(jnp.where(lane == LANES - 1, flux_left, flux_here), 1)
        rate = rc[p, var_rows(v), :] + flux_here - before
        here = cur[p, v, own, :]
        start = jnp.where(first_stage, here, base[p, var_rows(v), :])
        base[p, var_rows(v), :] = start
        out_rate[v, :, cells(p)] = rate
        new = 0.5 * (start + here) - factor * (dt[:, cells(p)] * rate)
        cur[p, v, own, :] = new
        return new

    def balance(n, _):
        odd = lax.rem(n, 2)
        first_stage = odd == 0
        factor = jnp.where(first_stage, 1.0, 0.5).astype(F32)
        earlier = jnp.where(first_stage, 0.5, 1.0).astype(F32)
        end = TILES - 1

        for p in range(1, end):
            slopes(p)
        for rows in (slice(0, ROWS), slice(end * ROWS, TILES * ROWS)):
            shi[rows, :] = jnp.zeros((ROWS, WIDE), BF16)
            slo[rows, :] = jnp.zeros((ROWS, WIDE), BF16)
        for v in range(NV):
            early_box[:, var_lanes(v)] = gathered(gout, fout, v)
        fix_edges(n, earlier, False)
        late_rows(n)
        for side in range(2):
            circ_copy(n, side, 1).start()
        for v in range(NV):
            shift(0, v, halo[0, v], cur[0, v, own, :])
            shift(TILES, v, cur[end, v, own, :], halo[1, v])
        slopes(0)
        slopes(end)
        for v in range(NV):
            picked = jnp.dot(gend[...], ends[:, var_lanes(v)], preferred_element_type=F32)
            sent = early_box[:, var_lanes(v)] + picked * fout[0] + rolled(picked, HALF) * fout[1]
            columns = slice(v // 2 * LANES, v // 2 * LANES + LANES)
            if v % 2:
                outbox[n, :, columns] = jnp.where(box_lane < HALF, previous, sent)
            elif v == NV - 1:
                outbox[n, :, columns] = sent
            previous = sent
        for k in FAR_FIRST:
            box_copy(n, k).start()

        @pl.when(n == 0)
        def _():
            for k in FAR_FIRST:
                label_copy(k).start()

        @pl.when(n == 0)
        def _():
            receive_constants()

        for v in range(NV):
            high, low = split(gathered(gloc, floc, v))
            c_loc[:SMALL, var_lanes(v)] = high
            c_loc[SMALL:, var_lanes(v)] = low
        for v in range(NV):
            scatter(a_loc, c_loc, v, range(TILES))

        halo_rows(n, False)
        at_seam = (c == 0) | (c == N_CIRC - 1)
        whole = [p for p in range(TILES) if not is_late(p, NV - 1)]

        @pl.when(jnp.logical_not(at_seam))
        def _():
            for p in whole:
                circ_rates(p, 0)

        halo_rows(n, True)

        @pl.when(at_seam)
        def _():
            for p in whole:
                circ_rates(p, 0)

        for p in range(TILES):
            if p not in whole:
                circ_rates(p, 0)

        for k in range(len(NEIGHBOURS)):
            box_copy(n, k).wait()

        @pl.when(n == 0)
        def _():
            receive_labels()

        for v in range(NV):
            columns = slice(v // 2 * LANES, v // 2 * LANES + LANES)
            packed = inbox[n, :, columns]
            if v == NV - 1:
                both = packed
            else:
                both = jnp.where((box_lane < HALF) == (v % 2 == 0), packed, rolled(packed, HALF))
            high, low = split(both * box_half[...])
            c_arr[:slots, var_lanes(v)] = high
            c_arr[slots:, var_lanes(v)] = low
        for v in range(NV):
            scatter(a_edge, c_arr, v, (0, 1, end - 1, end))

        for v in range(NV):
            vr = var_rows(v)
            right_face = face(0, v, 1)
            flux_first = flux(0, v, face(1, v, 1))
            left_face = face(end, v, 0)
            flux_before = flux(end - 1, v, face(end, v, 1))
            flux_last = jnp.where(lane == LANES - 1, 0.0, flux(end, v, 0.0))
            edges[0, vr, :] = right_face
            edges[1, vr, :] = left_face
            f_keep[0, vr, :] = flux_first
            f_keep[1, vr, :] = flux_before
            new_first = advance(0, v, flux_first, 0.0, first_stage, factor)
            new_last = advance(end, v, flux_last, flux_before, first_stage, factor)
            ax_send[n + 1, 0, v] = jnp.where(
                lane < HALF, new_first, rolled(right_face, LANES - 1)
            )
            ax_send[n + 1, 1, v] = jnp.where(lane >= HALF, new_last, rolled(left_face, 1))
        for side in range(2):
            axial_copy(n + 1, side).start()

        for v in range(NV):
            scatter(a_arr, c_arr, v, range(2, end - 1))
        for v in range(NV):
            before = f_keep[0, var_rows(v), :]
            tile = cur[0, v, own, :]
            for p in range(1, end):
                here = flux(p, v, face(p + 1, v, 1)) if p < end - 1 else f_keep[1, var_rows(v), :]
                new = advance(p, v, here, before, first_stage, factor)
                pack_rows(n + 1, p, v, new)
                shift(p, v, tile, new)
                before, tile = here, new
            shift(end, v, tile, cur[end, v, own, :])

        @pl.when(n < BALANCES - 1)
        def _():
            for side in range(2):
                circ_copy(n + 1, side, 0).start()

        return 0

    lax.fori_loop(0, BALANCES, balance, 0)
    fix_edges(BALANCES, jnp.float32(0.5), True)

    for p in range(TILES):
        for v in range(NV):
            out_u[v, :, cells(p)] = cur[p, v, own, :]


def local(
    flow_state, circ_speed, axial_speed, time_step, lsq_weights,
    partner, merge_owner, merge_source, merge_host, merge_frac,
):
    columns = TILES * LANES
    slots = len(NEIGHBOURS) * CAP
    vmem = pl.BlockSpec(memory_space=pltpu.VMEM)
    hbm = pl.BlockSpec(memory_space=pltpu.HBM)
    dma = pltpu.SemaphoreType.DMA
    shape = jax.ShapeDtypeStruct((NV, ROWS, columns), F32)
    scratch = [
        pltpu.VMEM((NV, ROWS, columns), F32),
        pltpu.VMEM((ROWS, columns), F32),
        pltpu.VMEM((ROWS, columns), F32),
        pltpu.VMEM((ROWS, columns), F32),
        pltpu.VMEM((BLOCKS, HALF, 3 * HALF), F32),
        pltpu.VMEM((1, columns), jnp.int32),
        pltpu.VMEM((TILES, LANES), jnp.int32),
        pltpu.VMEM((1, SMALL), jnp.int32),
        pltpu.VMEM((1, SMALL), jnp.int32),
        pltpu.VMEM((1, SMALL), jnp.int32),
        pltpu.VMEM((HALF, SMALL), F32),
        dma((11,)),
        pltpu.VMEM((TILES, NV, 2 * ROWS, LANES), F32),
        pltpu.VMEM((TILES, STACK, LANES), F32),
        pltpu.VMEM((TILES, 2 * ROWS, LANES), F32),
        pltpu.VMEM((TILES + 1, 2 * STACK, LANES), BF16),
        pltpu.VMEM((TILES, 2 * LANES, 2 * LANES), BF16),
        pltpu.VMEM((TILES, STACK, LANES), F32),
        pltpu.VMEM((TILES * ROWS, WIDE), BF16),
        pltpu.VMEM((TILES * ROWS, WIDE), BF16),
        pltpu.VMEM((TILES, STACK, LANES), F32),
        pltpu.VMEM((slots, TILES * ROWS), BF16),
        pltpu.VMEM((slots, 4 * ROWS), BF16),
        pltpu.VMEM((4 * ROWS, WIDE), BF16),
        pltpu.VMEM((SMALL, TILES * ROWS), BF16),
        pltpu.VMEM((2, slots, LANES), F32),
        pltpu.VMEM((2, SMALL, LANES), F32),
        pltpu.VMEM((TILES * ROWS, 2 * SMALL), BF16),
        pltpu.VMEM(((TILES - 4) * ROWS, 2 * slots), BF16),
        pltpu.VMEM((4 * ROWS, 2 * slots), BF16),
        pltpu.VMEM((2 * SMALL, WIDE), BF16),
        pltpu.VMEM((2 * slots, WIDE), BF16),
        pltpu.VMEM((2, STACK, LANES), F32),
        pltpu.VMEM((4, ROWS, LANES), F32),
        pltpu.VMEM((2, STACK, LANES), F32),
        pltpu.VMEM((2, NV, ROWS, LANES), F32),
        pltpu.VMEM((2, TILES, LANES), jnp.int32),
        pltpu.VMEM((2, TILES, 8, LANES), F32),
        pltpu.VMEM((BALANCES + 1, 2, NV, ROWS, LANES), F32),
        pltpu.VMEM((BALANCES + 1, 2, NV, ROWS, LANES), F32),
        pltpu.VMEM((3, ROWS, LANES), F32),
        pltpu.VMEM((TILES, LANES), F32),
        pltpu.VMEM((TILES, LANES), F32),
        pltpu.VMEM((BALANCES + 1, 2, ROW_TILES, 8, LANES), F32),
        pltpu.VMEM((BALANCES, 2, ROW_TILES, 8, LANES), F32),
        pltpu.VMEM((slots, LANES), F32),
        pltpu.VMEM((slots, LANES), F32),
        pltpu.VMEM((BALANCES, slots, BOX), F32),
        pltpu.VMEM((BALANCES, slots, BOX), F32),
        pltpu.VMEM((slots, LANES), F32),
        pltpu.VMEM((slots, WIDE), F32),
        dma((BALANCES + 1, 2)), dma((BALANCES + 1, 2)),
        dma((3,)), dma((3,)),
        dma((1,)), dma((1,)),
        dma((BALANCES, 2, 2)), dma((BALANCES, 2, 2)),
        dma((len(NEIGHBOURS),)), dma((len(NEIGHBOURS),)),
        dma((BALANCES, len(NEIGHBOURS))), dma((BALANCES, len(NEIGHBOURS))),
    ]
    return pl.pallas_call(
        kernel,
        out_shape=(pltpu.VMEM((NV, ROWS, columns), F32),) * 2,
        in_specs=[hbm] * 11,
        out_specs=(vmem, vmem),
        scratch_shapes=scratch,
        compiler_params=pltpu.CompilerParams(
            collective_id=0, has_side_effects=True, vmem_limit_bytes=56 * 1024 * 1024
        ),
    )(
        flow_state, circ_speed, axial_speed, time_step, lsq_weights,
        partner.reshape(1, columns), partner.reshape(TILES, LANES),
        merge_owner.reshape(1, SMALL), merge_source.reshape(1, SMALL),
        merge_host.reshape(1, SMALL), merge_frac.T,
    )


def solution(mesh):
    in_specs = (
        P(None, "circ", "axial"),
        P("circ", "axial"),
        P("circ", "axial"),
        P("circ", "axial"),
        P("axial", None, None),
        P("axial"),
        P(("circ", "axial"), None),
        P(("circ", "axial")),
        P(("circ", "axial")),
        P(("circ", "axial"), None),
    )
    out_specs = (P(None, "circ", "axial"), P(None, "circ", "axial"))
    return jax.shard_map(local, mesh=mesh, in_specs=in_specs, out_specs=out_specs, check_vma=False)
```

```python
import jax
import jax.numpy as jnp
from jax import lax
from jax.experimental import pallas as pl
from jax.experimental.pallas import tpu as pltpu
from jax.sharding import PartitionSpec as P

STEPS = 2
BALANCES = 2 * STEPS
CAP = 8
NV = 5
ROWS = 16
LANES = 128
TILES = 16
HALF = 64
SMALL = 128
BLOCKS = 32
N_CIRC = 16
N_AXIAL = 8
STACK = NV * ROWS
WIDE = NV * LANES
BOX = 3 * LANES
ROW_TILES = 20
EARLY = 17
FIRST = 8
MESH = pl.DeviceIdType.MESH
F32 = jnp.float32
BF16 = jnp.bfloat16
NEIGHBOURS = [(dc, da) for dc in (-1, 0, 1) for da in (-1, 0, 1) if (dc, da) != (0, 0)]
DIRECT = [(-1, 0), (1, 0), (0, -1), (0, 1)]
FAR_FIRST = (0, 2, 5, 7, 1, 6, 3, 4)


def split(x):
    high = x.astype(BF16)
    return high, (x - high.astype(F32)).astype(BF16)


def lanes_of(shape):
    return lax.broadcasted_iota(jnp.int32, shape, len(shape) - 1)


def rolled(x, steps):
    return pltpu.roll(x, steps, x.ndim - 1)


def var_rows(v):
    return slice(v * ROWS, (v + 1) * ROWS)


def var_lanes(v):
    return slice(v * LANES, (v + 1) * LANES)


def cells(p):
    return slice(p * LANES, (p + 1) * LANES)


def kernel(
    flow_hbm, cspd_hbm, aspd_hbm, dt_hbm, w_hbm, prow_hbm, ptile_hbm, owner_hbm, source_hbm,
    host_hbm, frac_hbm,
    out_u, out_rate,
    flow, cspd, aspd, dt, w, partner_row, partner_tile, owner, source, host, frac, load_sem,
    cur, base, cs, xs, wts, s32, shi, slo, rc, gout, gend, ends, gloc, fout, floc, a_loc, a_arr, a_edge, a_end, c_loc, c_arr,
    edges, consts, f_keep, halo, perm, permuted,
    ax_send, ax_recv, ini_recv, row_send, row_recv, ci_send, ci_recv, lab_send, lab_recv, outbox, inbox, box_half, early_box,
    end_send, end_recv, slope_send, slope_recv,
    ax_ss, ax_rs, ini_ss, ini_rs, row_ss, row_rs, ci_ss, ci_rs, lab_ss, lab_rs, box_ss, box_rs,
    end_ss, end_rs, slope_ss, slope_rs,
):
    c = lax.axis_index("circ")
    a = lax.axis_index("axial")

    def peer(dc, da):
        return (lax.rem(c + dc + N_CIRC, N_CIRC), lax.rem(a + da + N_AXIAL, N_AXIAL))

    def remote(src, dst, send, recv, dc, da):
        return pltpu.make_async_remote_copy(
            src_ref=src, dst_ref=dst, send_sem=send, recv_sem=recv,
            device_id=peer(dc, da), device_id_type=MESH,
        )

    def axial_copy(n, side):
        return remote(
            ax_send.at[n, side], ax_recv.at[n, side], ax_ss.at[n, side], ax_rs.at[n, side],
            0, 2 * side - 1,
        )

    head, tail = pl.ds(0, LANES), pl.ds((TILES - 1) * LANES, LANES)

    def first_axial_copy(side):
        return remote(
            flow_hbm.at[:, :, tail if side else head], ax_recv.at[0, side],
            ax_ss.at[0, side], ax_rs.at[0, side], 0, 2 * side - 1,
        )

    def init_copy(k):
        source_of = (dt_hbm.at[:, head], dt_hbm.at[:, tail], aspd_hbm.at[:, tail])
        return remote(
            source_of[k], ini_recv.at[k], ini_ss.at[k], ini_rs.at[k], 0, 1 if k else -1
        )

    def circ_copy(n, side, late):
        part = pl.ds(EARLY, ROW_TILES - EARLY) if late else pl.ds(0, EARLY)
        return remote(
            ci_send.at[n, side, part], ci_recv.at[n, side, part],
            ci_ss.at[n, side, late], ci_rs.at[n, side, late], 2 * side - 1, 0,
        )

    def row_copy():
        return remote(row_send, row_recv, row_ss.at[0], row_rs.at[0], 1, 0)

    def label_copy(k):
        dc, da = NEIGHBOURS[k]
        rows = pl.ds(k * CAP, CAP)
        return remote(lab_send.at[rows], lab_recv.at[rows], lab_ss.at[k], lab_rs.at[k], dc, da)

    def box_copy(n, k):
        dc, da = NEIGHBOURS[k]
        rows = pl.ds(k * CAP, CAP)
        return remote(
            outbox.at[n, rows], inbox.at[n, rows], box_ss.at[n, k], box_rs.at[n, k], dc, da
        )

    def end_target(which, k):
        dc, da = NEIGHBOURS[k]
        return dc, da + (1 if which else -1)

    def end_copy(which, k):
        return remote(
            end_send.at[which, k], end_recv.at[which, k], end_ss.at[which, k],
            end_rs.at[which, k], *end_target(which, k),
        )

    def slope_copy(side):
        return remote(
            slope_send.at[side], slope_recv.at[side], slope_ss.at[side], slope_rs.at[side],
            0, 2 * side - 1,
        )

    own = slice(FIRST, FIRST + ROWS)
    lane = lanes_of((ROWS, LANES))
    box_lane = lanes_of((len(NEIGHBOURS) * CAP, LANES))

    loads = [
        pltpu.make_async_copy(src, dst, load_sem.at[i])
        for i, (src, dst) in enumerate(
            (
                (owner_hbm, owner), (source_hbm, source), (host_hbm, host), (flow_hbm, flow),
                (dt_hbm, dt), (aspd_hbm, aspd), (cspd_hbm, cspd), (frac_hbm, frac),
                (prow_hbm, partner_row), (ptile_hbm, partner_tile), (w_hbm, w),
            )
        )
    ]
    for load in loads:
        load.start()

    barrier = pltpu.get_barrier_semaphore()
    for dc, da in DIRECT:
        pl.semaphore_signal(barrier, inc=1, device_id=peer(dc, da), device_id_type=MESH)

    def pair_place(p, v):
        slot = p - 1 if 0 < p < TILES - 1 else TILES - 2 + p // (TILES - 1)
        if v < NV - 1:
            return (slot if slot < TILES - 2 else slot + 3), 2 * v
        group = slot // 4
        return (TILES - 2 + group if group < 3 else ROW_TILES - 1), 2 * (slot % 4)

    def pack_rows(n, p, v, tile):
        where, row = pair_place(p, v)
        ci_send[n, 0, where, row:row + 2, :] = tile[0:2]
        ci_send[n, 1, where, row:row + 2, :] = tile[ROWS - 2:ROWS]

    def shift(q, v, left_tile, right_tile):
        moved = rolled(jnp.where(lane >= HALF, left_tile, right_tile), HALF)
        high, low = split(moved)
        xs[q, var_rows(v), :] = high
        xs[q, STACK + v * ROWS:STACK + (v + 1) * ROWS, :] = low

    for load in loads[:3]:
        load.wait()
    square = (SMALL, SMALL)
    t_row = owner[...]
    s_row = source[...]
    h_row = host[...]

    def as_columns(row):
        return jnp.broadcast_to(row.astype(F32), square).T.astype(jnp.int32)

    t_col, s_col, h_col = as_columns(t_row), as_columns(s_row), as_columns(h_row)
    myself = c * N_AXIAL + a
    first = lax.broadcasted_iota(jnp.int32, square, 0)
    second = lax.broadcasted_iota(jnp.int32, square, 1)
    shares = jnp.where((jnp.broadcast_to(t_row, square) == t_col) & (first < second), 1.0, 0.0)
    rank = jnp.sum(shares, axis=0, keepdims=True).astype(jnp.int32)
    circ_off = ((t_row >> 3) - c + 1 + N_CIRC) & (N_CIRC - 1)
    number = circ_off * 3 + (t_row & (N_AXIAL - 1)) - a + 1
    number = jnp.where(number > 4, number - 1, number)
    place = jnp.where(t_row == myself, -1, number * CAP + rank)
    slots = len(NEIGHBOURS) * CAP
    chosen = jnp.where(
        jnp.broadcast_to(place, (slots, SMALL))
        == lax.broadcasted_iota(jnp.int32, (slots, SMALL), 0),
        1.0, 0.0,
    )

    def row_index(s):
        return ((s & (BLOCKS - 1)) >> 1) * ROWS + (s >> 5)

    host_index = row_index(h_row)
    marks = 2 * (host_index + 1) + (h_row & 1)
    labels = jnp.sum(chosen * marks.astype(F32), axis=1, keepdims=True)
    lab_send[...] = jnp.broadcast_to(labels, (slots, LANES))

    edges[...] = jnp.zeros_like(edges)
    consts[...] = jnp.zeros_like(consts)
    pl.semaphore_wait(barrier, len(DIRECT))
    for side in range(2):
        first_axial_copy(side).start()
    for k in range(3):
        init_copy(k).start()
    for load in loads[3:7]:
        load.wait()
    for p in range(TILES):
        columns = slice(p * LANES, (p + 1) * LANES)
        speed = cspd[:, columns]
        cs[p, own, :] = speed
        row_send[p:p + 1, :] = speed[ROWS - 1:ROWS]
    row_copy().start()
    for v in range(NV):
        before = None
        for p in range(TILES):
            tile = flow[v, :, p * LANES:(p + 1) * LANES]
            cur[p, v, own, :] = tile
            pack_rows(0, p, v, tile)
            if p > 0:
                shift(p, v, before, tile)
            before = tile
    for side in range(2):
        circ_copy(0, side, 0).start()
    for load in loads[7:10]:
        load.wait()
    frac_twice = jnp.concatenate([frac[...], frac[...]], axis=0).T
    placed = jnp.where((second >> 6) == (h_col & 1), frac_twice, 0.0)
    same_half = (s_col & 1) == (h_col & 1)
    straight = jnp.where(same_half, placed, 0.0)
    crossed = jnp.where(same_half, 0.0, placed)
    is_local = t_col == myself
    floc[0] = jnp.where(is_local, straight, 0.0)
    floc[1] = jnp.where(is_local, crossed, 0.0)
    in_source = (second >> 6) == (s_col & 1)
    fout[0] = jnp.dot(
        chosen, jnp.where(in_source, frac_twice, 0.0), precision=lax.Precision.HIGHEST
    )
    fout[1] = jnp.dot(
        chosen, jnp.where(in_source, 0.0, frac_twice), precision=lax.Precision.HIGHEST
    )
    s_index = row_index(s_col)
    pick = jnp.concatenate(
        [
            jnp.where(s_index == second, 1.0, 0.0),
            jnp.where(s_index == second + LANES, 1.0, 0.0),
        ],
        axis=1,
    ).astype(BF16)
    gloc[...] = pick
    picked_out = jnp.dot(chosen.astype(BF16), pick, preferred_element_type=F32)
    gout[...] = picked_out.astype(BF16)
    picked_end = jnp.concatenate([picked_out[:, :ROWS], picked_out[:, -ROWS:]], axis=1)
    gend[...] = jnp.concatenate([picked_end, picked_end], axis=1).astype(BF16)
    tall = (TILES * ROWS, SMALL)
    tall_rows = lax.broadcasted_iota(jnp.int32, tall, 0)
    wanted = jnp.where(t_row == myself, host_index, -1)
    land = jnp.where(jnp.broadcast_to(wanted, tall) == tall_rows, 1.0, 0.0).astype(BF16)
    a_loc[...] = jnp.concatenate([land, land], axis=1)

    @pl.when(c > 0)
    def _():
        perm[0] = partner_tile[...] >> 7
        perm[1] = partner_tile[...] & (LANES - 1)

    @pl.when(c == 0)
    def _():
        columns = TILES * LANES
        target = partner_row[...]
        upper = jnp.where(
            jnp.broadcast_to(target >> 7, (TILES, columns))
            == lax.broadcasted_iota(jnp.int32, (TILES, columns), 0),
            1.0, 0.0,
        ).astype(BF16)
        tall_lanes = (LANES, columns)
        here = jnp.broadcast_to(target & (LANES - 1), tall_lanes) == lax.broadcasted_iota(
            jnp.int32, tall_lanes, 0
        )
        position = lanes_of(tall_lanes)
        for part, value in enumerate((position >> 7, position & (LANES - 1))):
            lower = jnp.where(here, value.astype(F32), 0.0).astype(BF16)
            perm[part] = lax.dot_general(
                upper, lower, (((1,), (1,)), ((), ())), preferred_element_type=F32
            ).astype(jnp.int32)

    def weigh(p, _):
        gap = jnp.zeros((HALF, HALF), F32)
        both = jnp.concatenate(
            [
                jnp.concatenate([w[2 * p], gap], axis=1),
                jnp.concatenate([gap, w[2 * p + 1]], axis=1),
            ],
            axis=0,
        )
        high, low = split(both.T)
        wts[p, :, 0:LANES] = high
        wts[p, :, LANES:] = low
        return 0

    loads[10].wait()
    lax.fori_loop(0, TILES, weigh, 0)

    def receive_constants():
        for k in range(3):
            init_copy(k).wait()
        consts[0] = jnp.where(a > 0, ini_recv[1], 0.0)
        consts[1] = jnp.where(a < N_AXIAL - 1, ini_recv[0], 0.0)
        consts[2] = jnp.where((a > 0) & (lane == 0), rolled(ini_recv[2], 1), 0.0)
        consts[3] = jnp.where(lane == LANES - 1, aspd[:, (TILES - 1) * LANES:], 0.0)
        row_copy().wait()
        for half in range(2):
            some = slice(half * 8, half * 8 + 8)
            below_row = row_recv[some, :]
            mixed = jnp.zeros_like(below_row)
            for q in range(TILES):
                found = jnp.take_along_axis(
                    jnp.broadcast_to(row_recv[q:q + 1, :], below_row.shape), perm[1, some, :], axis=1
                )
                mixed = jnp.where(perm[0, some, :] == q, found, mixed)
            below_row = jnp.where(c == 0, mixed, below_row)
            for k in range(8):
                cs[half * 8 + k, FIRST - 1:FIRST, :] = below_row[k:k + 1]

    def end_matrix():
        slot_marks = jnp.concatenate([lab_send[...], lab_send[...]], axis=0).T.astype(jnp.int32)
        slot_marks = jnp.concatenate([slot_marks, slot_marks], axis=0)
        index = tall_rows & (ROWS - 1)
        target = jnp.where(
            tall_rows < SMALL, 2 * (index + 1), 2 * ((TILES - 1) * ROWS + index + 1) + 1
        )
        slot_of = (lanes_of(tall) & (slots - 1)) >> 3
        hit = (slot_marks == target) & (slot_of == ((tall_rows >> 4) & 7))
        a_end[...] = jnp.where(hit, 1.0, 0.0).astype(BF16)

    def send_ends(n):
        packed_lane = lanes_of(tall)
        result = jnp.zeros(tall, F32)
        for t in range(BOX // LANES):
            high, low = split(outbox[n, :, t * LANES:(t + 1) * LANES])
            both = jnp.concatenate([high, low], axis=0)
            columns = jnp.dot(a_end[...], both, preferred_element_type=F32)
            for v in range(2 * t, min(2 * t + 2, NV)):
                moved = rolled(columns, v + HALF) if v % 2 else rolled(columns, v) if v else columns
                wanted = (packed_lane == v) | (packed_lane == HALF - 1 + v)
                result = jnp.where(wanted, moved, result)
        for which in range(2):
            for k in range(len(NEIGHBOURS)):
                start = (which * len(NEIGHBOURS) + k) * ROWS
                end_send[which, k] = result[start:start + ROWS]
        for k in FAR_FIRST:
            for which in range(2):
                if end_target(which, k) != (0, 0):
                    end_copy(which, k).start()

    def send_slopes():
        for side in range(2):
            total = jnp.zeros((ROWS, LANES), F32)
            for v in range(NV):
                tile = s32[side * (TILES - 1), var_rows(v), :]
                moved = rolled(tile, v + side) if v + side else tile
                total = jnp.where(lane == v, moved, total)
            slope_send[side] = total
            slope_copy(side).start()

    def receive_ends():
        for side in range(2):
            slope_copy(side).wait()
        sums = []
        for which in range(2):
            total = None
            for k in range(len(NEIGHBOURS)):
                if end_target(which, k) == (0, 0):
                    part = end_send[which, k]
                else:
                    end_copy(which, k).wait()
                    part = end_recv[which, k]
                total = part if total is None else total + part
            sums.append(total)
        slope_right = slope_recv[0] + sums[0]
        slope_left = slope_recv[1] + rolled(sums[1], LANES - HALF + 1)
        return slope_left, slope_right

    def receive_labels():
        for k in range(len(NEIGHBOURS)):
            label_copy(k).wait()
        arrived = lab_recv[...].astype(jnp.int32)
        box_half[...] = jnp.where((lanes_of(arrived.shape) >> 6) == (arrived & 1), 1.0, 0.0)
        places = ((arrived >> 1) - 1).astype(F32)
        label_row = jnp.concatenate([places, places], axis=0).T.astype(jnp.int32)
        land_here = jnp.where(
            jnp.concatenate([label_row, label_row], axis=0) == tall_rows, 1.0, 0.0
        ).astype(BF16)
        a_arr[...] = land_here[2 * ROWS:-2 * ROWS]
        a_edge[0:2 * ROWS, :] = land_here[0:2 * ROWS]
        a_edge[2 * ROWS:, :] = land_here[-2 * ROWS:]

    def fix_edges(n, factor, also_rate):
        if also_rate:
            slope_left, slope_right = receive_ends()
        else:
            for side in range(2):
                axial_copy(n, side).wait()
        left_speed, right_speed = consts[2], consts[3]
        last = (TILES - 1) * LANES
        for v in range(NV):
            vr = var_rows(v)
            if also_rate:
                aligned = rolled(slope_left, LANES - v) if v else slope_left
                from_left = rolled(halo[0, v], 1) + 0.5 * aligned
                from_right = rolled(halo[1, v], LANES - 1) - 0.5 * rolled(
                    slope_right, LANES - 1 - v
                )
            else:
                from_left, from_right = ax_recv[n, 1, v], ax_recv[n, 0, v]
            from_left = jnp.where(a > 0, from_left, 0.0)
            from_right = jnp.where(a < N_AXIAL - 1, from_right, 0.0)
            left_flux = jnp.maximum(left_speed, 0.0) * from_left + jnp.minimum(
                left_speed, 0.0
            ) * edges[0, vr, :]
            right_flux = jnp.maximum(right_speed, 0.0) * edges[1, vr, :] + jnp.minimum(
                right_speed, 0.0
            ) * from_right
            cur[0, v, own, :] = cur[0, v, own, :] + factor * dt[:, 0:LANES] * left_flux
            cur[TILES - 1, v, own, :] = (
                cur[TILES - 1, v, own, :] - factor * dt[:, last:] * right_flux
            )
            if also_rate:
                out_rate[v, :, 0:LANES] = out_rate[v, :, 0:LANES] - left_flux
                out_rate[v, :, last:] = out_rate[v, :, last:] + right_flux
            else:
                halo[0, v] = from_left - factor * consts[0] * rolled(left_flux, LANES - 1)
                halo[1, v] = from_right + factor * consts[1] * rolled(right_flux, 1)

    def slopes(p):
        left = jnp.concatenate([xs[p], xs[p + 1]], axis=1)
        full = jnp.dot(left, wts[p], preferred_element_type=F32)
        total = full[:STACK, :LANES] + full[:STACK, LANES:] + full[STACK:, :LANES]
        s32[p] = total
        high, low = split(total)
        rows = slice(p * ROWS, (p + 1) * ROWS)
        for v in range(NV):
            shi[rows, var_lanes(v)] = high[var_rows(v)]
            slo[rows, var_lanes(v)] = low[var_rows(v)]
            if p in (0, TILES - 1):
                start = ROWS * (p // (TILES - 1))
                ends[start:start + ROWS, var_lanes(v)] = high[var_rows(v)]
                ends[2 * ROWS + start:3 * ROWS + start, var_lanes(v)] = low[var_rows(v)]

    def gathered(picks, factors, v):
        vl = var_lanes(v)
        picked = jnp.dot(picks[...], shi[:, vl], preferred_element_type=F32) + jnp.dot(
            picks[...], slo[:, vl], preferred_element_type=F32
        )
        return picked * factors[0] + rolled(picked, HALF) * factors[1]

    def scatter(matrix, values, v, tiles):
        added = jnp.dot(matrix[...], values[:, var_lanes(v)], preferred_element_type=F32)
        for i, p in enumerate(tiles):
            s32[p, var_rows(v), :] = s32[p, var_rows(v), :] + added[i * ROWS:(i + 1) * ROWS]

    def late_rows(n):
        for v in range(NV):
            for p in (0, TILES - 1):
                pack_rows(n, p, v, cur[p, v, own, :])

    def is_late(p, v):
        return pair_place(p, v)[0] >= EARLY

    def unpack(n, side, late):
        start = FIRST - 2 if side else FIRST + ROWS
        for p in range(TILES):
            for v in range(NV):
                if is_late(p, v) == late:
                    where, row = pair_place(p, v)
                    cur[p, v, start:start + 2, :] = ci_recv[n, side, where, row:row + 2, :]

    def permute(n, side, late):
        start = FIRST - 2 if side else FIRST + ROWS
        rows = lax.broadcasted_iota(jnp.int32, (8, LANES), 0)

        def one(p):
            tile = jnp.broadcast_to(perm[0, pl.ds(p, 1), :], (8, LANES))
            column = jnp.broadcast_to(perm[1, pl.ds(p, 1), :], (8, LANES))
            slot = jnp.where(
                tile == 0, TILES - 2, jnp.where(tile == TILES - 1, TILES - 1, tile - 1)
            )
            offset = slot - (rows >> 1)
            if late:
                total, last = permuted[0, p], permuted[1, p]
            else:
                total = last = jnp.zeros((8, LANES), F32)
            for q in range(TILES):
                if is_late(q, 0) == late:
                    where, _ = pair_place(q, 0)
                    found = jnp.take_along_axis(ci_recv[n, side, where], column, axis=1)
                    total = jnp.where(tile == q, found, total)
            for g in range(4):
                if (g == 3) == late:
                    where = TILES - 2 + g if g < 3 else ROW_TILES - 1
                    found = jnp.take_along_axis(ci_recv[n, side, where], column, axis=1)
                    last = jnp.where(offset == 4 * g, found, last)
            if not late:
                permuted[0, p], permuted[1, p] = total, last
                return
            last = last + pltpu.roll(last, 4, 0)
            last = last + pltpu.roll(last, 2, 0)
            for v in range(NV - 1):
                cur[p, v, start:start + 2, :] = total[2 * v:2 * v + 2]
            cur[p, NV - 1, start:start + 2, :] = last[0:2]

        def four(i, _):
            for k in range(4):
                one(4 * i + k)
            return 0

        lax.fori_loop(0, TILES // 4, four, 0)

    def halo_rows(n, late):
        for side in range(2):
            circ_copy(n, side, int(late)).wait()

        @pl.when(c > 0)
        def _():
            unpack(n, 1, late)

        @pl.when(c < N_CIRC - 1)
        def _():
            unpack(n, 0, late)

        @pl.when(c == 0)
        def _():
            permute(n, 1, late)

        @pl.when(c == N_CIRC - 1)
        def _():
            permute(n, 0, late)

    def circ_rates(p, _):
        above = cs[p, own, :]
        below = cs[p, FIRST - 1:FIRST + ROWS - 1, :]
        above_pos, above_neg = jnp.maximum(above, 0.0), jnp.minimum(above, 0.0)
        below_pos, below_neg = jnp.maximum(below, 0.0), jnp.minimum(below, 0.0)
        for v in range(NV):
            at = [cur[p, v, FIRST + k:FIRST + k + ROWS, :] for k in (-2, -1, 0, 1, 2)]
            slope_below = 0.25 * (at[2] - at[0])
            slope_here = 0.25 * (at[3] - at[1])
            slope_above = 0.25 * (at[4] - at[2])
            upper = above_pos * (at[2] + slope_here) + above_neg * (at[3] - slope_above)
            lower = below_pos * (at[1] + slope_below) + below_neg * (at[2] - slope_here)
            rc[p, var_rows(v), :] = upper - lower
        return 0

    def face(p, v, kind):
        half_slope = 0.5 * s32[p, var_rows(v), :]
        here = cur[p, v, own, :]
        return here + half_slope if kind == 0 else here - half_slope

    def flux(p, v, right_lane):
        speed = aspd[:, cells(p)]
        right = rolled(jnp.where(lane == 0, right_lane, face(p, v, 1)), LANES - 1)
        return jnp.maximum(speed, 0.0) * face(p, v, 0) + jnp.minimum(speed, 0.0) * right

    def advance(p, v, flux_here, flux_left, first_stage, factor):
        before = rolled(jnp.where(lane == LANES - 1, flux_left, flux_here), 1)
        rate = rc[p, var_rows(v), :] + flux_here - before
        here = cur[p, v, own, :]
        start = jnp.where(first_stage, here, base[p, var_rows(v), :])
        base[p, var_rows(v), :] = start
        out_rate[v, :, cells(p)] = rate
        new = 0.5 * (start + here) - factor * (dt[:, cells(p)] * rate)
        cur[p, v, own, :] = new
        return new

    def balance(n, _):
        odd = lax.rem(n, 2)
        first_stage = odd == 0
        factor = jnp.where(first_stage, 1.0, 0.5).astype(F32)
        earlier = jnp.where(first_stage, 0.5, 1.0).astype(F32)
        end = TILES - 1

        for p in range(1, end):
            slopes(p)
        for rows in (slice(0, ROWS), slice(end * ROWS, TILES * ROWS)):
            shi[rows, :] = jnp.zeros((ROWS, WIDE), BF16)
            slo[rows, :] = jnp.zeros((ROWS, WIDE), BF16)
        for v in range(NV):
            early_box[:, var_lanes(v)] = gathered(gout, fout, v)
        fix_edges(n, earlier, False)
        late_rows(n)
        for side in range(2):
            circ_copy(n, side, 1).start()
        for v in range(NV):
            shift(0, v, halo[0, v], cur[0, v, own, :])
            shift(TILES, v, cur[end, v, own, :], halo[1, v])
        slopes(0)
        slopes(end)
        for v in range(NV):
            picked = jnp.dot(gend[...], ends[:, var_lanes(v)], preferred_element_type=F32)
            sent = early_box[:, var_lanes(v)] + picked * fout[0] + rolled(picked, HALF) * fout[1]
            columns = slice(v // 2 * LANES, v // 2 * LANES + LANES)
            if v % 2:
                outbox[n, :, columns] = jnp.where(box_lane < HALF, previous, sent)
            elif v == NV - 1:
                outbox[n, :, columns] = sent
            previous = sent
        for k in FAR_FIRST:
            box_copy(n, k).start()

        @pl.when(n == 0)
        def _():
            for k in FAR_FIRST:
                label_copy(k).start()

        @pl.when(n == 0)
        def _():
            receive_constants()
            end_matrix()

        @pl.when(n == BALANCES - 1)
        def _():
            send_ends(n)

        for v in range(NV):
            high, low = split(gathered(gloc, floc, v))
            c_loc[:SMALL, var_lanes(v)] = high
            c_loc[SMALL:, var_lanes(v)] = low
        for v in range(NV):
            scatter(a_loc, c_loc, v, range(TILES))

        @pl.when(n == BALANCES - 1)
        def _():
            send_slopes()

        halo_rows(n, False)
        at_seam = (c == 0) | (c == N_CIRC - 1)
        whole = [p for p in range(TILES) if not is_late(p, NV - 1)]

        @pl.when(jnp.logical_not(at_seam))
        def _():
            for p in whole:
                circ_rates(p, 0)

        halo_rows(n, True)

        @pl.when(at_seam)
        def _():
            for p in whole:
                circ_rates(p, 0)

        for p in range(TILES):
            if p not in whole:
                circ_rates(p, 0)

        for k in range(len(NEIGHBOURS)):
            box_copy(n, k).wait()

        @pl.when(n == 0)
        def _():
            receive_labels()

        for v in range(NV):
            columns = slice(v // 2 * LANES, v // 2 * LANES + LANES)
            packed = inbox[n, :, columns]
            if v == NV - 1:
                both = packed
            else:
                both = jnp.where((box_lane < HALF) == (v % 2 == 0), packed, rolled(packed, HALF))
            high, low = split(both * box_half[...])
            c_arr[:slots, var_lanes(v)] = high
            c_arr[slots:, var_lanes(v)] = low
        for v in range(NV):
            scatter(a_edge, c_arr, v, (0, 1, end - 1, end))

        for v in range(NV):
            vr = var_rows(v)
            right_face = face(0, v, 1)
            flux_first = flux(0, v, face(1, v, 1))
            left_face = face(end, v, 0)
            flux_before = flux(end - 1, v, face(end, v, 1))
            flux_last = jnp.where(lane == LANES - 1, 0.0, flux(end, v, 0.0))
            edges[0, vr, :] = right_face
            edges[1, vr, :] = left_face
            f_keep[0, vr, :] = flux_first
            f_keep[1, vr, :] = flux_before
            new_first = advance(0, v, flux_first, 0.0, first_stage, factor)
            new_last = advance(end, v, flux_last, flux_before, first_stage, factor)
            ax_send[n + 1, 0, v] = jnp.where(
                lane < HALF, new_first, rolled(right_face, LANES - 1)
            )
            ax_send[n + 1, 1, v] = jnp.where(lane >= HALF, new_last, rolled(left_face, 1))

        @pl.when(n < BALANCES - 1)
        def _():
            for side in range(2):
                axial_copy(n + 1, side).start()

        for v in range(NV):
            scatter(a_arr, c_arr, v, range(2, end - 1))
        for v in range(NV):
            before = f_keep[0, var_rows(v), :]
            tile = cur[0, v, own, :]
            for p in range(1, end):
                here = flux(p, v, face(p + 1, v, 1)) if p < end - 1 else f_keep[1, var_rows(v), :]
                new = advance(p, v, here, before, first_stage, factor)
                pack_rows(n + 1, p, v, new)
                shift(p, v, tile, new)
                before, tile = here, new
            shift(end, v, tile, cur[end, v, own, :])

        @pl.when(n < BALANCES - 1)
        def _():
            for side in range(2):
                circ_copy(n + 1, side, 0).start()

        return 0

    lax.fori_loop(0, BALANCES, balance, 0)
    fix_edges(BALANCES, jnp.float32(0.5), True)

    for p in range(TILES):
        for v in range(NV):
            out_u[v, :, cells(p)] = cur[p, v, own, :]


def local(
    flow_state, circ_speed, axial_speed, time_step, lsq_weights,
    partner, merge_owner, merge_source, merge_host, merge_frac,
):
    columns = TILES * LANES
    slots = len(NEIGHBOURS) * CAP
    vmem = pl.BlockSpec(memory_space=pltpu.VMEM)
    hbm = pl.BlockSpec(memory_space=pltpu.HBM)
    dma = pltpu.SemaphoreType.DMA
    shape = jax.ShapeDtypeStruct((NV, ROWS, columns), F32)
    scratch = [
        pltpu.VMEM((NV, ROWS, columns), F32),
        pltpu.VMEM((ROWS, columns), F32),
        pltpu.VMEM((ROWS, columns), F32),
        pltpu.VMEM((ROWS, columns), F32),
        pltpu.VMEM((BLOCKS, HALF, 3 * HALF), F32),
        pltpu.VMEM((1, columns), jnp.int32),
        pltpu.VMEM((TILES, LANES), jnp.int32),
        pltpu.VMEM((1, SMALL), jnp.int32),
        pltpu.VMEM((1, SMALL), jnp.int32),
        pltpu.VMEM((1, SMALL), jnp.int32),
        pltpu.VMEM((HALF, SMALL), F32),
        dma((11,)),
        pltpu.VMEM((TILES, NV, 2 * ROWS, LANES), F32),
        pltpu.VMEM((TILES, STACK, LANES), F32),
        pltpu.VMEM((TILES, 2 * ROWS, LANES), F32),
        pltpu.VMEM((TILES + 1, 2 * STACK, LANES), BF16),
        pltpu.VMEM((TILES, 2 * LANES, 2 * LANES), BF16),
        pltpu.VMEM((TILES, STACK, LANES), F32),
        pltpu.VMEM((TILES * ROWS, WIDE), BF16),
        pltpu.VMEM((TILES * ROWS, WIDE), BF16),
        pltpu.VMEM((TILES, STACK, LANES), F32),
        pltpu.VMEM((slots, TILES * ROWS), BF16),
        pltpu.VMEM((slots, 4 * ROWS), BF16),
        pltpu.VMEM((4 * ROWS, WIDE), BF16),
        pltpu.VMEM((SMALL, TILES * ROWS), BF16),
        pltpu.VMEM((2, slots, LANES), F32),
        pltpu.VMEM((2, SMALL, LANES), F32),
        pltpu.VMEM((TILES * ROWS, 2 * SMALL), BF16),
        pltpu.VMEM(((TILES - 4) * ROWS, 2 * slots), BF16),
        pltpu.VMEM((4 * ROWS, 2 * slots), BF16),
        pltpu.VMEM((TILES * ROWS, 2 * slots), BF16),
        pltpu.VMEM((2 * SMALL, WIDE), BF16),
        pltpu.VMEM((2 * slots, WIDE), BF16),
        pltpu.VMEM((2, STACK, LANES), F32),
        pltpu.VMEM((4, ROWS, LANES), F32),
        pltpu.VMEM((2, STACK, LANES), F32),
        pltpu.VMEM((2, NV, ROWS, LANES), F32),
        pltpu.VMEM((2, TILES, LANES), jnp.int32),
        pltpu.VMEM((2, TILES, 8, LANES), F32),
        pltpu.VMEM((BALANCES + 1, 2, NV, ROWS, LANES), F32),
        pltpu.VMEM((BALANCES + 1, 2, NV, ROWS, LANES), F32),
        pltpu.VMEM((3, ROWS, LANES), F32),
        pltpu.VMEM((TILES, LANES), F32),
        pltpu.VMEM((TILES, LANES), F32),
        pltpu.VMEM((BALANCES + 1, 2, ROW_TILES, 8, LANES), F32),
        pltpu.VMEM((BALANCES, 2, ROW_TILES, 8, LANES), F32),
        pltpu.VMEM((slots, LANES), F32),
        pltpu.VMEM((slots, LANES), F32),
        pltpu.VMEM((BALANCES, slots, BOX), F32),
        pltpu.VMEM((BALANCES, slots, BOX), F32),
        pltpu.VMEM((slots, LANES), F32),
        pltpu.VMEM((slots, WIDE), F32),
        pltpu.VMEM((2, len(NEIGHBOURS), ROWS, LANES), F32),
        pltpu.VMEM((2, len(NEIGHBOURS), ROWS, LANES), F32),
        pltpu.VMEM((2, ROWS, LANES), F32),
        pltpu.VMEM((2, ROWS, LANES), F32),
        dma((BALANCES + 1, 2)), dma((BALANCES + 1, 2)),
        dma((3,)), dma((3,)),
        dma((1,)), dma((1,)),
        dma((BALANCES, 2, 2)), dma((BALANCES, 2, 2)),
        dma((len(NEIGHBOURS),)), dma((len(NEIGHBOURS),)),
        dma((BALANCES, len(NEIGHBOURS))), dma((BALANCES, len(NEIGHBOURS))),
        dma((2, len(NEIGHBOURS))), dma((2, len(NEIGHBOURS))), dma((2,)), dma((2,)),
    ]
    return pl.pallas_call(
        kernel,
        out_shape=(pltpu.VMEM((NV, ROWS, columns), F32),) * 2,
        in_specs=[hbm] * 11,
        out_specs=(vmem, vmem),
        scratch_shapes=scratch,
        compiler_params=pltpu.CompilerParams(
            collective_id=0, has_side_effects=True, vmem_limit_bytes=56 * 1024 * 1024
        ),
    )(
        flow_state, circ_speed, axial_speed, time_step, lsq_weights,
        partner.reshape(1, columns), partner.reshape(TILES, LANES),
        merge_owner.reshape(1, SMALL), merge_source.reshape(1, SMALL),
        merge_host.reshape(1, SMALL), merge_frac.T,
    )


def solution(mesh):
    in_specs = (
        P(None, "circ", "axial"),
        P("circ", "axial"),
        P("circ", "axial"),
        P("circ", "axial"),
        P("axial", None, None),
        P("axial"),
        P(("circ", "axial"), None),
        P(("circ", "axial")),
        P(("circ", "axial")),
        P(("circ", "axial"), None),
    )
    out_specs = (P(None, "circ", "axial"), P(None, "circ", "axial"))
    return jax.shard_map(local, mesh=mesh, in_specs=in_specs, out_specs=out_specs, check_vma=False)
```

```python
import jax
import jax.numpy as jnp
from jax import lax
from jax.experimental import pallas as pl
from jax.experimental.pallas import tpu as pltpu
from jax.sharding import PartitionSpec as P

STEPS = 2
BALANCES = 2 * STEPS
CAP = 8
NV = 5
ROWS = 16
LANES = 128
TILES = 16
HALF = 64
SMALL = 128
BLOCKS = 32
N_CIRC = 16
N_AXIAL = 8
STACK = NV * ROWS
WIDE = NV * LANES
BOX = 3 * LANES
ROW_TILES = 20
EARLY = 17
FIRST = 8
MESH = pl.DeviceIdType.MESH
F32 = jnp.float32
BF16 = jnp.bfloat16
NEIGHBOURS = [(dc, da) for dc in (-1, 0, 1) for da in (-1, 0, 1) if (dc, da) != (0, 0)]
DIRECT = [(-1, 0), (1, 0), (0, -1), (0, 1)]
FAR_FIRST = (0, 2, 5, 7, 1, 6, 3, 4)


def split(x):
    high = x.astype(BF16)
    return high, (x - high.astype(F32)).astype(BF16)


def lanes_of(shape):
    return lax.broadcasted_iota(jnp.int32, shape, len(shape) - 1)


def rolled(x, steps):
    return pltpu.roll(x, steps, x.ndim - 1)


def var_rows(v):
    return slice(v * ROWS, (v + 1) * ROWS)


def var_lanes(v):
    return slice(v * LANES, (v + 1) * LANES)


def cells(p):
    return slice(p * LANES, (p + 1) * LANES)


def kernel(
    flow_hbm, cspd_hbm, aspd_hbm, dt_hbm, w_hbm, prow_hbm, ptile_hbm, owner_hbm, source_hbm,
    host_hbm, frac_hbm,
    out_half, out_circ, out_axial,
    flow, cspd, aspd, dt, w, partner_row, partner_tile, owner, source, host, frac, load_sem,
    cur, base, cs, xs, wts, s32, shi, slo, gout, gend, ends, gloc, fout, floc, a_loc, a_arr, a_edge, a_end, c_loc, c_arr,
    edges, consts, f_keep, halo, perm, permuted,
    ax_send, ax_recv, ini_recv, row_send, row_recv, ci_send, ci_recv, lab_send, lab_recv, outbox, inbox, box_half, early_box,
    end_send, end_recv, slope_send, slope_recv,
    ax_ss, ax_rs, ini_ss, ini_rs, row_ss, row_rs, ci_ss, ci_rs, lab_ss, lab_rs, box_ss, box_rs,
    end_ss, end_rs, slope_ss, slope_rs,
):
    c = lax.axis_index("circ")
    a = lax.axis_index("axial")

    def peer(dc, da):
        return (lax.rem(c + dc + N_CIRC, N_CIRC), lax.rem(a + da + N_AXIAL, N_AXIAL))

    def remote(src, dst, send, recv, dc, da):
        return pltpu.make_async_remote_copy(
            src_ref=src, dst_ref=dst, send_sem=send, recv_sem=recv,
            device_id=peer(dc, da), device_id_type=MESH,
        )

    def axial_copy(n, side):
        return remote(
            ax_send.at[n, side], ax_recv.at[n, side], ax_ss.at[n, side], ax_rs.at[n, side],
            0, 2 * side - 1,
        )

    head, tail = pl.ds(0, LANES), pl.ds((TILES - 1) * LANES, LANES)

    def first_axial_copy(side):
        return remote(
            flow_hbm.at[:, :, tail if side else head], ax_recv.at[0, side],
            ax_ss.at[0, side], ax_rs.at[0, side], 0, 2 * side - 1,
        )

    def init_copy(k):
        source_of = (dt_hbm.at[:, head], dt_hbm.at[:, tail], aspd_hbm.at[:, tail])
        return remote(
            source_of[k], ini_recv.at[k], ini_ss.at[k], ini_rs.at[k], 0, 1 if k else -1
        )

    def circ_copy(n, side, late):
        part = pl.ds(EARLY, ROW_TILES - EARLY) if late else pl.ds(0, EARLY)
        return remote(
            ci_send.at[n, side, part], ci_recv.at[n, side, part],
            ci_ss.at[n, side, late], ci_rs.at[n, side, late], 2 * side - 1, 0,
        )

    def row_copy():
        return remote(row_send, row_recv, row_ss.at[0], row_rs.at[0], 1, 0)

    def label_copy(k):
        dc, da = NEIGHBOURS[k]
        rows = pl.ds(k * CAP, CAP)
        return remote(lab_send.at[rows], lab_recv.at[rows], lab_ss.at[k], lab_rs.at[k], dc, da)

    def box_copy(n, k):
        dc, da = NEIGHBOURS[k]
        rows = pl.ds(k * CAP, CAP)
        return remote(
            outbox.at[n, rows], inbox.at[n, rows], box_ss.at[n, k], box_rs.at[n, k], dc, da
        )

    def end_target(which, k):
        dc, da = NEIGHBOURS[k]
        return dc, da + (1 if which else -1)

    def end_copy(which, k):
        return remote(
            end_send.at[which, k], end_recv.at[which, k], end_ss.at[which, k],
            end_rs.at[which, k], *end_target(which, k),
        )

    def slope_copy(side):
        return remote(
            slope_send.at[side], slope_recv.at[side], slope_ss.at[side], slope_rs.at[side],
            0, 2 * side - 1,
        )

    own = slice(FIRST, FIRST + ROWS)
    lane = lanes_of((ROWS, LANES))
    box_lane = lanes_of((len(NEIGHBOURS) * CAP, LANES))

    loads = [
        pltpu.make_async_copy(src, dst, load_sem.at[i])
        for i, (src, dst) in enumerate(
            (
                (owner_hbm, owner), (source_hbm, source), (host_hbm, host), (flow_hbm, flow),
                (dt_hbm, dt), (aspd_hbm, aspd), (cspd_hbm, cspd), (frac_hbm, frac),
                (prow_hbm, partner_row), (ptile_hbm, partner_tile), (w_hbm, w),
            )
        )
    ]
    for load in loads:
        load.start()

    barrier = pltpu.get_barrier_semaphore()
    for dc, da in DIRECT:
        pl.semaphore_signal(barrier, inc=1, device_id=peer(dc, da), device_id_type=MESH)

    def pair_place(p, v):
        slot = p - 1 if 0 < p < TILES - 1 else TILES - 2 + p // (TILES - 1)
        if v < NV - 1:
            return (slot if slot < TILES - 2 else slot + 3), 2 * v
        group = slot // 4
        return (TILES - 2 + group if group < 3 else ROW_TILES - 1), 2 * (slot % 4)

    def pack_rows(n, p, v, tile):
        where, row = pair_place(p, v)
        ci_send[n, 0, where, row:row + 2, :] = tile[0:2]
        ci_send[n, 1, where, row:row + 2, :] = tile[ROWS - 2:ROWS]

    def shift(q, v, left_tile, right_tile):
        moved = rolled(jnp.where(lane >= HALF, left_tile, right_tile), HALF)
        high, low = split(moved)
        xs[q, var_rows(v), :] = high
        xs[q, STACK + v * ROWS:STACK + (v + 1) * ROWS, :] = low

    for load in loads[:3]:
        load.wait()
    square = (SMALL, SMALL)
    t_row = owner[...]
    s_row = source[...]
    h_row = host[...]

    def as_columns(row):
        return jnp.broadcast_to(row.astype(F32), square).T.astype(jnp.int32)

    t_col, s_col, h_col = as_columns(t_row), as_columns(s_row), as_columns(h_row)
    myself = c * N_AXIAL + a
    first = lax.broadcasted_iota(jnp.int32, square, 0)
    second = lax.broadcasted_iota(jnp.int32, square, 1)
    shares = jnp.where((jnp.broadcast_to(t_row, square) == t_col) & (first < second), 1.0, 0.0)
    rank = jnp.sum(shares, axis=0, keepdims=True).astype(jnp.int32)
    circ_off = ((t_row >> 3) - c + 1 + N_CIRC) & (N_CIRC - 1)
    number = circ_off * 3 + (t_row & (N_AXIAL - 1)) - a + 1
    number = jnp.where(number > 4, number - 1, number)
    place = jnp.where(t_row == myself, -1, number * CAP + rank)
    slots = len(NEIGHBOURS) * CAP
    chosen = jnp.where(
        jnp.broadcast_to(place, (slots, SMALL))
        == lax.broadcasted_iota(jnp.int32, (slots, SMALL), 0),
        1.0, 0.0,
    )

    def row_index(s):
        return ((s & (BLOCKS - 1)) >> 1) * ROWS + (s >> 5)

    host_index = row_index(h_row)
    marks = 2 * (host_index + 1) + (h_row & 1)
    labels = jnp.sum(chosen * marks.astype(F32), axis=1, keepdims=True)
    lab_send[...] = jnp.broadcast_to(labels, (slots, LANES))

    edges[...] = jnp.zeros_like(edges)
    consts[...] = jnp.zeros_like(consts)
    pl.semaphore_wait(barrier, len(DIRECT))
    for side in range(2):
        first_axial_copy(side).start()
    for k in range(3):
        init_copy(k).start()
    for load in loads[3:7]:
        load.wait()
    for p in range(TILES):
        columns = slice(p * LANES, (p + 1) * LANES)
        speed = cspd[:, columns]
        cs[p, own, :] = speed
        row_send[p:p + 1, :] = speed[ROWS - 1:ROWS]
    row_copy().start()
    for v in range(NV):
        before = None
        for p in range(TILES):
            tile = flow[v, :, p * LANES:(p + 1) * LANES]
            cur[p, v, own, :] = tile
            pack_rows(0, p, v, tile)
            if p > 0:
                shift(p, v, before, tile)
            before = tile
    for side in range(2):
        circ_copy(0, side, 0).start()
    for load in loads[7:10]:
        load.wait()
    frac_twice = jnp.concatenate([frac[...], frac[...]], axis=0).T
    placed = jnp.where((second >> 6) == (h_col & 1), frac_twice, 0.0)
    same_half = (s_col & 1) == (h_col & 1)
    straight = jnp.where(same_half, placed, 0.0)
    crossed = jnp.where(same_half, 0.0, placed)
    is_local = t_col == myself
    floc[0] = jnp.where(is_local, straight, 0.0)
    floc[1] = jnp.where(is_local, crossed, 0.0)
    in_source = (second >> 6) == (s_col & 1)
    fout[0] = jnp.dot(
        chosen, jnp.where(in_source, frac_twice, 0.0), precision=lax.Precision.HIGHEST
    )
    fout[1] = jnp.dot(
        chosen, jnp.where(in_source, 0.0, frac_twice), precision=lax.Precision.HIGHEST
    )
    s_index = row_index(s_col)
    pick = jnp.concatenate(
        [
            jnp.where(s_index == second, 1.0, 0.0),
            jnp.where(s_index == second + LANES, 1.0, 0.0),
        ],
        axis=1,
    ).astype(BF16)
    gloc[...] = pick
    picked_out = jnp.dot(chosen.astype(BF16), pick, preferred_element_type=F32)
    gout[...] = picked_out.astype(BF16)
    picked_end = jnp.concatenate([picked_out[:, :ROWS], picked_out[:, -ROWS:]], axis=1)
    gend[...] = jnp.concatenate([picked_end, picked_end], axis=1).astype(BF16)
    tall = (TILES * ROWS, SMALL)
    tall_rows = lax.broadcasted_iota(jnp.int32, tall, 0)
    wanted = jnp.where(t_row == myself, host_index, -1)
    land = jnp.where(jnp.broadcast_to(wanted, tall) == tall_rows, 1.0, 0.0).astype(BF16)
    a_loc[...] = jnp.concatenate([land, land], axis=1)

    @pl.when(c > 0)
    def _():
        perm[0] = partner_tile[...] >> 7
        perm[1] = partner_tile[...] & (LANES - 1)

    @pl.when(c == 0)
    def _():
        columns = TILES * LANES
        target = partner_row[...]
        upper = jnp.where(
            jnp.broadcast_to(target >> 7, (TILES, columns))
            == lax.broadcasted_iota(jnp.int32, (TILES, columns), 0),
            1.0, 0.0,
        ).astype(BF16)
        tall_lanes = (LANES, columns)
        here = jnp.broadcast_to(target & (LANES - 1), tall_lanes) == lax.broadcasted_iota(
            jnp.int32, tall_lanes, 0
        )
        position = lanes_of(tall_lanes)
        for part, value in enumerate((position >> 7, position & (LANES - 1))):
            lower = jnp.where(here, value.astype(F32), 0.0).astype(BF16)
            perm[part] = lax.dot_general(
                upper, lower, (((1,), (1,)), ((), ())), preferred_element_type=F32
            ).astype(jnp.int32)

    def weigh(p, _):
        gap = jnp.zeros((HALF, HALF), F32)
        both = jnp.concatenate(
            [
                jnp.concatenate([w[2 * p], gap], axis=1),
                jnp.concatenate([gap, w[2 * p + 1]], axis=1),
            ],
            axis=0,
        )
        high, low = split(both.T)
        wts[p, :, 0:LANES] = high
        wts[p, :, LANES:] = low
        return 0

    loads[10].wait()
    lax.fori_loop(0, TILES, weigh, 0)

    def receive_constants():
        for k in range(3):
            init_copy(k).wait()
        consts[0] = jnp.where(a > 0, ini_recv[1], 0.0)
        consts[1] = jnp.where(a < N_AXIAL - 1, ini_recv[0], 0.0)
        consts[2] = jnp.where((a > 0) & (lane == 0), rolled(ini_recv[2], 1), 0.0)
        consts[3] = jnp.where(lane == LANES - 1, aspd[:, (TILES - 1) * LANES:], 0.0)
        row_copy().wait()
        for half in range(2):
            some = slice(half * 8, half * 8 + 8)
            below_row = row_recv[some, :]
            mixed = jnp.zeros_like(below_row)
            for q in range(TILES):
                found = jnp.take_along_axis(
                    jnp.broadcast_to(row_recv[q:q + 1, :], below_row.shape), perm[1, some, :], axis=1
                )
                mixed = jnp.where(perm[0, some, :] == q, found, mixed)
            below_row = jnp.where(c == 0, mixed, below_row)
            for k in range(8):
                cs[half * 8 + k, FIRST - 1:FIRST, :] = below_row[k:k + 1]

    def end_matrix():
        slot_marks = jnp.concatenate([lab_send[...], lab_send[...]], axis=0).T.astype(jnp.int32)
        slot_marks = jnp.concatenate([slot_marks, slot_marks], axis=0)
        index = tall_rows & (ROWS - 1)
        target = jnp.where(
            tall_rows < SMALL, 2 * (index + 1), 2 * ((TILES - 1) * ROWS + index + 1) + 1
        )
        slot_of = (lanes_of(tall) & (slots - 1)) >> 3
        hit = (slot_marks == target) & (slot_of == ((tall_rows >> 4) & 7))
        a_end[...] = jnp.where(hit, 1.0, 0.0).astype(BF16)

    def send_ends(n):
        packed_lane = lanes_of(tall)
        result = jnp.zeros(tall, F32)
        for t in range(BOX // LANES):
            high, low = split(outbox[n, :, t * LANES:(t + 1) * LANES])
            both = jnp.concatenate([high, low], axis=0)
            columns = jnp.dot(a_end[...], both, preferred_element_type=F32)
            for v in range(2 * t, min(2 * t + 2, NV)):
                moved = rolled(columns, v + HALF) if v % 2 else rolled(columns, v) if v else columns
                wanted = (packed_lane == v) | (packed_lane == HALF - 1 + v)
                result = jnp.where(wanted, moved, result)
        for which in range(2):
            for k in range(len(NEIGHBOURS)):
                start = (which * len(NEIGHBOURS) + k) * ROWS
                end_send[which, k] = result[start:start + ROWS]
        for k in FAR_FIRST:
            for which in range(2):
                if end_target(which, k) != (0, 0):
                    end_copy(which, k).start()

    def send_slopes():
        for side in range(2):
            total = jnp.zeros((ROWS, LANES), F32)
            for v in range(NV):
                tile = s32[side * (TILES - 1), var_rows(v), :]
                moved = rolled(tile, v + side) if v + side else tile
                total = jnp.where(lane == v, moved, total)
            slope_send[side] = total
            slope_copy(side).start()

    def receive_ends():
        for side in range(2):
            slope_copy(side).wait()
        sums = []
        for which in range(2):
            total = None
            for k in range(len(NEIGHBOURS)):
                if end_target(which, k) == (0, 0):
                    part = end_send[which, k]
                else:
                    end_copy(which, k).wait()
                    part = end_recv[which, k]
                total = part if total is None else total + part
            sums.append(total)
        slope_right = slope_recv[0] + sums[0]
        slope_left = slope_recv[1] + rolled(sums[1], LANES - HALF + 1)
        return slope_left, slope_right

    def receive_labels():
        for k in range(len(NEIGHBOURS)):
            label_copy(k).wait()
        arrived = lab_recv[...].astype(jnp.int32)
        box_half[...] = jnp.where((lanes_of(arrived.shape) >> 6) == (arrived & 1), 1.0, 0.0)
        places = ((arrived >> 1) - 1).astype(F32)
        label_row = jnp.concatenate([places, places], axis=0).T.astype(jnp.int32)
        land_here = jnp.where(
            jnp.concatenate([label_row, label_row], axis=0) == tall_rows, 1.0, 0.0
        ).astype(BF16)
        a_arr[...] = land_here[2 * ROWS:-2 * ROWS]
        a_edge[0:2 * ROWS, :] = land_here[0:2 * ROWS]
        a_edge[2 * ROWS:, :] = land_here[-2 * ROWS:]

    def fix_edges(n, factor, also_rate):
        if also_rate:
            slope_left, slope_right = receive_ends()
        else:
            for side in range(2):
                axial_copy(n, side).wait()
        left_speed, right_speed = consts[2], consts[3]
        last = (TILES - 1) * LANES
        for v in range(NV):
            vr = var_rows(v)
            if also_rate:
                aligned = rolled(slope_left, LANES - v) if v else slope_left
                from_left = rolled(halo[0, v], 1) + 0.5 * aligned
                from_right = rolled(halo[1, v], LANES - 1) - 0.5 * rolled(
                    slope_right, LANES - 1 - v
                )
            else:
                from_left, from_right = ax_recv[n, 1, v], ax_recv[n, 0, v]
            from_left = jnp.where(a > 0, from_left, 0.0)
            from_right = jnp.where(a < N_AXIAL - 1, from_right, 0.0)
            left_flux = jnp.maximum(left_speed, 0.0) * from_left + jnp.minimum(
                left_speed, 0.0
            ) * edges[0, vr, :]
            right_flux = jnp.maximum(right_speed, 0.0) * edges[1, vr, :] + jnp.minimum(
                right_speed, 0.0
            ) * from_right
            if also_rate:
                out_axial[v, :, 0:LANES] = out_axial[v, :, 0:LANES] - left_flux
                out_axial[v, :, last:] = out_axial[v, :, last:] + right_flux
            else:
                cur[0, v, own, :] = cur[0, v, own, :] + factor * dt[:, 0:LANES] * left_flux
                cur[TILES - 1, v, own, :] = (
                    cur[TILES - 1, v, own, :] - factor * dt[:, last:] * right_flux
                )
                halo[0, v] = from_left - factor * consts[0] * rolled(left_flux, LANES - 1)
                halo[1, v] = from_right + factor * consts[1] * rolled(right_flux, 1)

    def slopes(p):
        left = jnp.concatenate([xs[p], xs[p + 1]], axis=1)
        full = jnp.dot(left, wts[p], preferred_element_type=F32)
        total = full[:STACK, :LANES] + full[:STACK, LANES:] + full[STACK:, :LANES]
        s32[p] = total
        high, low = split(total)
        rows = slice(p * ROWS, (p + 1) * ROWS)
        for v in range(NV):
            shi[rows, var_lanes(v)] = high[var_rows(v)]
            slo[rows, var_lanes(v)] = low[var_rows(v)]
            if p in (0, TILES - 1):
                start = ROWS * (p // (TILES - 1))
                ends[start:start + ROWS, var_lanes(v)] = high[var_rows(v)]
                ends[2 * ROWS + start:3 * ROWS + start, var_lanes(v)] = low[var_rows(v)]

    def gathered(picks, factors, v):
        vl = var_lanes(v)
        picked = jnp.dot(picks[...], shi[:, vl], preferred_element_type=F32) + jnp.dot(
            picks[...], slo[:, vl], preferred_element_type=F32
        )
        return picked * factors[0] + rolled(picked, HALF) * factors[1]

    def scatter(matrix, values, v, tiles):
        added = jnp.dot(matrix[...], values[:, var_lanes(v)], preferred_element_type=F32)
        for i, p in enumerate(tiles):
            s32[p, var_rows(v), :] = s32[p, var_rows(v), :] + added[i * ROWS:(i + 1) * ROWS]

    def late_rows(n):
        for v in range(NV):
            for p in (0, TILES - 1):
                pack_rows(n, p, v, cur[p, v, own, :])

    def is_late(p, v):
        return pair_place(p, v)[0] >= EARLY

    def unpack(n, side, late):
        start = FIRST - 2 if side else FIRST + ROWS
        for p in range(TILES):
            for v in range(NV):
                if is_late(p, v) == late:
                    where, row = pair_place(p, v)
                    cur[p, v, start:start + 2, :] = ci_recv[n, side, where, row:row + 2, :]

    def permute(n, side, late):
        start = FIRST - 2 if side else FIRST + ROWS
        rows = lax.broadcasted_iota(jnp.int32, (8, LANES), 0)

        def one(p):
            tile = jnp.broadcast_to(perm[0, pl.ds(p, 1), :], (8, LANES))
            column = jnp.broadcast_to(perm[1, pl.ds(p, 1), :], (8, LANES))
            slot = jnp.where(
                tile == 0, TILES - 2, jnp.where(tile == TILES - 1, TILES - 1, tile - 1)
            )
            offset = slot - (rows >> 1)
            if late:
                total, last = permuted[0, p], permuted[1, p]
            else:
                total = last = jnp.zeros((8, LANES), F32)
            for q in range(TILES):
                if is_late(q, 0) == late:
                    where, _ = pair_place(q, 0)
                    found = jnp.take_along_axis(ci_recv[n, side, where], column, axis=1)
                    total = jnp.where(tile == q, found, total)
            for g in range(4):
                if (g == 3) == late:
                    where = TILES - 2 + g if g < 3 else ROW_TILES - 1
                    found = jnp.take_along_axis(ci_recv[n, side, where], column, axis=1)
                    last = jnp.where(offset == 4 * g, found, last)
            if not late:
                permuted[0, p], permuted[1, p] = total, last
                return
            last = last + pltpu.roll(last, 4, 0)
            last = last + pltpu.roll(last, 2, 0)
            for v in range(NV - 1):
                cur[p, v, start:start + 2, :] = total[2 * v:2 * v + 2]
            cur[p, NV - 1, start:start + 2, :] = last[0:2]

        def four(i, _):
            for k in range(4):
                one(4 * i + k)
            return 0

        lax.fori_loop(0, TILES // 4, four, 0)

    def halo_rows(n, late):
        for side in range(2):
            circ_copy(n, side, int(late)).wait()

        @pl.when(c > 0)
        def _():
            unpack(n, 1, late)

        @pl.when(c < N_CIRC - 1)
        def _():
            unpack(n, 0, late)

        @pl.when(c == 0)
        def _():
            permute(n, 1, late)

        @pl.when(c == N_CIRC - 1)
        def _():
            permute(n, 0, late)

    def circ_rates(p, _):
        above = cs[p, own, :]
        below = cs[p, FIRST - 1:FIRST + ROWS - 1, :]
        above_pos, above_neg = jnp.maximum(above, 0.0), jnp.minimum(above, 0.0)
        below_pos, below_neg = jnp.maximum(below, 0.0), jnp.minimum(below, 0.0)
        for v in range(NV):
            at = [cur[p, v, FIRST + k:FIRST + k + ROWS, :] for k in (-2, -1, 0, 1, 2)]
            slope_below = 0.25 * (at[2] - at[0])
            slope_here = 0.25 * (at[3] - at[1])
            slope_above = 0.25 * (at[4] - at[2])
            upper = above_pos * (at[2] + slope_here) + above_neg * (at[3] - slope_above)
            lower = below_pos * (at[1] + slope_below) + below_neg * (at[2] - slope_here)
            out_circ[v, :, cells(p)] = upper - lower
        return 0

    def face(p, v, kind):
        half_slope = 0.5 * s32[p, var_rows(v), :]
        here = cur[p, v, own, :]
        return here + half_slope if kind == 0 else here - half_slope

    def flux(p, v, right_lane):
        speed = aspd[:, cells(p)]
        right = rolled(jnp.where(lane == 0, right_lane, face(p, v, 1)), LANES - 1)
        return jnp.maximum(speed, 0.0) * face(p, v, 0) + jnp.minimum(speed, 0.0) * right

    def axial_rate(flux_here, flux_left):
        return flux_here - rolled(jnp.where(lane == LANES - 1, flux_left, flux_here), 1)

    def advance(p, v, flux_here, flux_left, first_stage, factor):
        rate = out_circ[v, :, cells(p)] + axial_rate(flux_here, flux_left)
        here = cur[p, v, own, :]
        start = jnp.where(first_stage, here, base[p, var_rows(v), :])
        base[p, var_rows(v), :] = start
        new = 0.5 * (start + here) - factor * (dt[:, cells(p)] * rate)
        cur[p, v, own, :] = new
        return new

    def conclude(p, v, flux_here, flux_left):
        out_axial[v, :, cells(p)] = axial_rate(flux_here, flux_left)
        out_half[v, :, cells(p)] = 0.5 * (base[p, var_rows(v), :] + cur[p, v, own, :])

    def balance(n, is_last):
        if is_last:
            first_stage, factor, earlier = False, 0.5, 1.0
        else:
            first_stage = lax.rem(n, 2) == 0
            factor = jnp.where(first_stage, 1.0, 0.5).astype(F32)
            earlier = jnp.where(first_stage, 0.5, 1.0).astype(F32)
        end = TILES - 1

        for p in range(1, end):
            slopes(p)
        for rows in (slice(0, ROWS), slice(end * ROWS, TILES * ROWS)):
            shi[rows, :] = jnp.zeros((ROWS, WIDE), BF16)
            slo[rows, :] = jnp.zeros((ROWS, WIDE), BF16)
        for v in range(NV):
            early_box[:, var_lanes(v)] = gathered(gout, fout, v)
        fix_edges(n, earlier, False)
        late_rows(n)
        for side in range(2):
            circ_copy(n, side, 1).start()
        for v in range(NV):
            shift(0, v, halo[0, v], cur[0, v, own, :])
            shift(TILES, v, cur[end, v, own, :], halo[1, v])
        slopes(0)
        slopes(end)
        for v in range(NV):
            picked = jnp.dot(gend[...], ends[:, var_lanes(v)], preferred_element_type=F32)
            sent = early_box[:, var_lanes(v)] + picked * fout[0] + rolled(picked, HALF) * fout[1]
            columns = slice(v // 2 * LANES, v // 2 * LANES + LANES)
            if v % 2:
                outbox[n, :, columns] = jnp.where(box_lane < HALF, previous, sent)
            elif v == NV - 1:
                outbox[n, :, columns] = sent
            previous = sent
        for k in FAR_FIRST:
            box_copy(n, k).start()

        if not is_last:

            @pl.when(n == 0)
            def _():
                for k in FAR_FIRST:
                    label_copy(k).start()

        if is_last:
            send_ends(n)
        else:

            @pl.when(n == 0)
            def _():
                receive_constants()
                end_matrix()

        for v in range(NV):
            high, low = split(gathered(gloc, floc, v))
            c_loc[:SMALL, var_lanes(v)] = high
            c_loc[SMALL:, var_lanes(v)] = low
        for v in range(NV):
            scatter(a_loc, c_loc, v, range(TILES))

        if is_last:
            send_slopes()

        halo_rows(n, False)
        at_seam = (c == 0) | (c == N_CIRC - 1)
        whole = [p for p in range(TILES) if not is_late(p, NV - 1)]

        @pl.when(jnp.logical_not(at_seam))
        def _():
            for p in whole:
                circ_rates(p, 0)

        halo_rows(n, True)

        @pl.when(at_seam)
        def _():
            for p in whole:
                circ_rates(p, 0)

        for p in range(TILES):
            if p not in whole:
                circ_rates(p, 0)

        for k in range(len(NEIGHBOURS)):
            box_copy(n, k).wait()

        if not is_last:

            @pl.when(n == 0)
            def _():
                receive_labels()

        for v in range(NV):
            columns = slice(v // 2 * LANES, v // 2 * LANES + LANES)
            packed = inbox[n, :, columns]
            if v == NV - 1:
                both = packed
            else:
                both = jnp.where((box_lane < HALF) == (v % 2 == 0), packed, rolled(packed, HALF))
            high, low = split(both * box_half[...])
            c_arr[:slots, var_lanes(v)] = high
            c_arr[slots:, var_lanes(v)] = low
        for v in range(NV):
            scatter(a_edge, c_arr, v, (0, 1, end - 1, end))

        for v in range(NV):
            vr = var_rows(v)
            right_face = face(0, v, 1)
            flux_first = flux(0, v, face(1, v, 1))
            left_face = face(end, v, 0)
            flux_before = flux(end - 1, v, face(end, v, 1))
            flux_last = jnp.where(lane == LANES - 1, 0.0, flux(end, v, 0.0))
            edges[0, vr, :] = right_face
            edges[1, vr, :] = left_face
            f_keep[0, vr, :] = flux_first
            f_keep[1, vr, :] = flux_before
            if is_last:
                conclude(0, v, flux_first, 0.0)
                conclude(end, v, flux_last, flux_before)
                continue
            new_first = advance(0, v, flux_first, 0.0, first_stage, factor)
            new_last = advance(end, v, flux_last, flux_before, first_stage, factor)
            ax_send[n + 1, 0, v] = jnp.where(
                lane < HALF, new_first, rolled(right_face, LANES - 1)
            )
            ax_send[n + 1, 1, v] = jnp.where(lane >= HALF, new_last, rolled(left_face, 1))
        if not is_last:
            for side in range(2):
                axial_copy(n + 1, side).start()

        for v in range(NV):
            scatter(a_arr, c_arr, v, range(2, end - 1))

        for v in range(NV):
            before = f_keep[0, var_rows(v), :]
            tile = cur[0, v, own, :]
            for p in range(1, end):
                here = flux(p, v, face(p + 1, v, 1)) if p < end - 1 else f_keep[1, var_rows(v), :]
                if is_last:
                    conclude(p, v, here, before)
                    before = here
                    continue
                new = advance(p, v, here, before, first_stage, factor)
                pack_rows(n + 1, p, v, new)
                shift(p, v, tile, new)
                before, tile = here, new
            if not is_last:
                shift(end, v, tile, cur[end, v, own, :])
        if not is_last:
            for side in range(2):
                circ_copy(n + 1, side, 0).start()

        return 0

    lax.fori_loop(0, BALANCES - 1, lambda n, _: balance(n, False), 0)
    balance(BALANCES - 1, True)
    fix_edges(BALANCES, None, True)


def local(
    flow_state, circ_speed, axial_speed, time_step, lsq_weights,
    partner, merge_owner, merge_source, merge_host, merge_frac,
):
    columns = TILES * LANES
    slots = len(NEIGHBOURS) * CAP
    vmem = pl.BlockSpec(memory_space=pltpu.VMEM)
    hbm = pl.BlockSpec(memory_space=pltpu.HBM)
    dma = pltpu.SemaphoreType.DMA
    scratch = [
        pltpu.VMEM((NV, ROWS, columns), F32),
        pltpu.VMEM((ROWS, columns), F32),
        pltpu.VMEM((ROWS, columns), F32),
        pltpu.VMEM((ROWS, columns), F32),
        pltpu.VMEM((BLOCKS, HALF, 3 * HALF), F32),
        pltpu.VMEM((1, columns), jnp.int32),
        pltpu.VMEM((TILES, LANES), jnp.int32),
        pltpu.VMEM((1, SMALL), jnp.int32),
        pltpu.VMEM((1, SMALL), jnp.int32),
        pltpu.VMEM((1, SMALL), jnp.int32),
        pltpu.VMEM((HALF, SMALL), F32),
        dma((11,)),
        pltpu.VMEM((TILES, NV, 2 * ROWS, LANES), F32),
        pltpu.VMEM((TILES, STACK, LANES), F32),
        pltpu.VMEM((TILES, 2 * ROWS, LANES), F32),
        pltpu.VMEM((TILES + 1, 2 * STACK, LANES), BF16),
        pltpu.VMEM((TILES, 2 * LANES, 2 * LANES), BF16),
        pltpu.VMEM((TILES, STACK, LANES), F32),
        pltpu.VMEM((TILES * ROWS, WIDE), BF16),
        pltpu.VMEM((TILES * ROWS, WIDE), BF16),
        pltpu.VMEM((slots, TILES * ROWS), BF16),
        pltpu.VMEM((slots, 4 * ROWS), BF16),
        pltpu.VMEM((4 * ROWS, WIDE), BF16),
        pltpu.VMEM((SMALL, TILES * ROWS), BF16),
        pltpu.VMEM((2, slots, LANES), F32),
        pltpu.VMEM((2, SMALL, LANES), F32),
        pltpu.VMEM((TILES * ROWS, 2 * SMALL), BF16),
        pltpu.VMEM(((TILES - 4) * ROWS, 2 * slots), BF16),
        pltpu.VMEM((4 * ROWS, 2 * slots), BF16),
        pltpu.VMEM((TILES * ROWS, 2 * slots), BF16),
        pltpu.VMEM((2 * SMALL, WIDE), BF16),
        pltpu.VMEM((2 * slots, WIDE), BF16),
        pltpu.VMEM((2, STACK, LANES), F32),
        pltpu.VMEM((4, ROWS, LANES), F32),
        pltpu.VMEM((2, STACK, LANES), F32),
        pltpu.VMEM((2, NV, ROWS, LANES), F32),
        pltpu.VMEM((2, TILES, LANES), jnp.int32),
        pltpu.VMEM((2, TILES, 8, LANES), F32),
        pltpu.VMEM((BALANCES + 1, 2, NV, ROWS, LANES), F32),
        pltpu.VMEM((BALANCES + 1, 2, NV, ROWS, LANES), F32),
        pltpu.VMEM((3, ROWS, LANES), F32),
        pltpu.VMEM((TILES, LANES), F32),
        pltpu.VMEM((TILES, LANES), F32),
        pltpu.VMEM((BALANCES + 1, 2, ROW_TILES, 8, LANES), F32),
        pltpu.VMEM((BALANCES, 2, ROW_TILES, 8, LANES), F32),
        pltpu.VMEM((slots, LANES), F32),
        pltpu.VMEM((slots, LANES), F32),
        pltpu.VMEM((BALANCES, slots, BOX), F32),
        pltpu.VMEM((BALANCES, slots, BOX), F32),
        pltpu.VMEM((slots, LANES), F32),
        pltpu.VMEM((slots, WIDE), F32),
        pltpu.VMEM((2, len(NEIGHBOURS), ROWS, LANES), F32),
        pltpu.VMEM((2, len(NEIGHBOURS), ROWS, LANES), F32),
        pltpu.VMEM((2, ROWS, LANES), F32),
        pltpu.VMEM((2, ROWS, LANES), F32),
        dma((BALANCES + 1, 2)), dma((BALANCES + 1, 2)),
        dma((3,)), dma((3,)),
        dma((1,)), dma((1,)),
        dma((BALANCES, 2, 2)), dma((BALANCES, 2, 2)),
        dma((len(NEIGHBOURS),)), dma((len(NEIGHBOURS),)),
        dma((BALANCES, len(NEIGHBOURS))), dma((BALANCES, len(NEIGHBOURS))),
        dma((2, len(NEIGHBOURS))), dma((2, len(NEIGHBOURS))), dma((2,)), dma((2,)),
    ]
    half, circ_rate, axial_rate = pl.pallas_call(
        kernel,
        out_shape=(pltpu.VMEM((NV, ROWS, columns), F32),) * 3,
        in_specs=[hbm] * 11,
        out_specs=(vmem, vmem, vmem),
        scratch_shapes=scratch,
        compiler_params=pltpu.CompilerParams(
            collective_id=0, has_side_effects=True, vmem_limit_bytes=56 * 1024 * 1024
        ),
    )(
        flow_state, circ_speed, axial_speed, time_step, lsq_weights,
        partner.reshape(1, columns), partner.reshape(TILES, LANES),
        merge_owner.reshape(1, SMALL), merge_source.reshape(1, SMALL),
        merge_host.reshape(1, SMALL), merge_frac.T,
    )
    last_rate = circ_rate + axial_rate
    return half - 0.5 * (time_step * last_rate), last_rate


def solution(mesh):
    in_specs = (
        P(None, "circ", "axial"),
        P("circ", "axial"),
        P("circ", "axial"),
        P("circ", "axial"),
        P("axial", None, None),
        P("axial"),
        P(("circ", "axial"), None),
        P(("circ", "axial")),
        P(("circ", "axial")),
        P(("circ", "axial"), None),
    )
    out_specs = (P(None, "circ", "axial"), P(None, "circ", "axial"))
    return jax.shard_map(local, mesh=mesh, in_specs=in_specs, out_specs=out_specs, check_vma=False)
```

```python
import jax
import jax.numpy as jnp
from jax import lax
from jax.experimental import pallas as pl
from jax.experimental.pallas import tpu as pltpu
from jax.sharding import PartitionSpec as P

STEPS = 2
BALANCES = 2 * STEPS
CAP = 8
NV = 5
ROWS = 16
LANES = 128
TILES = 16
HALF = 64
SMALL = 128
BLOCKS = 32
N_CIRC = 16
N_AXIAL = 8
STACK = NV * ROWS
WIDE = NV * LANES
BOX = 3 * LANES
ROW_TILES = 20
EARLY = 17
FIRST = 8
MESH = pl.DeviceIdType.MESH
F32 = jnp.float32
BF16 = jnp.bfloat16
NEIGHBOURS = [(dc, da) for dc in (-1, 0, 1) for da in (-1, 0, 1) if (dc, da) != (0, 0)]
DIRECT = [(-1, 0), (1, 0), (0, -1), (0, 1)]
FAR_FIRST = (0, 2, 5, 7, 1, 6, 3, 4)


def split(x):
    high = x.astype(BF16)
    return high, (x - high.astype(F32)).astype(BF16)


def lanes_of(shape):
    return lax.broadcasted_iota(jnp.int32, shape, len(shape) - 1)


def rolled(x, steps):
    return pltpu.roll(x, steps, x.ndim - 1)


def var_rows(v):
    return slice(v * ROWS, (v + 1) * ROWS)


def var_lanes(v):
    return slice(v * LANES, (v + 1) * LANES)


def cells(p):
    return slice(p * LANES, (p + 1) * LANES)


def kernel(
    flow_hbm, cspd_hbm, aspd_hbm, dt_hbm, w_hbm, prow_hbm, ptile_hbm, owner_hbm, source_hbm,
    host_hbm, frac_hbm,
    out_half, out_circ, out_axial,
    flow, cspd, aspd, dt, w, partner_row, partner_tile, owner, source, host, frac, load_sem,
    cur, base, cs, xs, wts, s32, shi, slo, gout, gend, ends, gloc, fout, floc, a_loc, a_arr, a_edge, a_end, c_loc, c_arr,
    edges, consts, f_keep, halo, perm, permuted,
    ax_send, ax_recv, ini_recv, row_send, row_recv, ci_send, ci_recv, lab_send, lab_recv, outbox, inbox, box_half, early_box,
    end_send, end_recv, slope_send, slope_recv,
    ax_ss, ax_rs, ini_ss, ini_rs, row_ss, row_rs, ci_ss, ci_rs, lab_ss, lab_rs, box_ss, box_rs,
    end_ss, end_rs, slope_ss, slope_rs,
):
    c = lax.axis_index("circ")
    a = lax.axis_index("axial")

    def peer(dc, da):
        return (lax.rem(c + dc + N_CIRC, N_CIRC), lax.rem(a + da + N_AXIAL, N_AXIAL))

    def remote(src, dst, send, recv, dc, da):
        return pltpu.make_async_remote_copy(
            src_ref=src, dst_ref=dst, send_sem=send, recv_sem=recv,
            device_id=peer(dc, da), device_id_type=MESH,
        )

    def axial_copy(n, side):
        return remote(
            ax_send.at[n, side], ax_recv.at[n, side], ax_ss.at[n, side], ax_rs.at[n, side],
            0, 2 * side - 1,
        )

    head, tail = pl.ds(0, LANES), pl.ds((TILES - 1) * LANES, LANES)

    def first_axial_copy(side):
        return remote(
            flow_hbm.at[:, :, tail if side else head], ax_recv.at[0, side],
            ax_ss.at[0, side], ax_rs.at[0, side], 0, 2 * side - 1,
        )

    def init_copy(k):
        source_of = (dt_hbm.at[:, head], dt_hbm.at[:, tail], aspd_hbm.at[:, tail])
        return remote(
            source_of[k], ini_recv.at[k], ini_ss.at[k], ini_rs.at[k], 0, 1 if k else -1
        )

    def circ_copy(n, side, late):
        part = pl.ds(EARLY, ROW_TILES - EARLY) if late else pl.ds(0, EARLY)
        return remote(
            ci_send.at[n, side, part], ci_recv.at[n, side, part],
            ci_ss.at[n, side, late], ci_rs.at[n, side, late], 2 * side - 1, 0,
        )

    def row_copy():
        return remote(row_send, row_recv, row_ss.at[0], row_rs.at[0], 1, 0)

    def label_copy(k):
        dc, da = NEIGHBOURS[k]
        rows = pl.ds(k * CAP, CAP)
        return remote(lab_send.at[rows], lab_recv.at[rows], lab_ss.at[k], lab_rs.at[k], dc, da)

    def box_copy(n, k):
        dc, da = NEIGHBOURS[k]
        rows = pl.ds(k * CAP, CAP)
        return remote(
            outbox.at[n, rows], inbox.at[n, rows], box_ss.at[n, k], box_rs.at[n, k], dc, da
        )

    def end_target(which, k):
        dc, da = NEIGHBOURS[k]
        return dc, da + (1 if which else -1)

    def end_copy(which, k):
        return remote(
            end_send.at[which, k], end_recv.at[which, k], end_ss.at[which, k],
            end_rs.at[which, k], *end_target(which, k),
        )

    def slope_copy(side):
        return remote(
            slope_send.at[side], slope_recv.at[side], slope_ss.at[side], slope_rs.at[side],
            0, 2 * side - 1,
        )

    own = slice(FIRST, FIRST + ROWS)
    lane = lanes_of((ROWS, LANES))
    box_lane = lanes_of((len(NEIGHBOURS) * CAP, LANES))

    loads = [
        pltpu.make_async_copy(src, dst, load_sem.at[i])
        for i, (src, dst) in enumerate(
            (
                (owner_hbm, owner), (source_hbm, source), (host_hbm, host), (flow_hbm, flow),
                (dt_hbm, dt), (aspd_hbm, aspd), (cspd_hbm, cspd), (frac_hbm, frac),
                (prow_hbm, partner_row), (ptile_hbm, partner_tile), (w_hbm, w),
            )
        )
    ]
    for load in loads:
        load.start()

    barrier = pltpu.get_barrier_semaphore()
    for dc, da in DIRECT:
        pl.semaphore_signal(barrier, inc=1, device_id=peer(dc, da), device_id_type=MESH)

    def pair_place(p, v):
        slot = p - 1 if 0 < p < TILES - 1 else TILES - 2 + p // (TILES - 1)
        if v < NV - 1:
            return (slot if slot < TILES - 2 else slot + 3), 2 * v
        group = slot // 4
        return (TILES - 2 + group if group < 3 else ROW_TILES - 1), 2 * (slot % 4)

    def pack_rows(n, p, v, tile):
        where, row = pair_place(p, v)
        ci_send[n, 0, where, row:row + 2, :] = tile[0:2]
        ci_send[n, 1, where, row:row + 2, :] = tile[ROWS - 2:ROWS]

    def shift(q, v, left_tile, right_tile):
        moved = rolled(jnp.where(lane >= HALF, left_tile, right_tile), HALF)
        high, low = split(moved)
        xs[q, var_rows(v), :] = high
        xs[q, STACK + v * ROWS:STACK + (v + 1) * ROWS, :] = low

    for load in loads[:3]:
        load.wait()
    square = (SMALL, SMALL)
    t_row = owner[...]
    s_row = source[...]
    h_row = host[...]

    def as_columns(row):
        return jnp.broadcast_to(row.astype(F32), square).T.astype(jnp.int32)

    t_col, s_col, h_col = as_columns(t_row), as_columns(s_row), as_columns(h_row)
    myself = c * N_AXIAL + a
    first = lax.broadcasted_iota(jnp.int32, square, 0)
    second = lax.broadcasted_iota(jnp.int32, square, 1)
    shares = jnp.where((jnp.broadcast_to(t_row, square) == t_col) & (first < second), 1.0, 0.0)
    rank = jnp.sum(shares, axis=0, keepdims=True).astype(jnp.int32)
    circ_off = ((t_row >> 3) - c + 1 + N_CIRC) & (N_CIRC - 1)
    number = circ_off * 3 + (t_row & (N_AXIAL - 1)) - a + 1
    number = jnp.where(number > 4, number - 1, number)
    place = jnp.where(t_row == myself, -1, number * CAP + rank)
    slots = len(NEIGHBOURS) * CAP
    chosen = jnp.where(
        jnp.broadcast_to(place, (slots, SMALL))
        == lax.broadcasted_iota(jnp.int32, (slots, SMALL), 0),
        1.0, 0.0,
    )

    def row_index(s):
        return ((s & (BLOCKS - 1)) >> 1) * ROWS + (s >> 5)

    host_index = row_index(h_row)
    marks = 2 * (host_index + 1) + (h_row & 1)
    labels = jnp.sum(chosen * marks.astype(F32), axis=1, keepdims=True)
    lab_send[...] = jnp.broadcast_to(labels, (slots, LANES))

    edges[...] = jnp.zeros_like(edges)
    consts[...] = jnp.zeros_like(consts)
    pl.semaphore_wait(barrier, len(DIRECT))
    for side in range(2):
        first_axial_copy(side).start()
    for k in range(3):
        init_copy(k).start()
    for load in loads[3:7]:
        load.wait()
    for p in range(TILES):
        columns = slice(p * LANES, (p + 1) * LANES)
        speed = cspd[:, columns]
        cs[p, own, :] = speed
        row_send[p:p + 1, :] = speed[ROWS - 1:ROWS]
    row_copy().start()
    for v in range(NV):
        before = None
        for p in range(TILES):
            tile = flow[v, :, p * LANES:(p + 1) * LANES]
            cur[p, v, own, :] = tile
            pack_rows(0, p, v, tile)
            if p > 0:
                shift(p, v, before, tile)
            before = tile
    for side in range(2):
        circ_copy(0, side, 0).start()
    for load in loads[7:10]:
        load.wait()
    frac_twice = jnp.concatenate([frac[...], frac[...]], axis=0).T
    placed = jnp.where((second >> 6) == (h_col & 1), frac_twice, 0.0)
    same_half = (s_col & 1) == (h_col & 1)
    straight = jnp.where(same_half, placed, 0.0)
    crossed = jnp.where(same_half, 0.0, placed)
    is_local = t_col == myself
    floc[0] = jnp.where(is_local, straight, 0.0)
    floc[1] = jnp.where(is_local, crossed, 0.0)
    in_source = (second >> 6) == (s_col & 1)
    fout[0] = jnp.dot(
        chosen, jnp.where(in_source, frac_twice, 0.0), precision=lax.Precision.HIGHEST
    )
    fout[1] = jnp.dot(
        chosen, jnp.where(in_source, 0.0, frac_twice), precision=lax.Precision.HIGHEST
    )
    s_index = row_index(s_col)
    pick = jnp.concatenate(
        [
            jnp.where(s_index == second, 1.0, 0.0),
            jnp.where(s_index == second + LANES, 1.0, 0.0),
        ],
        axis=1,
    ).astype(BF16)
    gloc[...] = pick
    picked_out = jnp.dot(chosen.astype(BF16), pick, preferred_element_type=F32)
    gout[...] = picked_out.astype(BF16)
    picked_end = jnp.concatenate([picked_out[:, :ROWS], picked_out[:, -ROWS:]], axis=1)
    gend[...] = jnp.concatenate([picked_end, picked_end], axis=1).astype(BF16)
    tall = (TILES * ROWS, SMALL)
    tall_rows = lax.broadcasted_iota(jnp.int32, tall, 0)
    wanted = jnp.where(t_row == myself, host_index, -1)
    land = jnp.where(jnp.broadcast_to(wanted, tall) == tall_rows, 1.0, 0.0).astype(BF16)
    a_loc[...] = jnp.concatenate([land, land], axis=1)

    @pl.when(c > 0)
    def _():
        perm[0] = partner_tile[...] >> 7
        perm[1] = partner_tile[...] & (LANES - 1)

    @pl.when(c == 0)
    def _():
        columns = TILES * LANES
        target = partner_row[...]
        upper = jnp.where(
            jnp.broadcast_to(target >> 7, (TILES, columns))
            == lax.broadcasted_iota(jnp.int32, (TILES, columns), 0),
            1.0, 0.0,
        ).astype(BF16)
        tall_lanes = (LANES, columns)
        here = jnp.broadcast_to(target & (LANES - 1), tall_lanes) == lax.broadcasted_iota(
            jnp.int32, tall_lanes, 0
        )
        position = lanes_of(tall_lanes)
        for part, value in enumerate((position >> 7, position & (LANES - 1))):
            lower = jnp.where(here, value.astype(F32), 0.0).astype(BF16)
            perm[part] = lax.dot_general(
                upper, lower, (((1,), (1,)), ((), ())), preferred_element_type=F32
            ).astype(jnp.int32)

    def weigh(p, _):
        gap = jnp.zeros((HALF, HALF), F32)
        both = jnp.concatenate(
            [
                jnp.concatenate([w[2 * p], gap], axis=1),
                jnp.concatenate([gap, w[2 * p + 1]], axis=1),
            ],
            axis=0,
        )
        high, low = split(both.T)
        wts[p, :, 0:LANES] = high
        wts[p, :, LANES:] = low
        return 0

    loads[10].wait()
    lax.fori_loop(0, TILES, weigh, 0)

    def receive_constants():
        for k in range(3):
            init_copy(k).wait()
        consts[0] = jnp.where(a > 0, ini_recv[1], 0.0)
        consts[1] = jnp.where(a < N_AXIAL - 1, ini_recv[0], 0.0)
        consts[2] = jnp.where((a > 0) & (lane == 0), rolled(ini_recv[2], 1), 0.0)
        consts[3] = jnp.where(lane == LANES - 1, aspd[:, (TILES - 1) * LANES:], 0.0)
        row_copy().wait()
        for half in range(2):
            some = slice(half * 8, half * 8 + 8)
            below_row = row_recv[some, :]
            mixed = jnp.zeros_like(below_row)
            for q in range(TILES):
                found = jnp.take_along_axis(
                    jnp.broadcast_to(row_recv[q:q + 1, :], below_row.shape), perm[1, some, :], axis=1
                )
                mixed = jnp.where(perm[0, some, :] == q, found, mixed)
            below_row = jnp.where(c == 0, mixed, below_row)
            for k in range(8):
                cs[half * 8 + k, FIRST - 1:FIRST, :] = below_row[k:k + 1]

    def end_matrix():
        slot_marks = jnp.concatenate([lab_send[...], lab_send[...]], axis=0).T.astype(jnp.int32)
        slot_marks = jnp.concatenate([slot_marks, slot_marks], axis=0)
        index = tall_rows & (ROWS - 1)
        target = jnp.where(
            tall_rows < SMALL, 2 * (index + 1), 2 * ((TILES - 1) * ROWS + index + 1) + 1
        )
        slot_of = (lanes_of(tall) & (slots - 1)) >> 3
        hit = (slot_marks == target) & (slot_of == ((tall_rows >> 4) & 7))
        a_end[...] = jnp.where(hit, 1.0, 0.0).astype(BF16)

    def send_ends(n):
        packed_lane = lanes_of(tall)
        result = jnp.zeros(tall, F32)
        for t in range(BOX // LANES):
            high, low = split(outbox[n, :, t * LANES:(t + 1) * LANES])
            both = jnp.concatenate([high, low], axis=0)
            columns = jnp.dot(a_end[...], both, preferred_element_type=F32)
            for v in range(2 * t, min(2 * t + 2, NV)):
                moved = rolled(columns, v + HALF) if v % 2 else rolled(columns, v) if v else columns
                wanted = (packed_lane == v) | (packed_lane == HALF - 1 + v)
                result = jnp.where(wanted, moved, result)
        for which in range(2):
            for k in range(len(NEIGHBOURS)):
                start = (which * len(NEIGHBOURS) + k) * ROWS
                end_send[which, k] = result[start:start + ROWS]
        for k in FAR_FIRST:
            for which in range(2):
                if end_target(which, k) != (0, 0):
                    end_copy(which, k).start()

    def send_slopes():
        for side in range(2):
            total = jnp.zeros((ROWS, LANES), F32)
            for v in range(NV):
                tile = s32[side * (TILES - 1), var_rows(v), :]
                moved = rolled(tile, v + side) if v + side else tile
                total = jnp.where(lane == v, moved, total)
            slope_send[side] = total
            slope_copy(side).start()

    def receive_ends():
        for side in range(2):
            slope_copy(side).wait()
        sums = []
        for which in range(2):
            total = None
            for k in range(len(NEIGHBOURS)):
                if end_target(which, k) == (0, 0):
                    part = end_send[which, k]
                else:
                    end_copy(which, k).wait()
                    part = end_recv[which, k]
                total = part if total is None else total + part
            sums.append(total)
        slope_right = slope_recv[0] + sums[0]
        slope_left = slope_recv[1] + rolled(sums[1], LANES - HALF + 1)
        return slope_left, slope_right

    def receive_labels():
        for k in range(len(NEIGHBOURS)):
            label_copy(k).wait()
        arrived = lab_recv[...].astype(jnp.int32)
        box_half[...] = jnp.where((lanes_of(arrived.shape) >> 6) == (arrived & 1), 1.0, 0.0)
        places = ((arrived >> 1) - 1).astype(F32)
        label_row = jnp.concatenate([places, places], axis=0).T.astype(jnp.int32)
        land_here = jnp.where(
            jnp.concatenate([label_row, label_row], axis=0) == tall_rows, 1.0, 0.0
        ).astype(BF16)
        a_arr[...] = land_here[2 * ROWS:-2 * ROWS]
        a_edge[0:2 * ROWS, :] = land_here[0:2 * ROWS]
        a_edge[2 * ROWS:, :] = land_here[-2 * ROWS:]

    def fix_edges(n, factor, also_rate):
        if also_rate:
            slope_left, slope_right = receive_ends()
        else:
            for side in range(2):
                axial_copy(n, side).wait()
        left_speed, right_speed = consts[2], consts[3]
        last = (TILES - 1) * LANES
        for v in range(NV):
            vr = var_rows(v)
            if also_rate:
                aligned = rolled(slope_left, LANES - v) if v else slope_left
                from_left = rolled(halo[0, v], 1) + 0.5 * aligned
                from_right = rolled(halo[1, v], LANES - 1) - 0.5 * rolled(
                    slope_right, LANES - 1 - v
                )
            else:
                from_left, from_right = ax_recv[n, 1, v], ax_recv[n, 0, v]
            from_left = jnp.where(a > 0, from_left, 0.0)
            from_right = jnp.where(a < N_AXIAL - 1, from_right, 0.0)
            left_flux = jnp.maximum(left_speed, 0.0) * from_left + jnp.minimum(
                left_speed, 0.0
            ) * edges[0, vr, :]
            right_flux = jnp.maximum(right_speed, 0.0) * edges[1, vr, :] + jnp.minimum(
                right_speed, 0.0
            ) * from_right
            if also_rate:
                out_axial[v, :, 0:LANES] = out_axial[v, :, 0:LANES] - left_flux
                out_axial[v, :, last:] = out_axial[v, :, last:] + right_flux
            else:
                cur[0, v, own, :] = cur[0, v, own, :] + factor * dt[:, 0:LANES] * left_flux
                cur[TILES - 1, v, own, :] = (
                    cur[TILES - 1, v, own, :] - factor * dt[:, last:] * right_flux
                )
                halo[0, v] = from_left - factor * consts[0] * rolled(left_flux, LANES - 1)
                halo[1, v] = from_right + factor * consts[1] * rolled(right_flux, 1)

    def slopes(p):
        left = jnp.concatenate([xs[p], xs[p + 1]], axis=1)
        full = jnp.dot(left, wts[p], preferred_element_type=F32)
        total = full[:STACK, :LANES] + full[:STACK, LANES:] + full[STACK:, :LANES]
        s32[p] = total
        high, low = split(total)
        rows = slice(p * ROWS, (p + 1) * ROWS)
        for v in range(NV):
            shi[rows, var_lanes(v)] = high[var_rows(v)]
            slo[rows, var_lanes(v)] = low[var_rows(v)]
            if p in (0, TILES - 1):
                start = ROWS * (p // (TILES - 1))
                ends[start:start + ROWS, var_lanes(v)] = high[var_rows(v)]
                ends[2 * ROWS + start:3 * ROWS + start, var_lanes(v)] = low[var_rows(v)]

    def gathered(picks, factors, v):
        vl = var_lanes(v)
        picked = jnp.dot(picks[...], shi[:, vl], preferred_element_type=F32) + jnp.dot(
            picks[...], slo[:, vl], preferred_element_type=F32
        )
        return picked * factors[0] + rolled(picked, HALF) * factors[1]

    def scatter(matrix, values, v, tiles):
        added = jnp.dot(matrix[...], values[:, var_lanes(v)], preferred_element_type=F32)
        for i, p in enumerate(tiles):
            s32[p, var_rows(v), :] = s32[p, var_rows(v), :] + added[i * ROWS:(i + 1) * ROWS]

    def late_rows(n):
        for v in range(NV):
            for p in (0, TILES - 1):
                pack_rows(n, p, v, cur[p, v, own, :])

    def is_late(p, v):
        return pair_place(p, v)[0] >= EARLY

    def unpack(n, side, late):
        start = FIRST - 2 if side else FIRST + ROWS
        for p in range(TILES):
            for v in range(NV):
                if is_late(p, v) == late:
                    where, row = pair_place(p, v)
                    cur[p, v, start:start + 2, :] = ci_recv[n, side, where, row:row + 2, :]

    def permute(n, side, late):
        start = FIRST - 2 if side else FIRST + ROWS
        rows = lax.broadcasted_iota(jnp.int32, (8, LANES), 0)

        def one(p):
            tile = jnp.broadcast_to(perm[0, pl.ds(p, 1), :], (8, LANES))
            column = jnp.broadcast_to(perm[1, pl.ds(p, 1), :], (8, LANES))
            slot = jnp.where(
                tile == 0, TILES - 2, jnp.where(tile == TILES - 1, TILES - 1, tile - 1)
            )
            offset = slot - (rows >> 1)
            if late:
                total, last = permuted[0, p], permuted[1, p]
            else:
                total = last = jnp.zeros((8, LANES), F32)
            for q in range(TILES):
                if is_late(q, 0) == late:
                    where, _ = pair_place(q, 0)
                    found = jnp.take_along_axis(ci_recv[n, side, where], column, axis=1)
                    total = jnp.where(tile == q, found, total)
            for g in range(4):
                if (g == 3) == late:
                    where = TILES - 2 + g if g < 3 else ROW_TILES - 1
                    found = jnp.take_along_axis(ci_recv[n, side, where], column, axis=1)
                    last = jnp.where(offset == 4 * g, found, last)
            if not late:
                permuted[0, p], permuted[1, p] = total, last
                return
            last = last + pltpu.roll(last, 4, 0)
            last = last + pltpu.roll(last, 2, 0)
            for v in range(NV - 1):
                cur[p, v, start:start + 2, :] = total[2 * v:2 * v + 2]
            cur[p, NV - 1, start:start + 2, :] = last[0:2]

        def four(i, _):
            for k in range(4):
                one(4 * i + k)
            return 0

        lax.fori_loop(0, TILES // 4, four, 0)

    def halo_rows(n, late):
        for side in range(2):
            circ_copy(n, side, int(late)).wait()

        @pl.when(c > 0)
        def _():
            unpack(n, 1, late)

        @pl.when(c < N_CIRC - 1)
        def _():
            unpack(n, 0, late)

        @pl.when(c == 0)
        def _():
            permute(n, 1, late)

        @pl.when(c == N_CIRC - 1)
        def _():
            permute(n, 0, late)

    def circ_rates(p, start=0, count=ROWS):
        at_row = FIRST + start
        above = cs[p, at_row:at_row + count, :]
        below = cs[p, at_row - 1:at_row - 1 + count, :]
        above_pos, above_neg = jnp.maximum(above, 0.0), jnp.minimum(above, 0.0)
        below_pos, below_neg = jnp.maximum(below, 0.0), jnp.minimum(below, 0.0)
        for v in range(NV):
            at = [cur[p, v, at_row + k:at_row + k + count, :] for k in (-2, -1, 0, 1, 2)]
            slope_below = 0.25 * (at[2] - at[0])
            slope_here = 0.25 * (at[3] - at[1])
            slope_above = 0.25 * (at[4] - at[2])
            upper = above_pos * (at[2] + slope_here) + above_neg * (at[3] - slope_above)
            lower = below_pos * (at[1] + slope_below) + below_neg * (at[2] - slope_here)
            out_circ[v, start:start + count, cells(p)] = upper - lower

    def face(p, v, kind):
        half_slope = 0.5 * s32[p, var_rows(v), :]
        here = cur[p, v, own, :]
        return here + half_slope if kind == 0 else here - half_slope

    def flux(p, v, right_lane):
        speed = aspd[:, cells(p)]
        right = rolled(jnp.where(lane == 0, right_lane, face(p, v, 1)), LANES - 1)
        return jnp.maximum(speed, 0.0) * face(p, v, 0) + jnp.minimum(speed, 0.0) * right

    def axial_rate(flux_here, flux_left):
        return flux_here - rolled(jnp.where(lane == LANES - 1, flux_left, flux_here), 1)

    def advance(p, v, flux_here, flux_left, first_stage, factor):
        rate = out_circ[v, :, cells(p)] + axial_rate(flux_here, flux_left)
        here = cur[p, v, own, :]
        start = jnp.where(first_stage, here, base[p, var_rows(v), :])
        base[p, var_rows(v), :] = start
        new = 0.5 * (start + here) - factor * (dt[:, cells(p)] * rate)
        cur[p, v, own, :] = new
        return new

    def conclude(p, v, flux_here, flux_left):
        out_axial[v, :, cells(p)] = axial_rate(flux_here, flux_left)
        out_half[v, :, cells(p)] = 0.5 * (base[p, var_rows(v), :] + cur[p, v, own, :])

    def balance(n, is_last):
        if is_last:
            first_stage, factor, earlier = False, 0.5, 1.0
        else:
            first_stage = lax.rem(n, 2) == 0
            factor = jnp.where(first_stage, 1.0, 0.5).astype(F32)
            earlier = jnp.where(first_stage, 0.5, 1.0).astype(F32)
        end = TILES - 1

        for p in range(1, end):
            slopes(p)
        for rows in (slice(0, ROWS), slice(end * ROWS, TILES * ROWS)):
            shi[rows, :] = jnp.zeros((ROWS, WIDE), BF16)
            slo[rows, :] = jnp.zeros((ROWS, WIDE), BF16)
        for v in range(NV):
            early_box[:, var_lanes(v)] = gathered(gout, fout, v)
        fix_edges(n, earlier, False)
        late_rows(n)
        for side in range(2):
            circ_copy(n, side, 1).start()
        for v in range(NV):
            shift(0, v, halo[0, v], cur[0, v, own, :])
            shift(TILES, v, cur[end, v, own, :], halo[1, v])
        slopes(0)
        slopes(end)
        for v in range(NV):
            picked = jnp.dot(gend[...], ends[:, var_lanes(v)], preferred_element_type=F32)
            sent = early_box[:, var_lanes(v)] + picked * fout[0] + rolled(picked, HALF) * fout[1]
            columns = slice(v // 2 * LANES, v // 2 * LANES + LANES)
            if v % 2:
                outbox[n, :, columns] = jnp.where(box_lane < HALF, previous, sent)
            elif v == NV - 1:
                outbox[n, :, columns] = sent
            previous = sent
        for k in FAR_FIRST:
            box_copy(n, k).start()

        if not is_last:

            @pl.when(n == 0)
            def _():
                for k in FAR_FIRST:
                    label_copy(k).start()

        if is_last:
            send_ends(n)
        else:

            @pl.when(n == 0)
            def _():
                receive_constants()
                end_matrix()

        for v in range(NV):
            high, low = split(gathered(gloc, floc, v))
            c_loc[:SMALL, var_lanes(v)] = high
            c_loc[SMALL:, var_lanes(v)] = low
        for v in range(NV):
            scatter(a_loc, c_loc, v, range(TILES))

        if is_last:
            send_slopes()

        halo_rows(n, False)
        whole = [p for p in range(TILES) if not is_late(p, NV - 1)]
        for p in whole:
            circ_rates(p)
        halo_rows(n, True)
        for p in range(TILES):
            if p not in whole:
                circ_rates(p)

        @pl.when(c == 0)
        def _():
            for p in whole:
                circ_rates(p, 0, 8)

        @pl.when(c == N_CIRC - 1)
        def _():
            for p in whole:
                circ_rates(p, 8, 8)

        for k in reversed(FAR_FIRST):
            box_copy(n, k).wait()

        if not is_last:

            @pl.when(n == 0)
            def _():
                receive_labels()

        for v in range(NV):
            columns = slice(v // 2 * LANES, v // 2 * LANES + LANES)
            packed = inbox[n, :, columns]
            if v == NV - 1:
                both = packed
            else:
                both = jnp.where((box_lane < HALF) == (v % 2 == 0), packed, rolled(packed, HALF))
            high, low = split(both * box_half[...])
            c_arr[:slots, var_lanes(v)] = high
            c_arr[slots:, var_lanes(v)] = low
        for v in range(NV):
            scatter(a_edge, c_arr, v, (0, 1, end - 1, end))

        for v in range(NV):
            vr = var_rows(v)
            right_face = face(0, v, 1)
            flux_first = flux(0, v, face(1, v, 1))
            left_face = face(end, v, 0)
            flux_before = flux(end - 1, v, face(end, v, 1))
            flux_last = jnp.where(lane == LANES - 1, 0.0, flux(end, v, 0.0))
            edges[0, vr, :] = right_face
            edges[1, vr, :] = left_face
            f_keep[0, vr, :] = flux_first
            f_keep[1, vr, :] = flux_before
            if is_last:
                conclude(0, v, flux_first, 0.0)
                conclude(end, v, flux_last, flux_before)
                continue
            new_first = advance(0, v, flux_first, 0.0, first_stage, factor)
            new_last = advance(end, v, flux_last, flux_before, first_stage, factor)
            ax_send[n + 1, 0, v] = jnp.where(
                lane < HALF, new_first, rolled(right_face, LANES - 1)
            )
            ax_send[n + 1, 1, v] = jnp.where(lane >= HALF, new_last, rolled(left_face, 1))
        if not is_last:
            for side in range(2):
                axial_copy(n + 1, side).start()

        for v in range(NV):
            scatter(a_arr, c_arr, v, range(2, end - 1))

        for v in range(NV):
            before = f_keep[0, var_rows(v), :]
            tile = cur[0, v, own, :]
            for p in range(1, end):
                here = flux(p, v, face(p + 1, v, 1)) if p < end - 1 else f_keep[1, var_rows(v), :]
                if is_last:
                    conclude(p, v, here, before)
                    before = here
                    continue
                new = advance(p, v, here, before, first_stage, factor)
                pack_rows(n + 1, p, v, new)
                shift(p, v, tile, new)
                before, tile = here, new
            if not is_last:
                shift(end, v, tile, cur[end, v, own, :])
        if not is_last:
            for side in range(2):
                circ_copy(n + 1, side, 0).start()

        return 0

    lax.fori_loop(0, BALANCES - 1, lambda n, _: balance(n, False), 0)
    balance(BALANCES - 1, True)
    fix_edges(BALANCES, None, True)


def local(
    flow_state, circ_speed, axial_speed, time_step, lsq_weights,
    partner, merge_owner, merge_source, merge_host, merge_frac,
):
    columns = TILES * LANES
    slots = len(NEIGHBOURS) * CAP
    vmem = pl.BlockSpec(memory_space=pltpu.VMEM)
    hbm = pl.BlockSpec(memory_space=pltpu.HBM)
    dma = pltpu.SemaphoreType.DMA
    scratch = [
        pltpu.VMEM((NV, ROWS, columns), F32),
        pltpu.VMEM((ROWS, columns), F32),
        pltpu.VMEM((ROWS, columns), F32),
        pltpu.VMEM((ROWS, columns), F32),
        pltpu.VMEM((BLOCKS, HALF, 3 * HALF), F32),
        pltpu.VMEM((1, columns), jnp.int32),
        pltpu.VMEM((TILES, LANES), jnp.int32),
        pltpu.VMEM((1, SMALL), jnp.int32),
        pltpu.VMEM((1, SMALL), jnp.int32),
        pltpu.VMEM((1, SMALL), jnp.int32),
        pltpu.VMEM((HALF, SMALL), F32),
        dma((11,)),
        pltpu.VMEM((TILES, NV, 2 * ROWS, LANES), F32),
        pltpu.VMEM((TILES, STACK, LANES), F32),
        pltpu.VMEM((TILES, 2 * ROWS, LANES), F32),
        pltpu.VMEM((TILES + 1, 2 * STACK, LANES), BF16),
        pltpu.VMEM((TILES, 2 * LANES, 2 * LANES), BF16),
        pltpu.VMEM((TILES, STACK, LANES), F32),
        pltpu.VMEM((TILES * ROWS, WIDE), BF16),
        pltpu.VMEM((TILES * ROWS, WIDE), BF16),
        pltpu.VMEM((slots, TILES * ROWS), BF16),
        pltpu.VMEM((slots, 4 * ROWS), BF16),
        pltpu.VMEM((4 * ROWS, WIDE), BF16),
        pltpu.VMEM((SMALL, TILES * ROWS), BF16),
        pltpu.VMEM((2, slots, LANES), F32),
        pltpu.VMEM((2, SMALL, LANES), F32),
        pltpu.VMEM((TILES * ROWS, 2 * SMALL), BF16),
        pltpu.VMEM(((TILES - 4) * ROWS, 2 * slots), BF16),
        pltpu.VMEM((4 * ROWS, 2 * slots), BF16),
        pltpu.VMEM((TILES * ROWS, 2 * slots), BF16),
        pltpu.VMEM((2 * SMALL, WIDE), BF16),
        pltpu.VMEM((2 * slots, WIDE), BF16),
        pltpu.VMEM((2, STACK, LANES), F32),
        pltpu.VMEM((4, ROWS, LANES), F32),
        pltpu.VMEM((2, STACK, LANES), F32),
        pltpu.VMEM((2, NV, ROWS, LANES), F32),
        pltpu.VMEM((2, TILES, LANES), jnp.int32),
        pltpu.VMEM((2, TILES, 8, LANES), F32),
        pltpu.VMEM((BALANCES + 1, 2, NV, ROWS, LANES), F32),
        pltpu.VMEM((BALANCES + 1, 2, NV, ROWS, LANES), F32),
        pltpu.VMEM((3, ROWS, LANES), F32),
        pltpu.VMEM((TILES, LANES), F32),
        pltpu.VMEM((TILES, LANES), F32),
        pltpu.VMEM((BALANCES + 1, 2, ROW_TILES, 8, LANES), F32),
        pltpu.VMEM((BALANCES, 2, ROW_TILES, 8, LANES), F32),
        pltpu.VMEM((slots, LANES), F32),
        pltpu.VMEM((slots, LANES), F32),
        pltpu.VMEM((BALANCES, slots, BOX), F32),
        pltpu.VMEM((BALANCES, slots, BOX), F32),
        pltpu.VMEM((slots, LANES), F32),
        pltpu.VMEM((slots, WIDE), F32),
        pltpu.VMEM((2, len(NEIGHBOURS), ROWS, LANES), F32),
        pltpu.VMEM((2, len(NEIGHBOURS), ROWS, LANES), F32),
        pltpu.VMEM((2, ROWS, LANES), F32),
        pltpu.VMEM((2, ROWS, LANES), F32),
        dma((BALANCES + 1, 2)), dma((BALANCES + 1, 2)),
        dma((3,)), dma((3,)),
        dma((1,)), dma((1,)),
        dma((BALANCES, 2, 2)), dma((BALANCES, 2, 2)),
        dma((len(NEIGHBOURS),)), dma((len(NEIGHBOURS),)),
        dma((BALANCES, len(NEIGHBOURS))), dma((BALANCES, len(NEIGHBOURS))),
        dma((2, len(NEIGHBOURS))), dma((2, len(NEIGHBOURS))), dma((2,)), dma((2,)),
    ]
    half, circ_rate, axial_rate = pl.pallas_call(
        kernel,
        out_shape=(pltpu.VMEM((NV, ROWS, columns), F32),) * 3,
        in_specs=[hbm] * 11,
        out_specs=(vmem, vmem, vmem),
        scratch_shapes=scratch,
        compiler_params=pltpu.CompilerParams(
            collective_id=0, has_side_effects=True, vmem_limit_bytes=56 * 1024 * 1024
        ),
    )(
        flow_state, circ_speed, axial_speed, time_step, lsq_weights,
        partner.reshape(1, columns), partner.reshape(TILES, LANES),
        merge_owner.reshape(1, SMALL), merge_source.reshape(1, SMALL),
        merge_host.reshape(1, SMALL), merge_frac.T,
    )
    last_rate = circ_rate + axial_rate
    return half - 0.5 * (time_step * last_rate), last_rate


def solution(mesh):
    in_specs = (
        P(None, "circ", "axial"),
        P("circ", "axial"),
        P("circ", "axial"),
        P("circ", "axial"),
        P("axial", None, None),
        P("axial"),
        P(("circ", "axial"), None),
        P(("circ", "axial")),
        P(("circ", "axial")),
        P(("circ", "axial"), None),
    )
    out_specs = (P(None, "circ", "axial"), P(None, "circ", "axial"))
    return jax.shard_map(local, mesh=mesh, in_specs=in_specs, out_specs=out_specs, check_vma=False)
```
